32 devices in a mesh: wide: 8 (over z, core), narrow: 4 (over y, x).
Axes of the slice: x: 2, y: 2, z: 4, core: 2. Of those that a mesh axis runs over, the one named last changes fastest.
Arguments:
- series: bfloat16 [12288, 3600], P(('wide', 'narrow')), may hold values from -6 to 6
- padding: int32 [12288], P('wide'), may hold values from 0 to 1800, as said below
- coarse_first: bfloat16 [512, 900], P(('wide', 'narrow')), may hold values from -0.1875 to 0.1875
- coarse_first_bias: float32 [512], replicated, may hold values from -3 to 3
- coarse_second: bfloat16 [512, 512], P(('wide', 'narrow')), may hold values from -0.25 to 0.25
- coarse_second_bias: float32 [512], replicated, may hold values from -3 to 3
- coarse_third: bfloat16 [512, 512], P(('wide', 'narrow')), may hold values from -0.25 to 0.25
- coarse_third_bias: float32 [512], replicated, may hold values from -3 to 3
- coarse_basis: bfloat16 [512, 360], P(('wide', 'narrow')), may hold values from -0.25 to 0.25
- coarse_basis_bias: float32 [360], replicated, may hold values from -3 to 3
- fine_first: bfloat16 [512, 3600], P('wide', 'narrow'), may hold values from -0.09375 to 0.09375
- fine_first_bias: float32 [512], replicated, may hold values from -3 to 3
- fine_second: bfloat16 [512, 512], P(('wide', 'narrow')), may hold values from -0.25 to 0.25
- fine_second_bias: float32 [512], replicated, may hold values from -3 to 3
- fine_third: bfloat16 [512, 512], P(('wide', 'narrow')), may hold values from -0.25 to 0.25
- fine_third_bias: float32 [512], replicated, may hold values from -3 to 3
- fine_back: bfloat16 [512, 3600], P('wide', 'narrow'), may hold values from -0.25 to 0.25
- fine_back_bias: float32 [3600], replicated, may hold values from -3 to 3
- fine_fore: bfloat16 [512, 720], P('wide', 'narrow'), may hold values from -0.25 to 0.25
- detailed_predict_offset: float32 [720], replicated, may hold values from -3 to 3
- grad_resid: bfloat16 [12288, 3600], P('wide', 'narrow'), may hold values from -6 to 6
- future_cotangent_array: bfloat16 [12288, 720], P('wide', 'narrow'), may hold values from -6 to 6
Outputs:
- leftover_signal: bfloat16 [12288, 3600], P('wide', 'narrow')
- predicted_future: float32 [12288, 720], P('wide', 'narrow')
- temporal_input_derivative: bfloat16 [12288, 3600], P(('wide', 'narrow'))
- grad_coarse_first: float32 [512, 900], P(('wide', 'narrow'))
- grad_coarse_first_bias: float32 [512], replicated
- grad_coarse_second: float32 [512, 512], P(('wide', 'narrow'))
- grad_coarse_second_bias: float32 [512], replicated
- grad_coarse_third: float32 [512, 512], P(('wide', 'narrow'))
- grad_coarse_third_bias: float32 [512], replicated
- grad_coarse_basis: float32 [512, 360], P(('wide', 'narrow'))
- grad_coarse_basis_bias: float32 [360], replicated
- grad_fine_first: float32 [512, 3600], P('wide', 'narrow')
- grad_fine_first_bias: float32 [512], replicated
- grad_fine_second: float32 [512, 512], P(('wide', 'narrow'))
- grad_fine_second_bias: float32 [512], replicated
- grad_fine_third: float32 [512, 512], P(('wide', 'narrow'))
- grad_fine_third_bias: float32 [512], replicated
- grad_fine_back: float32 [512, 3600], P('wide', 'narrow')
- grad_fine_back_bias: float32 [3600], replicated
- grad_fine_fore: float32 [512, 720], P('wide', 'narrow')
- grad_fine_fore_bias: float32 [720], replicated
The draws below stay inside these ranges and needn't reach their ends.
Inputs may be any that keep to these rules, and one draw needn't show every extreme that they name: padding[r] counts the leading padded steps of window r: its mask is 1 at steps t >= padding[r] and 0 before.
All inputs are finite; a program needn't handle non-finite values.
Results may differ from the reference program's by a relative error of at most 0.017.
Values may be sent and summed in bfloat16 or wider, within the bound.
A program may use at most 192 MiB of HBM per device.

```python
import math
import jax
import jax.numpy as jnp
from jax import lax

L = 3600
AHEAD_TIMES = 720
HID = 512
POOL = 4
KB = 300
KF = 60
ROWS = 12288


def draw_padding(key, part):
    key = jax.random.fold_in(key, 7)
    first_key, second_key, third_key = jax.random.split(key, 3)
    padded = jax.random.randint(first_key, (ROWS,), 0, 2)
    counts = jax.random.randint(second_key, (ROWS,), 1, L // 2 + 1)
    result = jnp.where(padded == 1, counts, 0).astype(jnp.int32)
    chosen = jax.random.randint(third_key, (), 0, ROWS)
    return result.at[chosen].set(L // 2)


def level_of(rng, dims, cuts, least, largest):
    gain, own = 1.0, jax.random.fold_in(rng, 6)
    for dim, parts in cuts:
        draws = jnp.exp(jax.random.uniform(jax.random.fold_in(own, dim), (parts,), jnp.float32, least / len(cuts), largest / len(cuts)))
        gain = gain * jnp.repeat(draws, dims[dim] // parts).reshape([-1 if axis == dim else 1 for axis in range(len(dims))])
    return gain


def normal_values(rng, extent, width, limit, cuts=(), kind=jnp.bfloat16):
    entries = width * jax.random.normal(rng, extent, jnp.float32)
    if cuts:
        entries = entries * level_of(rng, extent, cuts, -0.22, 0.18)
    return jnp.clip(entries, -limit, limit).astype(kind)


def setup_inputs(seed: int = 0) -> dict:
    key_list = jax.random.split(jax.random.key(seed), 23)
    series = normal_values(key_list[0], (ROWS, L), 1.0, 6.0, ((0, 32),))
    padding = draw_padding(jax.random.fold_in(key_list[22], 71), 0)
    coarse_first = normal_values(key_list[2], (HID, L // POOL), (L // POOL) ** -0.5, 0.1875, ((0, 32),))
    coarse_first_bias = normal_values(key_list[3], (HID,), 0.5, 3.0, (), jnp.float32)
    coarse_second = normal_values(key_list[4], (HID, HID), HID ** -0.5, 0.25, ((0, 32),))
    coarse_second_bias = normal_values(key_list[5], (HID,), 0.5, 3.0, (), jnp.float32)
    coarse_third = normal_values(key_list[6], (HID, HID), HID ** -0.5, 0.25, ((0, 32),))
    coarse_third_bias = normal_values(key_list[7], (HID,), 0.5, 3.0, (), jnp.float32)
    coarse_basis = normal_values(key_list[8], (HID, KB + KF), HID ** -0.5, 0.25, ((0, 32),))
    coarse_basis_bias = normal_values(key_list[9], (KB + KF,), 0.5, 3.0, (), jnp.float32)
    fine_first = normal_values(key_list[10], (HID, L), L ** -0.5, 0.09375, ((0, 8), (1, 4)))
    fine_first_bias = normal_values(key_list[11], (HID,), 0.5, 3.0, (), jnp.float32)
    fine_second = normal_values(key_list[12], (HID, HID), HID ** -0.5, 0.25, ((0, 32),))
    fine_second_bias = normal_values(key_list[13], (HID,), 0.5, 3.0, (), jnp.float32)
    fine_third = normal_values(key_list[14], (HID, HID), HID ** -0.5, 0.25, ((0, 32),))
    fine_third_bias = normal_values(key_list[15], (HID,), 0.5, 3.0, (), jnp.float32)
    fine_back = normal_values(key_list[16], (HID, L), HID ** -0.5, 0.25, ((0, 8), (1, 4)))
    fine_back_bias = normal_values(key_list[17], (L,), 0.5, 3.0, (), jnp.float32)
    fine_fore = normal_values(key_list[18], (HID, AHEAD_TIMES), HID ** -0.5, 0.25, ((0, 8), (1, 4)))
    detailed_predict_offset = normal_values(key_list[19], (AHEAD_TIMES,), 0.5, 3.0, (), jnp.float32)
    grad_resid = normal_values(key_list[20], (ROWS, L), 1.0, 6.0, ((0, 8), (1, 4)))
    future_cotangent_array = normal_values(key_list[21], (ROWS, AHEAD_TIMES), 1.0, 6.0, ((0, 8), (1, 4)))
    return dict(series=series, padding=padding, coarse_first=coarse_first, coarse_first_bias=coarse_first_bias, coarse_second=coarse_second, coarse_second_bias=coarse_second_bias, coarse_third=coarse_third, coarse_third_bias=coarse_third_bias, coarse_basis=coarse_basis, coarse_basis_bias=coarse_basis_bias, fine_first=fine_first, fine_first_bias=fine_first_bias, fine_second=fine_second, fine_second_bias=fine_second_bias, fine_third=fine_third, fine_third_bias=fine_third_bias, fine_back=fine_back, fine_back_bias=fine_back_bias, fine_fore=fine_fore, detailed_predict_offset=detailed_predict_offset, grad_resid=grad_resid, future_cotangent_array=future_cotangent_array)


@jax.custom_vjp
def low(v):
    return lax.optimization_barrier(v.astype(jnp.bfloat16)).astype(jnp.float32)

@jax.custom_vjp
def low_back(v):
    return v

def low_keep(v):
    return (low(v), None)

def low_pass(kept, grad):
    return (grad,)

def back_keep(v):
    return (v, None)

def back_low(kept, grad):
    return (low(grad),)
low.defvjp(low_keep, low_pass)
low_back.defvjp(back_keep, back_low)

def upsample(coef, length):
    coef_count = coef.shape[1]
    stride = length // coef_count
    halfway = stride // 2
    padded = jnp.concatenate([coef[:, :1], coef, coef[:, -1:]], axis=1)
    preceding = jnp.repeat(padded[:, :coef_count], stride, axis=1)
    central = jnp.repeat(padded[:, 1:coef_count + 1], stride, axis=1)
    following = jnp.repeat(padded[:, 2:], stride, axis=1)
    offsets = jnp.arange(length, dtype=jnp.int32) % stride
    in_front = offsets < halfway
    fraction = (jnp.where(in_front, offsets + halfway, offsets - halfway).astype(jnp.float32) + 0.5) / stride
    lower_val = jnp.where(in_front[None, :], preceding, central)
    upper_val = jnp.where(in_front[None, :], central, following)
    return lower_val * (1.0 - fraction) + upper_val * fraction

def project_rows(rows_in, matrix):
    return jnp.dot(rows_in, matrix.T, precision=lax.Precision.HIGHEST, preferred_element_type=jnp.float32)

def apply_rows(rows_in, matrix):
    return jnp.dot(rows_in, matrix, precision=lax.Precision.HIGHEST, preferred_element_type=jnp.float32)

def forward(params, series_rows, mask):
    coarse_first, coarse_first_bias, coarse_second, coarse_second_bias, coarse_third, coarse_third_bias, coarse_basis, coarse_basis_bias, fine_first, fine_first_bias, fine_second, fine_second_bias, fine_third, fine_third_bias, fine_back, fine_back_bias, fine_fore, detailed_predict_offset = params
    started = series_rows * mask
    row_count = started.shape[0]
    pooled = low(lax.optimization_barrier(jnp.mean(started.reshape(row_count, L // POOL, POOL), axis=2)))
    linear_one = low_back(project_rows(pooled, coarse_first) + coarse_first_bias)
    hidden_one = low(jax.nn.silu(linear_one))
    linear_two = low_back(project_rows(hidden_one, coarse_second) + coarse_second_bias)
    hidden_two = low(jax.nn.silu(linear_two))
    linear_three = low_back(project_rows(hidden_two, coarse_third) + coarse_third_bias)
    hidden_three = low(jax.nn.silu(linear_three))
    theta = low_back(apply_rows(hidden_three, coarse_basis) + coarse_basis_bias)
    backcast = upsample(theta[:, :KB], L)
    coarse_fore = upsample(theta[:, KB:], AHEAD_TIMES)
    sent_resid = low(low_back((started - backcast) * mask))
    sent_fore = low(low_back(coarse_fore))
    lift_one = low_back(project_rows(sent_resid, fine_first) + fine_first_bias)
    fine_one = low(jax.nn.silu(lift_one))
    lift_two = low_back(project_rows(fine_one, fine_second) + fine_second_bias)
    fine_two = low(jax.nn.silu(lift_two))
    lift_three = low_back(project_rows(fine_two, fine_third) + fine_third_bias)
    fine_three = low(jax.nn.silu(lift_three))
    coef_back = low_back(apply_rows(fine_three, fine_back) + fine_back_bias)
    coef_fore = low_back(apply_rows(fine_three, fine_fore) + detailed_predict_offset)
    return ((sent_resid - coef_back) * mask, sent_fore + coef_fore)

def reference(series, padding, coarse_first, coarse_first_bias, coarse_second, coarse_second_bias, coarse_third, coarse_third_bias, coarse_basis, coarse_basis_bias, fine_first, fine_first_bias, fine_second, fine_second_bias, fine_third, fine_third_bias, fine_back, fine_back_bias, fine_fore, detailed_predict_offset, grad_resid, future_cotangent_array):
    params = tuple((p.astype(jnp.float32) for p in (coarse_first, coarse_first_bias, coarse_second, coarse_second_bias, coarse_third, coarse_third_bias, coarse_basis, coarse_basis_bias, fine_first, fine_first_bias, fine_second, fine_second_bias, fine_third, fine_third_bias, fine_back, fine_back_bias, fine_fore, detailed_predict_offset)))
    entire_record_tally = series.shape[0]
    block = math.gcd(entire_record_tally, 512)
    stack_module_tally = entire_record_tally // block
    steps_all = jnp.arange(L, dtype=jnp.int32)

    def solitary_module(carry, index):
        begin = index * block
        rows_in = lax.dynamic_slice_in_dim(series, begin, block, 0).astype(jnp.float32)
        pads_in = lax.dynamic_slice_in_dim(padding, begin, block, 0)
        mask = (steps_all[None, :] >= pads_in[:, None]).astype(jnp.float32)
        resid_cot = lax.dynamic_slice_in_dim(grad_resid, begin, block, 0).astype(jnp.float32)
        fore_cot = lax.dynamic_slice_in_dim(future_cotangent_array, begin, block, 0).astype(jnp.float32)
        outputs, pullback = jax.vjp(lambda weights, values: forward(weights, values, mask), params, rows_in)
        weight_grads, input_grad = pullback((resid_cot, fore_cot))
        carry = tuple((total + term for total, term in zip(carry, weight_grads)))
        return (carry, (outputs[0].astype(jnp.bfloat16), outputs[1], input_grad.astype(jnp.bfloat16)))
    starting_accumulations = tuple((jnp.zeros(p.shape, jnp.float32) for p in params))
    derivative_sequence, (leftover_signal, predicted_future, temporal_input_derivative) = lax.scan(solitary_module, starting_accumulations, jnp.arange(stack_module_tally, dtype=jnp.int32))
    leftover_signal = leftover_signal.reshape(entire_record_tally, L)
    predicted_future = predicted_future.reshape(entire_record_tally, AHEAD_TIMES)
    temporal_input_derivative = temporal_input_derivative.reshape(entire_record_tally, L)
    return (leftover_signal, predicted_future, temporal_input_derivative, derivative_sequence[0], derivative_sequence[1], derivative_sequence[2], derivative_sequence[3], derivative_sequence[4], derivative_sequence[5], derivative_sequence[6], derivative_sequence[7], derivative_sequence[8], derivative_sequence[9], derivative_sequence[10], derivative_sequence[11], derivative_sequence[12], derivative_sequence[13], derivative_sequence[14], derivative_sequence[15], derivative_sequence[16], derivative_sequence[17])
```

```python
import functools

import jax
import jax.numpy as jnp
import numpy as np
from jax import lax
from jax.experimental import pallas as pl
from jax.experimental.pallas import tpu as pltpu
from jax.sharding import PartitionSpec as P

MESH = pl.DeviceIdType.MESH
POOL = 4
KB = 300
PASSES = 1
LANE = 128
F32 = jnp.float32
BF16 = jnp.bfloat16


def up(value, unit):
    return -(-value // unit) * unit


def interp_table(count, length):
    stride = length // count
    table = np.zeros((count, length), np.float32)
    for t in range(length):
        doubled = 2 * t + 1 - stride
        low = doubled // (2 * stride)
        part = doubled - low * 2 * stride
        table[min(max(low, 0), count - 1), t] += 2 * stride - part
        table[min(max(low + 1, 0), count - 1), t] += part
    return table


def window_tables(nn, length, ahead, back_count, fore_count):
    back, fore = interp_table(back_count, length), interp_table(fore_count, ahead)
    piece, part = length // nn, ahead // nn
    spans = []
    for n in range(nn):
        rows_b = np.nonzero(back[:, n * piece : (n + 1) * piece].any(1))[0]
        rows_f = np.nonzero(fore[:, n * part : (n + 1) * part].any(1))[0]
        spans.append((rows_b, rows_f))
    wide_b = max(len(b) for b, _ in spans)
    wide_f = max(len(f) for _, f in spans)
    width = up(wide_b + wide_f, LANE)
    bw, fw = up(back_count, LANE), up(fore_count, LANE)
    pick = np.zeros((nn, bw + fw, width), np.float32)
    mix_b = np.zeros((nn, width, piece), np.float32)
    mix_f = np.zeros((nn, width, part), np.float32)
    all_f = np.zeros((nn, fw, part), np.float32)
    for n, (rows_b, rows_f) in enumerate(spans):
        all_f[n, :fore_count] = fore[:, n * part : (n + 1) * part]
        for slot, row in enumerate(rows_b):
            pick[n, row, slot] = 1
            mix_b[n, slot] = back[row, n * piece : (n + 1) * piece]
        for slot, row in enumerate(rows_f):
            pick[n, bw + row, wide_b + slot] = 1
            mix_f[n, wide_b + slot] = fore[row, n * part : (n + 1) * part]
    return tuple(t.astype(BF16) for t in (pick, mix_b, mix_f, all_f))


class Net:
    def __init__(self, sizes, sends, recvs):
        self.nn, self.nc = sizes
        self.sends, self.recvs = sends, recvs
        self.count = 0
        self.w, self.n = lax.axis_index("wide"), lax.axis_index("narrow")
        self.chip, self.core = self.w // 2, self.w % 2

    def at(self, d=0, e=0, c=0):
        return ((self.chip ^ e) * 2 + (self.core ^ c), self.n ^ d)

    def partners(self):
        return (
            [self.at(d=d) for d in range(1, self.nn)]
            + [self.at(e=e) for e in range(1, self.nc)]
            + [self.at(c=1)]
        )

    def greet(self):
        barrier = pltpu.get_barrier_semaphore()
        others = self.partners()
        for other in others:
            pl.semaphore_signal(barrier, 1, device_id=other, device_id_type=MESH)
        pl.semaphore_wait(barrier, len(others))

    def send(self, src, dst, to):
        k = self.count
        self.count += 1
        copy = pltpu.make_async_remote_copy(
            src_ref=src,
            dst_ref=dst,
            send_sem=self.sends.at[k],
            recv_sem=self.recvs.at[k],
            device_id=to,
            device_id_type=MESH,
        )
        copy.start()
        return copy


def in_kernel(sizes, series, grad, mid, fsh, fb, land_s, land_g, wmid, wf, wfb, sends, recvs, own):
    net = Net(sizes, sends, recvs)
    nn, nc = sizes
    rows = series.shape[1]
    hs = mid.shape[0]
    hw = fsh.shape[0]
    n, w, chip, core = net.n, net.w, net.chip, net.core

    def mrows(wi, ni):
        return pl.ds(pl.multiple_of((wi * nn + ni) * hs, hs), hs)

    def wrows(wi):
        return pl.ds(pl.multiple_of(wi * hw, hw), hw)

    def grows(ni):
        return pl.ds(pl.multiple_of(ni * rows, rows), rows)

    locals_ = [
        pltpu.make_async_copy(mid, wmid.at[mrows(w, n)], own.at[0]),
        pltpu.make_async_copy(fsh, wf.at[n, wrows(w)], own.at[1]),
        pltpu.make_async_copy(fb, wfb.at[wrows(w)], own.at[2]),
        pltpu.make_async_copy(series.at[n], land_s.at[n], own.at[3]),
        pltpu.make_async_copy(grad.at[grows(n)], land_g.at[n], own.at[4]),
    ]
    for c in locals_:
        c.start()
    net.greet()
    done = []
    zm = [net.send(mid, wmid.at[mrows(w, n)], net.at(e=e)) for e in range(1, nc)]
    fn = [net.send(fsh, wf.at[n, wrows(w)], net.at(d=d)) for d in range(1, nn)]
    zb = [net.send(fb, wfb.at[wrows(w)], net.at(e=e)) for e in range(1, nc)]
    locals_[0].wait()
    locals_[1].wait()
    locals_[2].wait()
    nm = {}
    for e in range(nc):
        if e:
            zm[e - 1].wait_recv()
        r = mrows((chip ^ e) * 2 + core, n)
        nm[e] = [net.send(wmid.at[r], wmid.at[r], net.at(d=d)) for d in range(1, nn)]
    for c in fn:
        c.wait_recv()
    zf = [net.send(wf.at[:, wrows(w)], wf.at[:, wrows(w)], net.at(e=e)) for e in range(1, nc)]
    last = []
    for e in range(nc):
        for c in nm[e]:
            c.wait_recv()
        r = wrows((chip ^ e) * 2 + core)
        last.append(net.send(wmid.at[r], wmid.at[r], net.at(c=1)))
    ga = [net.send(grad.at[grows(n ^ d)], land_g.at[n], net.at(d=d)) for d in range(1, nn)]
    sa = [net.send(series.at[n ^ d], land_s.at[n], net.at(d=d)) for d in range(1, nn)]
    for e in range(nc):
        if e:
            zb[e - 1].wait_recv()
        r = wrows((chip ^ e) * 2 + core)
        last.append(net.send(wfb.at[r], wfb.at[r], net.at(c=1)))
    for e in range(nc):
        if e:
            zf[e - 1].wait_recv()
        r = wrows((chip ^ e) * 2 + core)
        last.append(net.send(wf.at[:, r], wf.at[:, r], net.at(c=1)))
    for c in last + ga + sa:
        c.wait()
    for c in zm + fn + zb + zf + [c for e in range(nc) for c in nm[e]]:
        c.wait_send()
    locals_[3].wait()
    locals_[4].wait()


def partial_kernel(sizes, part, out, land, sends, recvs):
    net = Net(sizes, sends, recvs)
    nn, nc = sizes
    net.greet()
    cs = [net.send(part.at[net.n ^ d], land.at[d], net.at(d=d)) for d in range(1, nn)]
    for c in cs:
        c.wait()
    total = part[net.n].astype(F32)
    for d in range(1, nn):
        total += land[d].astype(F32)
    out[...] = total


def share_kernel(sizes, f3, tw, out_f3, out_tw, sends, recvs, own):
    net = Net(sizes, sends, recvs)
    nn, nc = sizes
    n = net.n
    a = pltpu.make_async_copy(f3, out_f3.at[n], own.at[0])
    b = pltpu.make_async_copy(tw.at[n], out_tw.at[n], own.at[1])
    a.start()
    b.start()
    net.greet()
    cs = []
    for d in range(1, nn):
        cs.append(net.send(tw.at[n ^ d], out_tw.at[n], net.at(d=d)))
        cs.append(net.send(f3, out_f3.at[n], net.at(d=d)))
    for c in cs:
        c.wait()
    a.wait()
    b.wait()


def out_kernel(
    sizes, gm, gf, gb, bias, om, of, ob, obias,
    cm, cf, cb, m1, f1, b1, zm, nf, zb, m2, f2, nm, zf, bl, bt, sends, recvs,
):
    net = Net(sizes, sends, recvs)
    nn, nc = sizes
    n, chip, core = net.n, net.chip, net.core
    net.greet()
    other = net.at(c=1)
    keep = []

    def go(*a):
        c = net.send(*a)
        keep.append(c)
        return c

    s_b = go(gb.at[:, 1 - core], cb, other)
    s_f = go(gf.at[:, :, 1 - core], cf, other)
    s_m = go(gm.at[:, 1 - core], cm, other)
    s_v = go(bias, bl.at[0], other)
    s_b.wait_recv()
    for z in range(nc):
        b1[z] = (gb[z, core].astype(F32) + cb[z].astype(F32)).astype(BF16)
    r_b = [go(b1.at[chip ^ e], zb.at[e], net.at(e=e)) for e in range(1, nc)]
    s_f.wait_recv()

    def add_f(i, carry):
        for z in range(nc):
            f1[i, z] = (gf[i, z, core].astype(F32) + cf[i, z].astype(F32)).astype(BF16)
        return carry

    lax.fori_loop(0, nn, add_f, 0)
    r_f = [go(f1.at[n ^ d], nf.at[d], net.at(d=d)) for d in range(1, nn)]
    s_m.wait_recv()
    for z in range(nc):
        m1[z] = (gm[z, core].astype(F32) + cm[z].astype(F32)).astype(BF16)
    hs = om.shape[0]
    r_m = [go(m1.at[chip ^ e], zm.at[e], net.at(e=e)) for e in range(1, nc)]
    s_v.wait_recv()
    bt[0] = bias[...] + bl[0]
    r_v = [go(bt.at[0], bl.at[e], net.at(e=e)) for e in range(1, nc)]
    for c in r_f:
        c.wait_recv()
    for z in range(nc):
        total = f1[n, z].astype(F32)
        for d in range(1, nn):
            total += nf[d, z].astype(F32)
        f2[z] = total.astype(BF16)
    q_f = [go(f2.at[chip ^ e], zf.at[e], net.at(e=e)) for e in range(1, nc)]
    for c in r_m:
        c.wait_recv()
    total = m1[chip].astype(F32)
    for e in range(1, nc):
        total += zm[e].astype(F32)
    m2[...] = total.astype(BF16)

    def block(i):
        return m2.at[pl.ds(pl.multiple_of(i * hs, hs), hs)]

    q_m = [go(block(n ^ d), nm.at[d], net.at(d=d)) for d in range(1, nn)]
    for c in r_v:
        c.wait_recv()
    total = bt[0]
    for e in range(1, nc):
        total += bl[e]
    bt[1] = total
    q_v = [go(bt.at[1], bl.at[nc - 1 + d], net.at(d=d)) for d in range(1, nn)]
    for c in r_b:
        c.wait_recv()
    total = b1[chip].astype(F32)
    for e in range(1, nc):
        total += zb[e].astype(F32)
    ob[...] = total
    for c in q_m:
        c.wait_recv()
    total = block(n)[...].astype(F32)
    for d in range(1, nn):
        total += nm[d].astype(F32)
    om[...] = total
    for c in q_v:
        c.wait_recv()
    total = bt[1]
    for d in range(1, nn):
        total += bl[nc - 1 + d]
    obias[...] = total
    for c in q_f:
        c.wait_recv()
    total = f2[chip].astype(F32)
    for e in range(1, nc):
        total += zf[e].astype(F32)
    of[...] = total
    for c in keep:
        c.wait_send()


def params(cid):
    return pltpu.CompilerParams(
        collective_id=cid, has_side_effects=True, vmem_limit_bytes=56 << 20
    )


def dot_nt(a, b):
    return lax.dot_general(a, b, (((1,), (1,)), ((), ())), preferred_element_type=F32)


def dot_nn(a, b):
    return lax.dot_general(a, b, (((1,), (0,)), ((), ())), preferred_element_type=F32)


def dot_tn(a, b):
    return lax.dot_general(a, b, (((0,), (0,)), ((), ())), preferred_element_type=F32)


def slope(v):
    s = jax.nn.sigmoid(v)
    return s * (1.0 + v * (1.0 - s))


def pad_to(x, width):
    return jnp.pad(x, ((0, 0), (0, width - x.shape[1])))


def spread_basis(x, back_count, bw, fw):
    return jnp.concatenate([pad_to(x[:, :back_count], bw), pad_to(x[:, back_count:], fw)], axis=1)


def fast(nn, nw, series, padding, *rest):
    (cf, cfb, cs, csb, ct, ctb, cb, cbb, ff, ffb, fs, fsb, ft, ftb, fk, fkb, fo, fob, grad, fut) = rest
    nc = nw // 2
    sizes = (nn, nc)
    rows, length = series.shape
    piece, part = grad.shape[1], fut.shape[1]
    ahead = part * nn
    hid = cfb.shape[0]
    hs, hw = hid // (nn * nw), hid // nw
    back_count, fore_count = KB, cbb.shape[0] - KB
    bw, fw = up(back_count, LANE), up(fore_count, LANE)
    pick, mix_b, mix_f, all_f = window_tables(nn, length, ahead, back_count, fore_count)
    width = pick.shape[2]
    scale = 1.0 / (2 * (length // back_count))
    scale_f = 1.0 / (2 * (ahead // fore_count))
    n = lax.axis_index("narrow")
    mids = (cf, cs, ct, spread_basis(cb, back_count, bw, fw), fs, ft)
    mwid = [up(m.shape[1], LANE) for m in mids]
    moff = np.concatenate([[0], np.cumsum(mwid)]).tolist()
    mid = jnp.concatenate([pad_to(m, c) for m, c in zip(mids, mwid)], axis=1)
    pw, qw = up(piece, LANE), up(part, LANE)
    fsh = pad_to(ff, pw)
    fbo = jnp.concatenate([pad_to(fk, pw), pad_to(fo, qw)], axis=1)
    chunks = jnp.transpose(series.reshape(rows, nn, piece), (1, 0, 2))
    anyspec = pl.BlockSpec(memory_space=pl.ANY)
    vspec = pl.BlockSpec(memory_space=pltpu.VMEM)
    ncopies = 16 + 3 * (nn + nc) + 2 * nn * nc
    sems = [pltpu.SemaphoreType.DMA((ncopies,)), pltpu.SemaphoreType.DMA((ncopies,))]
    S = jax.ShapeDtypeStruct
    land_s, land_g, wmid, wf, wfb = pl.pallas_call(
        functools.partial(in_kernel, sizes),
        out_shape=(
            S((nn, rows, piece), BF16),
            S((nn, rows, piece), BF16),
            S((hid, moff[-1]), BF16),
            S((nn, hid, pw), BF16),
            S((hid, pw + qw), BF16),
        ),
        in_specs=[anyspec] * 5,
        out_specs=[anyspec] * 5,
        scratch_shapes=sems + [pltpu.SemaphoreType.DMA((5,))],
        compiler_params=params(0),
    )(chunks, grad, mid, fsh, fbo)
    w1, w2, w3, wb, v2, v3 = (wmid[:, moff[i] : moff[i + 1]] for i in range(6))
    w1 = w1[:, : cf.shape[1]]
    fkw, fow = wfb[:, :piece], wfb[:, pw : pw + part]
    wf = wf[:, :, :piece]
    pads = padding.reshape(nn, rows)
    steps = n * piece + jnp.arange(piece, dtype=jnp.int32)
    gmask = (steps[None, None, :] >= pads[:, :, None]).reshape(nn * rows, piece)
    back_grad = jnp.where(gmask, -grad, 0)
    my_b, my_f, my_all = jnp.asarray(mix_b)[n], jnp.asarray(mix_f)[n], jnp.asarray(all_f)[n]
    part3 = dot_nt(back_grad, fkw) + dot_nt(fut, fow)
    partf = dot_nt(fut, my_all) * scale_f
    part3 = jnp.concatenate([part3, partf], axis=1).astype(BF16).reshape(nn, rows, hid + fw)
    sum3 = pl.pallas_call(
        functools.partial(partial_kernel, sizes),
        out_shape=S((rows, hid + fw), F32),
        in_specs=[vspec],
        out_specs=vspec,
        scratch_shapes=[pltpu.VMEM((nn, rows, hid + fw), BF16)] + sems,
        compiler_params=params(1),
    )(part3)
    own_pads = lax.dynamic_slice_in_dim(pads, n, 1, 0)[0]
    omask = jnp.arange(length, dtype=jnp.int32).reshape(nn, 1, piece) >= own_pads[None, :, None]
    start = jnp.where(omask, chunks, 0)
    flat = jnp.transpose(start, (1, 0, 2)).reshape(rows, length).astype(F32)
    pooled = jnp.mean(flat.reshape(rows, length // POOL, POOL), axis=2).astype(BF16)
    l1 = dot_nt(pooled, w1) + cfb
    h1 = jax.nn.silu(l1).astype(BF16)
    l2 = dot_nt(h1, w2) + csb
    h2 = jax.nn.silu(l2).astype(BF16)
    l3 = dot_nt(h2, w3) + ctb
    h3 = jax.nn.silu(l3).astype(BF16)
    theta = (dot_nn(h3, wb) + spread_basis(cbb[None], back_count, bw, fw)).astype(BF16)
    tw = [dot_nn(theta, pick[j]).astype(BF16) for j in range(nn)]
    resid = [
        jnp.where(omask[j], start[j].astype(F32) - dot_nn(tw[j], mix_b[j]) * scale, 0).astype(BF16)
        for j in range(nn)
    ]
    g1 = sum(dot_nt(resid[j], wf[j]) for j in range(nn)) + ffb
    f1 = jax.nn.silu(g1).astype(BF16)
    g2 = dot_nt(f1, v2) + fsb
    f2 = jax.nn.silu(g2).astype(BF16)
    g3 = dot_nt(f2, v3) + ftb
    f3 = jax.nn.silu(g3).astype(BF16)
    all3, allw = pl.pallas_call(
        functools.partial(share_kernel, sizes),
        out_shape=(S((nn, rows, hid), BF16), S((nn, rows, width), BF16)),
        in_specs=[anyspec] * 2,
        out_specs=[anyspec] * 2,
        scratch_shapes=sems + [pltpu.SemaphoreType.DMA((2,))],
        compiler_params=params(2),
    )(f3, jnp.stack(tw))
    d3 = (sum3[:, :hid] * slope(g3)).astype(BF16)
    d2 = (dot_nn(d3, v3) * slope(g2)).astype(BF16)
    d1 = (dot_nn(d2, v2) * slope(g1)).astype(BF16)
    sent = [
        (jnp.where(omask[j], land_g[j], 0).astype(F32) + dot_nn(d1, wf[j])).astype(BF16)
        for j in range(nn)
    ]
    back_pull = 0
    for j in range(nn):
        pull = dot_nt(jnp.where(omask[j], -sent[j], 0), mix_b[j]) * scale
        back_pull += dot_nt(pull.astype(BF16), pick[j, :bw])
    dth = jnp.concatenate([back_pull, sum3[:, hid:]], axis=1).astype(BF16)
    c3 = (dot_nt(dth, wb) * slope(l3)).astype(BF16)
    c2 = (dot_nn(c3, w3) * slope(l2)).astype(BF16)
    c1 = (dot_nn(c2, w2) * slope(l1)).astype(BF16)
    dpool = jnp.repeat(dot_nn(c1, w1), POOL, axis=1) / POOL
    dsent = jnp.transpose(jnp.stack(sent), (1, 0, 2)).reshape(rows, length)
    rmask = jnp.arange(length, dtype=jnp.int32)[None] >= own_pads[:, None]
    tid = jnp.where(rmask, dsent.astype(F32) + dpool, 0).astype(BF16)
    f3a = all3.reshape(nn * rows, hid)
    twa = allw.reshape(nn * rows, width)
    back_bias = lax.dynamic_slice_in_dim(fkb, n * piece, piece, 0)
    fore_bias = lax.dynamic_slice_in_dim(fob, n * part, part, 0)
    land = land_s.reshape(nn * rows, piece)
    res = (land.astype(F32) - dot_nn(twa, my_b) * scale).astype(BF16).astype(F32)
    leftover = jnp.where(gmask, res - (dot_nn(f3a, fkw) + back_bias), 0).astype(BF16)
    pred = dot_nn(twa, my_f) * scale_f + dot_nn(f3a, fow) + fore_bias
    gmid = [
        pad_to(dot_tn(c1, pooled), mwid[0]),
        dot_tn(c2, h1),
        dot_tn(c3, h2),
        dot_tn(h3, dth),
        dot_tn(d2, f1),
        dot_tn(d3, f2),
    ]
    gmid = jnp.concatenate(gmid, axis=1).astype(BF16).reshape(nc, 2, hw, moff[-1])
    gf = jnp.stack([pad_to(dot_tn(d1, resid[j]), pw) for j in range(nn)]).astype(BF16)
    gf = gf.reshape(nn, nc, 2, hw, pw)
    gb = jnp.concatenate([pad_to(dot_tn(f3a, back_grad), pw), pad_to(dot_tn(f3a, fut), qw)], axis=1)
    gb = gb.astype(BF16).reshape(nc, 2, hw, pw + qw)
    sums = [jnp.sum(v.astype(F32), axis=0) for v in (c1, c2, c3, dth, d1, d2, d3, back_grad, fut)]
    sums[7] = lax.dynamic_update_slice_in_dim(jnp.zeros((length,), F32), sums[7], n * piece, 0)
    sums[8] = lax.dynamic_update_slice_in_dim(jnp.zeros((ahead,), F32), sums[8], n * part, 0)
    soff = np.concatenate([[0], np.cumsum([s.shape[0] for s in sums])]).tolist()
    bias = jnp.pad(jnp.concatenate(sums), (0, up(soff[-1], 8 * LANE) - soff[-1])).reshape(8, -1)
    V = pltpu.VMEM
    mw = moff[-1]
    bs = bias.shape
    om, of, ob, obias = pl.pallas_call(
        functools.partial(out_kernel, sizes),
        out_shape=(S((hs, mw), F32), S((hw, pw), F32), S((hw, pw + qw), F32), S(bs, F32)),
        in_specs=[vspec] * 4,
        out_specs=[vspec] * 4,
        scratch_shapes=[
            V((nc, hw, mw), BF16),
            V((nn, nc, hw, pw), BF16),
            V((nc, hw, pw + qw), BF16),
            V((nc, hw, mw), BF16),
            V((nn, nc, hw, pw), BF16),
            V((nc, hw, pw + qw), BF16),
            V((nc, hw, mw), BF16),
            V((nn, nc, hw, pw), BF16),
            V((nc, hw, pw + qw), BF16),
            V((hw, mw), BF16),
            V((nc, hw, pw), BF16),
            V((nn, hs, mw), BF16),
            V((nc, hw, pw), BF16),
            V((nn + nc,) + bs, F32),
            V((2,) + bs, F32),
        ]
        + sems,
        compiler_params=params(3),
    )(gmid, gf, gb, bias)
    om = [om[:, moff[i] : moff[i] + m.shape[1]] for i, m in enumerate(mids)]
    om[3] = jnp.concatenate([om[3][:, :back_count], om[3][:, bw : bw + fore_count]], axis=1)
    flat = obias.reshape(-1)
    bsum = [flat[a:b] for a, b in zip(soff[:-1], soff[1:])]
    bsum[3] = jnp.concatenate([bsum[3][:back_count], bsum[3][bw : bw + fore_count]])
    return (
        leftover,
        pred,
        tid,
        om[0],
        bsum[0],
        om[1],
        bsum[1],
        om[2],
        bsum[2],
        om[3],
        bsum[3],
        of[:, :piece],
        bsum[4],
        om[4],
        bsum[5],
        om[5],
        bsum[6],
        ob[:, :piece],
        bsum[7],
        ob[:, pw : pw + part],
        bsum[8],
    )


def upsample(coef, length):
    coef_count = coef.shape[1]
    stride = length // coef_count
    halfway = stride // 2
    padded = jnp.concatenate([coef[:, :1], coef, coef[:, -1:]], axis=1)
    preceding = jnp.repeat(padded[:, :coef_count], stride, axis=1)
    central = jnp.repeat(padded[:, 1 : coef_count + 1], stride, axis=1)
    following = jnp.repeat(padded[:, 2:], stride, axis=1)
    offsets = jnp.arange(length, dtype=jnp.int32) % stride
    in_front = offsets < halfway
    fraction = (
        jnp.where(in_front, offsets + halfway, offsets - halfway).astype(jnp.float32) + 0.5
    ) / stride
    lower_val = jnp.where(in_front[None, :], preceding, central)
    upper_val = jnp.where(in_front[None, :], central, following)
    return lower_val * (1.0 - fraction) + upper_val * fraction


def silu_slope(value):
    sigma = jax.nn.sigmoid(value)
    return sigma * (1.0 + value * (1.0 - sigma))


def project_rows(rows_in, matrix):
    return lax.dot_general(
        rows_in, matrix, (((1,), (1,)), ((), ())), preferred_element_type=jnp.float32
    )


def apply_rows(rows_in, matrix):
    return jnp.dot(rows_in, matrix, preferred_element_type=jnp.float32)


def column_outer(first_rows, second_rows):
    return lax.dot_general(
        first_rows, second_rows, (((0,), (0,)), ((), ())), preferred_element_type=jnp.float32
    )


def own_slice(values, begin, amount):
    return lax.dynamic_slice_in_dim(values, begin, amount, 0)


def column_sums(values):
    return jnp.sum(values.astype(jnp.float32), axis=0)


def general(
    series,
    padding,
    coarse_first,
    coarse_first_bias,
    coarse_second,
    coarse_second_bias,
    coarse_third,
    coarse_third_bias,
    coarse_basis,
    coarse_basis_bias,
    fine_first,
    fine_first_bias,
    fine_second,
    fine_second_bias,
    fine_third,
    fine_third_bias,
    fine_back,
    fine_back_bias,
    fine_fore,
    detailed_predict_offset,
    grad_resid,
    future_cotangent_array,
):
    slim_breadth = lax.axis_size("narrow")
    slim_position = lax.axis_index("narrow")
    onsite_tally, length = series.shape
    ahead = future_cotangent_array.shape[1] * slim_breadth
    sample_group = onsite_tally // PASSES
    piece = length // slim_breadth
    predicted_portion = ahead // slim_breadth
    group_pads = padding.reshape(slim_breadth, onsite_tally)
    own_pads = lax.dynamic_slice_in_dim(group_pads, slim_position, 1, 0)[0]
    steps_all = jnp.arange(length, dtype=jnp.int32)
    time_start = slim_position * piece
    predict_onset = slim_position * predicted_portion
    steps_piece = time_start + jnp.arange(piece, dtype=jnp.int32)
    back_bias = lax.dynamic_slice_in_dim(fine_back_bias, time_start, piece, 0)
    predict_offset = lax.dynamic_slice_in_dim(
        detailed_predict_offset, predict_onset, predicted_portion, 0
    )
    resid_grid = grad_resid.reshape(slim_breadth, PASSES, sample_group, piece)
    predict_mesh = future_cotangent_array.reshape(
        slim_breadth, PASSES, sample_group, predicted_portion
    )
    own_start = slim_position * sample_group
    coarse_local = (
        coarse_first,
        coarse_second,
        coarse_third,
        coarse_basis,
        fine_second,
        fine_third,
    )
    fine_local = (fine_first, fine_back, fine_fore)
    totals = tuple((jnp.zeros(w.shape, jnp.float32) for w in coarse_local))
    fine_totals = tuple((jnp.zeros(w.shape, jnp.float32) for w in fine_local))
    bias_totals = tuple(
        (
            jnp.zeros(b.shape, jnp.float32)
            for b in (
                coarse_first_bias,
                coarse_second_bias,
                coarse_third_bias,
                coarse_basis_bias,
                fine_first_bias,
                fine_second_bias,
                fine_third_bias,
                fine_back_bias,
                detailed_predict_offset,
            )
        )
    )
    residual_parts = []
    predicted_portions = []
    grad_parts = []
    for iteration_index in range(PASSES):
        shared = (
            lax.all_gather(coarse_first, ("wide", "narrow"), axis=0, tiled=True),
            lax.all_gather(coarse_second, ("wide", "narrow"), axis=0, tiled=True),
            lax.all_gather(coarse_third, ("wide", "narrow"), axis=0, tiled=True),
            lax.all_gather(coarse_basis, ("wide", "narrow"), axis=0, tiled=True),
            lax.all_gather(fine_second, ("wide", "narrow"), axis=0, tiled=True),
            lax.all_gather(fine_third, ("wide", "narrow"), axis=0, tiled=True),
        )
        pieces = (
            lax.all_gather(fine_first, "wide", axis=0, tiled=True),
            lax.all_gather(fine_back, "wide", axis=0, tiled=True),
            lax.all_gather(fine_fore, "wide", axis=0, tiled=True),
        )
        weight_one, weight_two, weight_three, weight_basis, inner_two, inner_three = shared
        inner_one, inner_back, inner_fore = pieces
        lower = iteration_index * sample_group
        mask = (steps_all[None, :] >= own_pads[lower : lower + sample_group, None]).astype(
            jnp.float32
        )
        started = series[lower : lower + sample_group].astype(jnp.float32) * mask
        pooled = jnp.mean(started.reshape(sample_group, length // POOL, POOL), axis=2).astype(
            jnp.bfloat16
        )
        linear_one = project_rows(pooled, weight_one) + coarse_first_bias
        hidden_one = jax.nn.silu(linear_one).astype(jnp.bfloat16)
        linear_two = project_rows(hidden_one, weight_two) + coarse_second_bias
        hidden_two = jax.nn.silu(linear_two).astype(jnp.bfloat16)
        linear_three = project_rows(hidden_two, weight_three) + coarse_third_bias
        hidden_three = jax.nn.silu(linear_three).astype(jnp.bfloat16)
        theta = apply_rows(hidden_three, weight_basis) + coarse_basis_bias
        backcast = upsample(theta[:, :KB], length)
        coarse_fore = upsample(theta[:, KB:], ahead)
        residual_here = (started - backcast) * mask
        sent_resid, sent_fore = (
            lax.all_to_all(
                residual_here.astype(jnp.bfloat16),
                "narrow",
                split_axis=1,
                concat_axis=0,
                tiled=True,
            ),
            lax.all_to_all(
                coarse_fore.astype(jnp.bfloat16), "narrow", split_axis=1, concat_axis=0, tiled=True
            ),
        )
        pads_here = group_pads[:, lower : lower + sample_group].reshape(-1)
        piece_mask = (steps_piece[None, :] >= pads_here[:, None]).astype(jnp.float32)
        first_partial = project_rows(sent_resid, inner_one)
        lift_one = lax.psum(first_partial, "narrow") + fine_first_bias
        fine_one = jax.nn.silu(lift_one).astype(jnp.bfloat16)
        lift_two = project_rows(fine_one, inner_two) + fine_second_bias
        fine_two = jax.nn.silu(lift_two).astype(jnp.bfloat16)
        lift_three = project_rows(fine_two, inner_three) + fine_third_bias
        fine_three = jax.nn.silu(lift_three).astype(jnp.bfloat16)
        coef_back = apply_rows(fine_three, inner_back) + back_bias
        coef_fore = apply_rows(fine_three, inner_fore) + predict_offset
        residual_parts.append(
            ((sent_resid.astype(jnp.float32) - coef_back) * piece_mask)
            .astype(jnp.bfloat16)
            .reshape(slim_breadth, sample_group, piece)
        )
        predicted_portions.append(
            (sent_fore.astype(jnp.float32) + coef_fore).reshape(
                slim_breadth, sample_group, predicted_portion
            )
        )
        out_grad = (
            resid_grid[:, iteration_index]
            .reshape(slim_breadth * sample_group, piece)
            .astype(jnp.float32)
        )
        predict_cotan = predict_mesh[:, iteration_index].reshape(
            slim_breadth * sample_group, predicted_portion
        )
        back_grad = (-out_grad * piece_mask).astype(jnp.bfloat16)
        coef_partial = project_rows(back_grad, inner_back) + project_rows(predict_cotan, inner_fore)
        three_grad = lax.psum(coef_partial, "narrow")
        lift_three_grad = (three_grad * silu_slope(lift_three)).astype(jnp.bfloat16)
        lift_two_grad = (apply_rows(lift_three_grad, inner_three) * silu_slope(lift_two)).astype(
            jnp.bfloat16
        )
        lift_one_grad = (apply_rows(lift_two_grad, inner_two) * silu_slope(lift_one)).astype(
            jnp.bfloat16
        )
        own_one_grad = own_slice(lift_one_grad, own_start, sample_group)
        own_two_grad = own_slice(lift_two_grad, own_start, sample_group)
        own_three_grad = own_slice(lift_three_grad, own_start, sample_group)
        own_fine_one = own_slice(fine_one, own_start, sample_group)
        own_fine_two = own_slice(fine_two, own_start, sample_group)
        sent_grad = (out_grad * piece_mask + apply_rows(lift_one_grad, inner_one)).astype(
            jnp.bfloat16
        )
        resid_back, fore_back = (
            lax.all_to_all(sent_grad, "narrow", split_axis=0, concat_axis=1, tiled=True),
            lax.all_to_all(predict_cotan, "narrow", split_axis=0, concat_axis=1, tiled=True),
        )
        grad_inner_one = column_outer(lift_one_grad, sent_resid)
        grad_inner_back = column_outer(fine_three, back_grad)
        grad_inner_fore = column_outer(fine_three, predict_cotan)
        grad_inner_two = column_outer(own_two_grad, own_fine_one)
        grad_inner_three = column_outer(own_three_grad, own_fine_two)
        resid_grad = resid_back.astype(jnp.float32)
        back_pull = jax.vjp(lambda coef: upsample(coef, length), theta[:, :KB])[1]
        fore_pull = jax.vjp(lambda coef: upsample(coef, ahead), theta[:, KB:])[1]
        back_coef_grad = back_pull(-resid_grad * mask)[0]
        fore_coef_grad = fore_pull(fore_back.astype(jnp.float32))[0]
        theta_grad = jnp.concatenate([back_coef_grad, fore_coef_grad], axis=1).astype(jnp.bfloat16)
        coarse_three_grad = (
            project_rows(theta_grad, weight_basis) * silu_slope(linear_three)
        ).astype(jnp.bfloat16)
        coarse_two_grad = (
            apply_rows(coarse_three_grad, weight_three) * silu_slope(linear_two)
        ).astype(jnp.bfloat16)
        coarse_one_grad = (apply_rows(coarse_two_grad, weight_two) * silu_slope(linear_one)).astype(
            jnp.bfloat16
        )
        pooled_grad = apply_rows(coarse_one_grad, weight_one)
        start_grad = resid_grad * mask + jnp.repeat(pooled_grad, POOL, axis=1) / POOL
        grad_parts.append((start_grad * mask).astype(jnp.bfloat16))
        grad_weight_one = column_outer(coarse_one_grad, pooled)
        grad_weight_two = column_outer(coarse_two_grad, hidden_one)
        grad_weight_three = column_outer(coarse_three_grad, hidden_two)
        grad_weight_basis = column_outer(hidden_three, theta_grad)
        bias_terms = (
            column_sums(coarse_one_grad),
            column_sums(coarse_two_grad),
            column_sums(coarse_three_grad),
            column_sums(theta_grad),
            column_sums(own_one_grad),
            column_sums(own_two_grad),
            column_sums(own_three_grad),
            lax.dynamic_update_slice_in_dim(
                jnp.zeros((length,), jnp.float32), column_sums(back_grad), time_start, 0
            ),
            lax.dynamic_update_slice_in_dim(
                jnp.zeros((ahead,), jnp.float32), column_sums(predict_cotan), predict_onset, 0
            ),
        )
        bias_totals = tuple((total + term for total, term in zip(bias_totals, bias_terms)))
        scattered = (
            lax.psum_scatter(grad_weight_one, ("wide", "narrow"), scatter_dimension=0, tiled=True),
            lax.psum_scatter(grad_weight_two, ("wide", "narrow"), scatter_dimension=0, tiled=True),
            lax.psum_scatter(
                grad_weight_three, ("wide", "narrow"), scatter_dimension=0, tiled=True
            ),
            lax.psum_scatter(
                grad_weight_basis, ("wide", "narrow"), scatter_dimension=0, tiled=True
            ),
            lax.psum_scatter(grad_inner_two, ("wide", "narrow"), scatter_dimension=0, tiled=True),
            lax.psum_scatter(grad_inner_three, ("wide", "narrow"), scatter_dimension=0, tiled=True),
        )
        spread = (
            lax.psum_scatter(
                grad_inner_one.astype(jnp.bfloat16), "wide", scatter_dimension=0, tiled=True
            ).astype(jnp.float32),
            lax.psum_scatter(
                grad_inner_back.astype(jnp.bfloat16), "wide", scatter_dimension=0, tiled=True
            ).astype(jnp.float32),
            lax.psum_scatter(
                grad_inner_fore.astype(jnp.bfloat16), "wide", scatter_dimension=0, tiled=True
            ).astype(jnp.float32),
        )
        totals = tuple((total + term for total, term in zip(totals, scattered)))
        fine_totals = tuple((total + term for total, term in zip(fine_totals, spread)))
    bias_sums = lax.psum(
        (
            bias_totals[0],
            bias_totals[1],
            bias_totals[2],
            bias_totals[3],
            bias_totals[4],
            bias_totals[5],
            bias_totals[6],
            bias_totals[7],
            bias_totals[8],
        ),
        ("wide", "narrow"),
    )
    leftover_signal = jnp.stack(residual_parts, axis=1).reshape(slim_breadth * onsite_tally, piece)
    predicted_future = jnp.stack(predicted_portions, axis=1).reshape(
        slim_breadth * onsite_tally, predicted_portion
    )
    temporal_input_derivative = jnp.concatenate(grad_parts, axis=0)
    return (
        leftover_signal,
        predicted_future,
        temporal_input_derivative,
        totals[0],
        bias_sums[0],
        totals[1],
        bias_sums[1],
        totals[2],
        bias_sums[2],
        totals[3],
        bias_sums[3],
        fine_totals[0],
        bias_sums[4],
        totals[4],
        bias_sums[5],
        totals[5],
        bias_sums[6],
        fine_totals[1],
        bias_sums[7],
        fine_totals[2],
        bias_sums[8],
    )


def fits(nn, nw, series, padding, first, first_bias, *rest):
    hid, length = first_bias.shape[0], series.shape[1]
    paired = all(k & (k - 1) == 0 for k in (nn, nw)) and nw % 2 == 0
    return paired and hid % (16 * nn * nw) == 0 and length % (POOL * nn) == 0 and series.shape[0] % LANE == 0


def solution(mesh):
    both, rows = P(("wide", "narrow"), None), P("wide", "narrow")
    in_specs = (both, P("wide"))
    in_specs += (both, P()) * 4 + (rows, P()) + (both, P()) * 2 + (rows, P()) * 2 + (rows, rows)
    out_specs = (rows, rows, both) + (both, P()) * 4 + (rows, P()) + (both, P()) * 2 + (rows, P()) * 2
    nn, nw = mesh.shape["narrow"], mesh.shape["wide"]

    def body(*args):
        if fits(nn, nw, *args):
            return fast(nn, nw, *args)
        return general(*args)

    return jax.shard_map(body, mesh=mesh, in_specs=in_specs, out_specs=out_specs, check_vma=False)
```

```python
import functools
import types

import jax
import jax.numpy as jnp
import numpy as np
from jax import lax
from jax.experimental import pallas as pl
from jax.experimental.pallas import tpu as pltpu
from jax.sharding import PartitionSpec as P

MESH = pl.DeviceIdType.MESH
POOL = 4
KB = 300
PASSES = 1
LANE = 128
F32 = jnp.float32
BF16 = jnp.bfloat16


def up(value, unit):
    return -(-value // unit) * unit


def interp_table(count, length):
    stride = length // count
    table = np.zeros((count, length), np.float32)
    for t in range(length):
        doubled = 2 * t + 1 - stride
        low = doubled // (2 * stride)
        part = doubled - low * 2 * stride
        table[min(max(low, 0), count - 1), t] += 2 * stride - part
        table[min(max(low + 1, 0), count - 1), t] += part
    return table


def window_tables(nn, length, ahead, back_count, fore_count):
    back, fore = interp_table(back_count, length), interp_table(fore_count, ahead)
    piece, part = length // nn, ahead // nn
    spans = []
    for n in range(nn):
        rows_b = np.nonzero(back[:, n * piece : (n + 1) * piece].any(1))[0]
        rows_f = np.nonzero(fore[:, n * part : (n + 1) * part].any(1))[0]
        spans.append((rows_b, rows_f))
    wide_b = max(len(b) for b, _ in spans)
    wide_f = max(len(f) for _, f in spans)
    width = up(wide_b + wide_f, LANE)
    bw, fw = up(back_count, LANE), up(fore_count, LANE)
    pick = np.zeros((nn, bw + fw, width), np.float32)
    mix_b = np.zeros((nn, width, piece), np.float32)
    mix_f = np.zeros((nn, width, part), np.float32)
    all_f = np.zeros((nn, fw, part), np.float32)
    for n, (rows_b, rows_f) in enumerate(spans):
        all_f[n, :fore_count] = fore[:, n * part : (n + 1) * part]
        for slot, row in enumerate(rows_b):
            pick[n, row, slot] = 1
            mix_b[n, slot] = back[row, n * piece : (n + 1) * piece]
        for slot, row in enumerate(rows_f):
            pick[n, bw + row, wide_b + slot] = 1
            mix_f[n, wide_b + slot] = fore[row, n * part : (n + 1) * part]
    return tuple(t.astype(BF16) for t in (pick, mix_b, mix_f, all_f))


class Net:
    def __init__(self, sizes, sends, recvs):
        self.nn, self.nc = sizes
        self.sends, self.recvs = sends, recvs
        self.count = 0
        self.w, self.n = lax.axis_index("wide"), lax.axis_index("narrow")
        self.chip, self.core = self.w // 2, self.w % 2

    def at(self, d=0, e=0, c=0):
        return ((self.chip ^ e) * 2 + (self.core ^ c), self.n ^ d)

    def partners(self):
        return (
            [self.at(d=d) for d in range(1, self.nn)]
            + [self.at(e=e) for e in range(1, self.nc)]
            + [self.at(c=1)]
        )

    def greet(self):
        barrier = pltpu.get_barrier_semaphore()
        others = self.partners()
        for other in others:
            pl.semaphore_signal(barrier, 1, device_id=other, device_id_type=MESH)
        pl.semaphore_wait(barrier, len(others))

    def send(self, src, dst, to):
        k = self.count
        self.count += 1
        copy = pltpu.make_async_remote_copy(
            src_ref=src,
            dst_ref=dst,
            send_sem=self.sends.at[k],
            recv_sem=self.recvs.at[k],
            device_id=to,
            device_id_type=MESH,
        )
        copy.start()
        return copy


def params(cid):
    return pltpu.CompilerParams(
        collective_id=cid, has_side_effects=True, vmem_limit_bytes=62 << 20
    )


def dot_nt(a, b):
    return lax.dot_general(a, b, (((1,), (1,)), ((), ())), preferred_element_type=F32)


def dot_nn(a, b):
    return lax.dot_general(a, b, (((1,), (0,)), ((), ())), preferred_element_type=F32)


def dot_tn(a, b):
    return lax.dot_general(a, b, (((0,), (0,)), ((), ())), preferred_element_type=F32)


def slope(v):
    s = jax.nn.sigmoid(v)
    return s * (1.0 + v * (1.0 - s))


def pad_to(x, width):
    return jnp.pad(x, ((0, 0), (0, width - x.shape[1])))


def spread_basis(x, back_count, bw, fw):
    return jnp.concatenate([pad_to(x[:, :back_count], bw), pad_to(x[:, back_count:], fw)], axis=1)


def row_loop(total, unit, body):
    def step(i, carry):
        body(pl.multiple_of(i * unit, unit))
        return carry

    lax.fori_loop(0, total // unit, step, 0)


def each(count, body):
    def step(i, carry):
        body(i)
        return carry

    lax.fori_loop(0, count, step, 0)


def whole(c, *refs):
    (
        pads, pick, mix_b, mix_f, all_f, pool, cfb, csb, ctb, cbb, ffb, fsb, ftb, fkb, fob,
        series, grad, fut_in, mid, ff, fk, fo,
        left_out, pred_out, tid_out, om, of, ok, oo, obias, chunk_hbm, land_s,
        ser, chunk, land_g, bg, fut, wmid, wf, wk, wo, part3, land3, f3a, tw, twa,
        pre, act, pooled, pred, gk, go, cm, cf, ck, co, nm, m2, zm, zf, f2, nf, zk, zo,
        temp, temp2, grads, sfore, pgb, bt, bl, kbias, obias_own, sends, recvs, own,
    ) = refs
    nn, nc, rows, piece, part, hid, pw, bw = c.nn, c.nc, c.rows, c.piece, c.part, c.hid, c.pw, c.bw
    net = Net((nn, nc), sends, recvs)
    n, chip, core = net.n, net.chip, net.core
    keep = []
    owned = []
    unit = 32
    ds = pl.ds

    def go_send(*a):
        copy = net.send(*a)
        keep.append(copy)
        return copy

    def local(src, dst):
        copy = pltpu.make_async_copy(src, dst, own.at[len(owned)])
        owned.append(copy)
        copy.start()
        return copy

    def weight(k):
        return wmid[:, :, :, :, c.off[k] : c.off[k + 1]].reshape(hid, c.off[k + 1] - c.off[k])

    def put_weight(k, value):
        width = c.off[k + 1] - c.off[k]
        wmid[:, :, :, :, c.off[k] : c.off[k + 1]] = value.astype(BF16).reshape(nc, 2, nn, c.hs, width)

    def lane(count):
        return lax.broadcasted_iota(jnp.int32, (unit, count), 1)

    def row_mask(j, r):
        return lane(piece) + j * piece >= pads[ds(pl.multiple_of(n * rows + r, unit), unit), :]

    def piece_mask(j, r):
        return lane(piece) + n * piece >= pads[ds(pl.multiple_of(j * rows + r, unit), unit), :]

    def activate(k, bias, out):
        def body(r):
            v = pre[k, ds(r, unit), :] + bias[...]
            pre[k, ds(r, unit), :] = v
            act[out, ds(r, unit), :] = (v * jax.nn.sigmoid(v)).astype(BF16)

        row_loop(rows, unit, body)

    def sloped(k, out):
        def body(r):
            grads[out, ds(r, unit), :] = (temp[ds(r, unit), :hid] * slope(pre[k, ds(r, unit), :])).astype(BF16)

        row_loop(rows, unit, body)

    ones = jnp.ones((8, rows), BF16)

    def sums(value):
        return dot_nn(ones, value)[0:1]

    c_ser = local(series, ser)
    c_mid = local(mid, wmid.at[chip, core, n])
    c_ff = local(ff, wf.at[n, chip, core])
    c_fk = local(fk, wk.at[chip, core])
    c_fo = local(fo, wo.at[chip, core])
    c_bg = local(grad, bg)
    c_fut = local(fut_in, fut)
    net.greet()
    a_zm = [go_send(mid, wmid.at[chip, core, n], net.at(e=e)) for e in range(1, nc)]
    a_nm = [[go_send(mid, wmid.at[chip, core, n], net.at(d=d)) for d in range(1, nn)]]
    a_fn = [go_send(ff, wf.at[n, chip, core], net.at(d=d)) for d in range(1, nn)]
    a_zk = [go_send(fk, wk.at[chip, core], net.at(e=e)) for e in range(1, nc)]
    a_zk += [go_send(fo, wo.at[chip, core], net.at(e=e)) for e in range(1, nc)]
    for j in range(nn):
        pl.when(n == j)(functools.partial(take_bias, kbias, obias_own, fkb, fob, j, piece, part))
    bt[...] = jnp.zeros_like(bt)
    c_ser.wait()
    for j in range(nn):

        def cut(r, j=j):
            x = ser[ds(r, unit), j * piece : (j + 1) * piece]
            chunk[j, ds(r, unit), :] = jnp.where(row_mask(j, r), x.astype(F32), 0).astype(BF16)

        row_loop(rows, unit, cut)
    c_chunk = local(chunk, chunk_hbm)
    c_mid.wait()
    for e in range(1, nc):
        a_zm[e - 1].wait_recv()
        block = wmid.at[chip ^ e, core, n]
        a_nm.append([go_send(block, block, net.at(d=d)) for d in range(1, nn)])
    c_ff.wait()
    for copy in a_fn:
        copy.wait_recv()
    block = wf.at[:, chip, core]
    a_zf = [go_send(block, block, net.at(e=e)) for e in range(1, nc)]
    for j in range(nn):
        pooled[:, j * c.poolw : (j + 1) * c.poolw] = dot_nn(chunk[j], pool[...]).astype(BF16)
    c_bg.wait()
    c_fut.wait()

    def negate(j):
        def body(r):
            at = ds(pl.multiple_of(j * rows + r, unit), unit)
            bg[at, :] = jnp.where(piece_mask(j, r), -bg[at, :].astype(F32), 0).astype(BF16)

        row_loop(rows, unit, body)

    each(nn, negate)
    c_fk.wait()
    c_fo.wait()
    for copy in a_zk:
        copy.wait_recv()
    a_ck = [go_send(wk.at[:, core], wk.at[:, core], net.at(c=1)), go_send(wo.at[:, core], wo.at[:, core], net.at(c=1))]
    a_cm = []
    for e in range(nc):
        for copy in a_nm[e]:
            copy.wait_recv()
        block = wmid.at[chip ^ e, core]
        a_cm.append(go_send(block, block, net.at(c=1)))
    for copy in a_ck:
        copy.wait_recv()

    def partial(j):
        at = ds(pl.multiple_of(j * rows, rows), rows)
        back = wk[...].reshape(hid, piece)
        fore = wo[...].reshape(hid, part)
        part3[j, :, :hid] = (dot_nt(bg[at, :], back) + dot_nt(fut[at, :], fore)).astype(BF16)
        part3[j, :, hid:] = (dot_nt(fut[at, :], all_f[n]) * c.scale_f).astype(BF16)
        bt[0, ds(4 + n, 1), :piece] += sums(bg[at, :])
        bt[0, ds(4 + nn + n, 1), :part] += sums(fut[at, :])

    each(nn, partial)
    a_p = [go_send(part3.at[n ^ d], land3.at[d], net.at(d=d)) for d in range(1, nn)]

    def grad_rows(j):
        return grad.at[ds(pl.multiple_of(j * rows, rows), rows)]

    c_ga = local(grad_rows(n), land_g.at[n])
    a_ga = [go_send(grad_rows(n ^ d), land_g.at[n], net.at(d=d)) for d in range(1, nn)]
    for copy in a_cm:
        copy.wait_recv()
    pre[0] = dot_nt(pooled[...], weight(0))
    activate(0, cfb, 0)
    pre[1] = dot_nt(act[0], weight(1))
    activate(1, csb, 1)
    pre[2] = dot_nt(act[1], weight(2))
    activate(2, ctb, 2)
    theta = act.at[6]
    theta[...] = (dot_nn(act[2], weight(3)) + cbb[...]).astype(BF16)
    c_chunk.wait()

    def residual(j):
        tw[j] = dot_nn(theta[...], pick[j]).astype(BF16)
        temp[:, :piece] = dot_nn(tw[j], mix_b[j])

        def body(r):
            x = chunk[j, ds(r, unit), :].astype(F32) - temp[ds(r, unit), :piece] * c.scale
            chunk[j, ds(r, unit), :] = jnp.where(row_mask(j, r), x, 0).astype(BF16)

        row_loop(rows, unit, body)

    each(nn, residual)
    a_tw = [go_send(tw.at[n ^ d], twa.at[n], net.at(d=d)) for d in range(1, nn)]
    twa[n] = tw[n]
    a_cf = []
    for e in range(nc):
        if e:
            a_zf[e - 1].wait_recv()
        block = wf.at[:, chip ^ e, core]
        a_cf.append(go_send(block, block, net.at(c=1)))
    for copy in a_cf:
        copy.wait_recv()
    pre[3] = jnp.zeros((rows, hid), F32)

    def lift(j):
        pre[3] += dot_nt(chunk[j], wf[j].reshape(hid, piece))

    each(nn, lift)
    activate(3, ffb, 3)
    pre[4] = dot_nt(act[3], weight(4))
    activate(4, fsb, 4)
    pre[5] = dot_nt(act[4], weight(5))
    activate(5, ftb, 5)
    f3a[n] = act[5]
    a_f3 = [go_send(act.at[5], f3a.at[n], net.at(d=d)) for d in range(1, nn)]
    a_sa = [go_send(chunk_hbm.at[n ^ d], land_s.at[n], net.at(d=d)) for d in range(1, nn)]
    c_sa = local(chunk_hbm.at[n], land_s.at[n])
    for copy in a_p:
        copy.wait_recv()

    def collect(r):
        at = ds(r, unit)
        total = part3[n, at, :].astype(F32)
        for d in range(1, nn):
            total += land3[d, at, :].astype(F32)
        grads[0, at, :] = (total[:, :hid] * slope(pre[5, at, :])).astype(BF16)
        sfore[at, :] = total[:, hid:].astype(BF16)

    row_loop(rows, unit, collect)
    temp[:, :hid] = dot_nn(grads[0], weight(5))
    sloped(4, 1)
    temp[:, :hid] = dot_nn(grads[1], weight(4))
    sloped(3, 2)
    c_ga.wait()
    for copy in a_ga:
        copy.wait_recv()
    for copy in a_cf + a_zf + a_fn:
        copy.wait_send()
    temp2[...] = jnp.zeros_like(temp2)

    def resid_grad(j):
        temp[:, :piece] = dot_nn(grads[2], wf[j].reshape(hid, piece))

        def body(r):
            at = ds(r, unit)
            x = land_g[j, at, :].astype(F32) + temp[at, :piece]
            land_g[j, at, :] = jnp.where(row_mask(j, r), x, 0).astype(BF16)

        row_loop(rows, unit, body)
        pull = (dot_nt(land_g[j], mix_b[j]) * -c.scale).astype(BF16)
        temp2[...] += dot_nt(pull, pick[j, :bw])
        wf[j] = dot_tn(grads[2], chunk[j]).astype(BF16).reshape(nc, 2, c.hw, piece)

    each(nn, resid_grad)
    r_cf = go_send(wf.at[:, :, 1 - core], cf, net.at(c=1))
    dth = grads.at[3]
    dth[:, :bw] = temp2[...].astype(BF16)
    dth[:, bw:] = sfore[...]
    temp[:, :hid] = dot_nt(dth[...], weight(3))
    sloped(2, 4)
    temp[:, :hid] = dot_nn(grads[4], weight(2))
    sloped(1, 5)
    temp[:, :hid] = dot_nn(grads[5], weight(1))
    sloped(0, 6)
    pgb[...] = dot_nn(grads[6], weight(0)).astype(BF16)
    for copy in a_cm + a_zm + [x for y in a_nm for x in y]:
        copy.wait_send()
    r_cf.wait_recv()

    def add_f(j):
        for z in range(nc):
            cf[j, z] = (wf[j, z, core].astype(F32) + cf[j, z].astype(F32)).astype(BF16)

    each(nn, add_f)
    r_zf = [go_send(cf.at[:, chip ^ e], zf.at[e], net.at(e=e)) for e in range(1, nc)]
    put_weight(5, dot_tn(grads[0], act[4]))
    put_weight(4, dot_tn(grads[1], act[3]))
    put_weight(3, dot_tn(act[2], dth[...]))
    put_weight(2, dot_tn(grads[4], act[1]))
    put_weight(1, dot_tn(grads[5], act[0]))
    put_weight(0, dot_tn(grads[6], pooled[...]))
    r_cm = go_send(wmid.at[:, 1 - core], cm, net.at(c=1))
    for k, slot in enumerate((6, 5, 4, 3, 2, 1, 0)):
        bt[0, k // 2 : k // 2 + 1, (k % 2) * hid : (k % 2 + 1) * hid] = sums(grads[slot])
    r_cv = go_send(bt.at[0], bl.at[0], net.at(c=1))
    for copy in a_f3:
        copy.wait_recv()
    every = f3a[...].reshape(nn * rows, hid)
    gk[...] = dot_tn(every, bg[...]).astype(BF16).reshape(nc, 2, c.hw, piece)
    go[...] = dot_tn(every, fut[...]).astype(BF16).reshape(nc, 2, c.hw, part)
    r_ck = [go_send(gk.at[:, 1 - core], ck, net.at(c=1)), go_send(go.at[:, 1 - core], co, net.at(c=1))]
    r_cm.wait_recv()
    for z in range(nc):
        cm[z] = (wmid[z, core].astype(F32) + cm[z].astype(F32)).astype(BF16)
    r_nm = [go_send(cm.at[:, n ^ d], nm.at[d], net.at(d=d)) for d in range(1, nn)]
    r_cv.wait_recv()
    bt[1] = bt[0] + bl[0]
    r_zv = [go_send(bt.at[1], bl.at[e], net.at(e=e)) for e in range(1, nc)]
    for copy in r_ck:
        copy.wait_recv()
    for z in range(nc):
        ck[z] = (gk[z, core].astype(F32) + ck[z].astype(F32)).astype(BF16)
        co[z] = (go[z, core].astype(F32) + co[z].astype(F32)).astype(BF16)
    r_zk = [go_send(ck.at[chip ^ e], zk.at[e], net.at(e=e)) for e in range(1, nc)]
    r_zo = [go_send(co.at[chip ^ e], zo.at[e], net.at(e=e)) for e in range(1, nc)]
    for j in range(nn):
        temp[:, :piece] = dot_nt(pgb[:, j * c.poolw : (j + 1) * c.poolw], pool[...])

        def join(r, j=j):
            at = ds(r, unit)
            x = land_g[j, at, :].astype(F32) + temp[at, :piece]
            ser[at, j * piece : (j + 1) * piece] = jnp.where(row_mask(j, r), x, 0).astype(BF16)

        row_loop(rows, unit, join)
    c_tid = local(ser, tid_out)
    for copy in a_tw:
        copy.wait_recv()
    c_sa.wait()
    for copy in a_sa:
        copy.wait_recv()
    c_land = local(land_s, chunk)
    c_land.wait()

    def outputs(j):
        at = ds(pl.multiple_of(j * rows, rows), rows)
        temp[:, :piece] = dot_nn(twa[j], mix_b[n])

        def first(r):
            x = chunk[j, ds(r, unit), :].astype(F32) - temp[ds(r, unit), :piece] * c.scale
            chunk[j, ds(r, unit), :] = x.astype(BF16)

        row_loop(rows, unit, first)
        temp[:, :piece] = dot_nn(f3a[j], wk[...].reshape(hid, piece))

        def second(r):
            x = chunk[j, ds(r, unit), :].astype(F32) - (temp[ds(r, unit), :piece] + kbias[...])
            chunk[j, ds(r, unit), :] = jnp.where(piece_mask(j, r), x, 0).astype(BF16)

        row_loop(rows, unit, second)
        pred[at, :] = (
            dot_nn(twa[j], mix_f[n]) * c.scale_f
            + dot_nn(f3a[j], wo[...].reshape(hid, part))
            + obias_own[...]
        )

    each(nn, outputs)
    c_left = [local(chunk.at[j], left_out.at[ds(j * rows, rows)]) for j in range(nn)]
    c_pred = local(pred, pred_out)
    for copy in r_zv:
        copy.wait_recv()
    total = bt[1]
    for e in range(1, nc):
        total += bl[e]
    bt[2] = total
    r_nv = [go_send(bt.at[2], bl.at[nc - 1 + d], net.at(d=d)) for d in range(1, nn)]
    for copy in r_nm:
        copy.wait_recv()
    for z in range(nc):
        total = cm[z, n].astype(F32)
        for d in range(1, nn):
            total += nm[d, z].astype(F32)
        m2[z] = total.astype(BF16)
    r_zm = [go_send(m2.at[chip ^ e], zm.at[e], net.at(e=e)) for e in range(1, nc)]
    for copy in r_zf:
        copy.wait_recv()

    def sum_f(j):
        total = cf[j, chip].astype(F32)
        for e in range(1, nc):
            total += zf[e, j].astype(F32)
        f2[j] = total.astype(BF16)

    each(nn, sum_f)
    r_nf = [go_send(f2.at[n ^ d], nf.at[d], net.at(d=d)) for d in range(1, nn)]
    for copy in r_zk + r_zo:
        copy.wait_recv()
    total, other = ck[chip].astype(F32), co[chip].astype(F32)
    for e in range(1, nc):
        total += zk[e].astype(F32)
        other += zo[e].astype(F32)
    ok[...] = total
    oo[...] = other
    for copy in r_nv:
        copy.wait_recv()
    total = bt[2]
    for d in range(1, nn):
        total += bl[nc - 1 + d]
    obias[...] = total
    for copy in r_zm:
        copy.wait_recv()
    total = m2[chip].astype(F32)
    for e in range(1, nc):
        total += zm[e].astype(F32)
    om[...] = total
    for copy in r_nf:
        copy.wait_recv()
    total = f2[n].astype(F32)
    for d in range(1, nn):
        total += nf[d].astype(F32)
    of[...] = total
    waited = a_cf + a_zf + a_fn + a_cm + a_zm + [x for y in a_nm for x in y]
    for copy in keep:
        if not any(copy is x for x in waited):
            copy.wait_send()
    for copy in [c_tid, c_pred] + c_left:
        copy.wait()


def take_bias(kbias, obias_own, fkb, fob, j, piece, part):
    kbias[...] = fkb[:, j * piece : (j + 1) * piece]
    obias_own[...] = fob[:, j * part : (j + 1) * part]


def fast(nn, nw, series, padding, *rest):
    (cf, cfb, cs, csb, ct, ctb, cb, cbb, ff, ffb, fs, fsb, ft, ftb, fk, fkb, fo, fob, grad, fut) = rest
    nc = nw // 2
    rows, length = series.shape
    piece, part = grad.shape[1], fut.shape[1]
    ahead = part * nn
    hid = cfb.shape[0]
    hs, hw = hid // (nn * nw), hid // nw
    back_count, fore_count = KB, cbb.shape[0] - KB
    bw, fw = up(back_count, LANE), up(fore_count, LANE)
    pick, mix_b, mix_f, all_f = window_tables(nn, length, ahead, back_count, fore_count)
    width = pick.shape[2]
    pools = piece // POOL
    poolw = up(pools, LANE)
    pool = np.zeros((piece, poolw), np.float32)
    pool[np.arange(piece), np.arange(piece) // POOL] = 1 / POOL
    first = jnp.pad(cf.reshape(hs, nn, pools), ((0, 0), (0, 0), (0, poolw - pools))).reshape(hs, -1)
    mids = (first, cs, ct, spread_basis(cb, back_count, bw, fw), fs, ft)
    off = np.concatenate([[0], np.cumsum([m.shape[1] for m in mids])]).tolist()
    mid = jnp.concatenate(mids, axis=1)
    mw = off[-1]
    pw = up(piece, LANE)
    c = types.SimpleNamespace(
        nn=nn, nc=nc, rows=rows, piece=piece, part=part, hid=hid, hs=hs, hw=hw, pw=pw, bw=bw,
        off=off, poolw=poolw,
        scale=1.0 / (2 * (length // back_count)),
        scale_f=1.0 / (2 * (ahead // fore_count)),
    )
    anyspec = pl.BlockSpec(memory_space=pl.ANY)
    vspec = pl.BlockSpec(memory_space=pltpu.VMEM)
    S, V = jax.ShapeDtypeStruct, pltpu.VMEM
    bs = (up(4 + 2 * nn, 8), max(2 * hid, pw))
    ncopies = 24 + 10 * (nn + nc) + 2 * nn * nc
    line = lambda b: b.reshape(1, -1)
    small = (cfb, csb, ctb, spread_basis(line(cbb), back_count, bw, fw), ffb, fsb, ftb, fkb, fob)
    scratch = [
        V((rows, length), BF16),
        V((nn, rows, piece), BF16),
        V((nn, rows, piece), BF16),
        V((nn * rows, piece), BF16),
        V((nn * rows, part), BF16),
        V((nc, 2, nn, hs, mw), BF16),
        V((nn, nc, 2, hw, piece), BF16),
        V((nc, 2, hw, piece), BF16),
        V((nc, 2, hw, part), BF16),
        V((nn, rows, hid + fw), BF16),
        V((nn, rows, hid + fw), BF16),
        V((nn, rows, hid), BF16),
        V((nn, rows, width), BF16),
        V((nn, rows, width), BF16),
        V((6, rows, hid), F32),
        V((7, rows, max(hid, bw + fw)), BF16),
        V((rows, nn * poolw), BF16),
        V((nn * rows, part), F32),
        V((nc, 2, hw, piece), BF16),
        V((nc, 2, hw, part), BF16),
        V((nc, nn, hs, mw), BF16),
        V((nn, nc, hw, piece), BF16),
        V((nc, hw, piece), BF16),
        V((nc, hw, part), BF16),
        V((nn, nc, hs, mw), BF16),
        V((nc, hs, mw), BF16),
        V((nc, hs, mw), BF16),
        V((nc, nn, hw, piece), BF16),
        V((nn, hw, piece), BF16),
        V((nn, hw, piece), BF16),
        V((nc, hw, piece), BF16),
        V((nc, hw, part), BF16),
        V((rows, max(pw, nn * poolw, hid)), F32),
        V((rows, bw), F32),
        V((7, rows, max(hid, bw + fw)), BF16),
        V((rows, fw), BF16),
        V((rows, nn * poolw), BF16),
        V((3,) + bs, F32),
        V((nn + nc,) + bs, F32),
        V((1, piece), F32),
        V((1, part), F32),
        pltpu.SemaphoreType.DMA((ncopies,)),
        pltpu.SemaphoreType.DMA((ncopies,)),
        pltpu.SemaphoreType.DMA((16 + nn,)),
    ]
    leftover, pred, tid, om, of, ok, oo, obias, _, _ = pl.pallas_call(
        functools.partial(whole, c),
        out_shape=(
            S((nn * rows, piece), BF16),
            S((nn * rows, part), F32),
            S((rows, length), BF16),
            S((hs, mw), F32),
            S((hw, piece), F32),
            S((hw, piece), F32),
            S((hw, part), F32),
            S(bs, F32),
            S((nn, rows, piece), BF16),
            S((nn, rows, piece), BF16),
        ),
        in_specs=[vspec] * 15 + [anyspec] * 7,
        out_specs=[anyspec] * 3 + [vspec] * 5 + [anyspec] * 2,
        scratch_shapes=scratch,
        compiler_params=params(0),
    )(
        padding.reshape(-1, 1), pick, mix_b, mix_f, all_f, pool.astype(BF16), *[line(b) for b in small],
        series, grad, fut, mid, ff, fk, fo,
    )
    om = [om[:, off[i] : off[i + 1]] for i in range(6)]
    om[0] = om[0].reshape(hs, nn, poolw)[:, :, :pools].reshape(hs, -1)
    om[3] = jnp.concatenate([om[3][:, :back_count], om[3][:, bw : bw + fore_count]], axis=1)
    flat = [obias[k // 2, (k % 2) * hid : (k % 2 + 1) * hid] for k in range(7)]
    tg = flat[3]
    flat[3] = jnp.concatenate([tg[:back_count], tg[bw : bw + fore_count]])
    back_sum = obias[4 : 4 + nn, :piece].reshape(-1)
    fore_sum = obias[4 + nn : 4 + 2 * nn, :part].reshape(-1)
    return (
        leftover,
        pred,
        tid,
        om[0],
        flat[0],
        om[1],
        flat[1],
        om[2],
        flat[2],
        om[3],
        flat[3],
        of,
        flat[4],
        om[4],
        flat[5],
        om[5],
        flat[6],
        ok,
        back_sum,
        oo,
        fore_sum,
    )


def upsample(coef, length):
    coef_count = coef.shape[1]
    stride = length // coef_count
    halfway = stride // 2
    padded = jnp.concatenate([coef[:, :1], coef, coef[:, -1:]], axis=1)
    preceding = jnp.repeat(padded[:, :coef_count], stride, axis=1)
    central = jnp.repeat(padded[:, 1 : coef_count + 1], stride, axis=1)
    following = jnp.repeat(padded[:, 2:], stride, axis=1)
    offsets = jnp.arange(length, dtype=jnp.int32) % stride
    in_front = offsets < halfway
    fraction = (
        jnp.where(in_front, offsets + halfway, offsets - halfway).astype(jnp.float32) + 0.5
    ) / stride
    lower_val = jnp.where(in_front[None, :], preceding, central)
    upper_val = jnp.where(in_front[None, :], central, following)
    return lower_val * (1.0 - fraction) + upper_val * fraction


def silu_slope(value):
    sigma = jax.nn.sigmoid(value)
    return sigma * (1.0 + value * (1.0 - sigma))


def project_rows(rows_in, matrix):
    return lax.dot_general(
        rows_in, matrix, (((1,), (1,)), ((), ())), preferred_element_type=jnp.float32
    )


def apply_rows(rows_in, matrix):
    return jnp.dot(rows_in, matrix, preferred_element_type=jnp.float32)


def column_outer(first_rows, second_rows):
    return lax.dot_general(
        first_rows, second_rows, (((0,), (0,)), ((), ())), preferred_element_type=jnp.float32
    )


def own_slice(values, begin, amount):
    return lax.dynamic_slice_in_dim(values, begin, amount, 0)


def column_sums(values):
    return jnp.sum(values.astype(jnp.float32), axis=0)


def general(
    series,
    padding,
    coarse_first,
    coarse_first_bias,
    coarse_second,
    coarse_second_bias,
    coarse_third,
    coarse_third_bias,
    coarse_basis,
    coarse_basis_bias,
    fine_first,
    fine_first_bias,
    fine_second,
    fine_second_bias,
    fine_third,
    fine_third_bias,
    fine_back,
    fine_back_bias,
    fine_fore,
    detailed_predict_offset,
    grad_resid,
    future_cotangent_array,
):
    slim_breadth = lax.axis_size("narrow")
    slim_position = lax.axis_index("narrow")
    onsite_tally, length = series.shape
    ahead = future_cotangent_array.shape[1] * slim_breadth
    sample_group = onsite_tally // PASSES
    piece = length // slim_breadth
    predicted_portion = ahead // slim_breadth
    group_pads = padding.reshape(slim_breadth, onsite_tally)
    own_pads = lax.dynamic_slice_in_dim(group_pads, slim_position, 1, 0)[0]
    steps_all = jnp.arange(length, dtype=jnp.int32)
    time_start = slim_position * piece
    predict_onset = slim_position * predicted_portion
    steps_piece = time_start + jnp.arange(piece, dtype=jnp.int32)
    back_bias = lax.dynamic_slice_in_dim(fine_back_bias, time_start, piece, 0)
    predict_offset = lax.dynamic_slice_in_dim(
        detailed_predict_offset, predict_onset, predicted_portion, 0
    )
    resid_grid = grad_resid.reshape(slim_breadth, PASSES, sample_group, piece)
    predict_mesh = future_cotangent_array.reshape(
        slim_breadth, PASSES, sample_group, predicted_portion
    )
    own_start = slim_position * sample_group
    coarse_local = (
        coarse_first,
        coarse_second,
        coarse_third,
        coarse_basis,
        fine_second,
        fine_third,
    )
    fine_local = (fine_first, fine_back, fine_fore)
    totals = tuple((jnp.zeros(w.shape, jnp.float32) for w in coarse_local))
    fine_totals = tuple((jnp.zeros(w.shape, jnp.float32) for w in fine_local))
    bias_totals = tuple(
        (
            jnp.zeros(b.shape, jnp.float32)
            for b in (
                coarse_first_bias,
                coarse_second_bias,
                coarse_third_bias,
                coarse_basis_bias,
                fine_first_bias,
                fine_second_bias,
                fine_third_bias,
                fine_back_bias,
                detailed_predict_offset,
            )
        )
    )
    residual_parts = []
    predicted_portions = []
    grad_parts = []
    for iteration_index in range(PASSES):
        shared = (
            lax.all_gather(coarse_first, ("wide", "narrow"), axis=0, tiled=True),
            lax.all_gather(coarse_second, ("wide", "narrow"), axis=0, tiled=True),
            lax.all_gather(coarse_third, ("wide", "narrow"), axis=0, tiled=True),
            lax.all_gather(coarse_basis, ("wide", "narrow"), axis=0, tiled=True),
            lax.all_gather(fine_second, ("wide", "narrow"), axis=0, tiled=True),
            lax.all_gather(fine_third, ("wide", "narrow"), axis=0, tiled=True),
        )
        pieces = (
            lax.all_gather(fine_first, "wide", axis=0, tiled=True),
            lax.all_gather(fine_back, "wide", axis=0, tiled=True),
            lax.all_gather(fine_fore, "wide", axis=0, tiled=True),
        )
        weight_one, weight_two, weight_three, weight_basis, inner_two, inner_three = shared
        inner_one, inner_back, inner_fore = pieces
        lower = iteration_index * sample_group
        mask = (steps_all[None, :] >= own_pads[lower : lower + sample_group, None]).astype(
            jnp.float32
        )
        started = series[lower : lower + sample_group].astype(jnp.float32) * mask
        pooled = jnp.mean(started.reshape(sample_group, length // POOL, POOL), axis=2).astype(
            jnp.bfloat16
        )
        linear_one = project_rows(pooled, weight_one) + coarse_first_bias
        hidden_one = jax.nn.silu(linear_one).astype(jnp.bfloat16)
        linear_two = project_rows(hidden_one, weight_two) + coarse_second_bias
        hidden_two = jax.nn.silu(linear_two).astype(jnp.bfloat16)
        linear_three = project_rows(hidden_two, weight_three) + coarse_third_bias
        hidden_three = jax.nn.silu(linear_three).astype(jnp.bfloat16)
        theta = apply_rows(hidden_three, weight_basis) + coarse_basis_bias
        backcast = upsample(theta[:, :KB], length)
        coarse_fore = upsample(theta[:, KB:], ahead)
        residual_here = (started - backcast) * mask
        sent_resid, sent_fore = (
            lax.all_to_all(
                residual_here.astype(jnp.bfloat16),
                "narrow",
                split_axis=1,
                concat_axis=0,
                tiled=True,
            ),
            lax.all_to_all(
                coarse_fore.astype(jnp.bfloat16), "narrow", split_axis=1, concat_axis=0, tiled=True
            ),
        )
        pads_here = group_pads[:, lower : lower + sample_group].reshape(-1)
        piece_mask = (steps_piece[None, :] >= pads_here[:, None]).astype(jnp.float32)
        first_partial = project_rows(sent_resid, inner_one)
        lift_one = lax.psum(first_partial, "narrow") + fine_first_bias
        fine_one = jax.nn.silu(lift_one).astype(jnp.bfloat16)
        lift_two = project_rows(fine_one, inner_two) + fine_second_bias
        fine_two = jax.nn.silu(lift_two).astype(jnp.bfloat16)
        lift_three = project_rows(fine_two, inner_three) + fine_third_bias
        fine_three = jax.nn.silu(lift_three).astype(jnp.bfloat16)
        coef_back = apply_rows(fine_three, inner_back) + back_bias
        coef_fore = apply_rows(fine_three, inner_fore) + predict_offset
        residual_parts.append(
            ((sent_resid.astype(jnp.float32) - coef_back) * piece_mask)
            .astype(jnp.bfloat16)
            .reshape(slim_breadth, sample_group, piece)
        )
        predicted_portions.append(
            (sent_fore.astype(jnp.float32) + coef_fore).reshape(
                slim_breadth, sample_group, predicted_portion
            )
        )
        out_grad = (
            resid_grid[:, iteration_index]
            .reshape(slim_breadth * sample_group, piece)
            .astype(jnp.float32)
        )
        predict_cotan = predict_mesh[:, iteration_index].reshape(
            slim_breadth * sample_group, predicted_portion
        )
        back_grad = (-out_grad * piece_mask).astype(jnp.bfloat16)
        coef_partial = project_rows(back_grad, inner_back) + project_rows(predict_cotan, inner_fore)
        three_grad = lax.psum(coef_partial, "narrow")
        lift_three_grad = (three_grad * silu_slope(lift_three)).astype(jnp.bfloat16)
        lift_two_grad = (apply_rows(lift_three_grad, inner_three) * silu_slope(lift_two)).astype(
            jnp.bfloat16
        )
        lift_one_grad = (apply_rows(lift_two_grad, inner_two) * silu_slope(lift_one)).astype(
            jnp.bfloat16
        )
        own_one_grad = own_slice(lift_one_grad, own_start, sample_group)
        own_two_grad = own_slice(lift_two_grad, own_start, sample_group)
        own_three_grad = own_slice(lift_three_grad, own_start, sample_group)
        own_fine_one = own_slice(fine_one, own_start, sample_group)
        own_fine_two = own_slice(fine_two, own_start, sample_group)
        sent_grad = (out_grad * piece_mask + apply_rows(lift_one_grad, inner_one)).astype(
            jnp.bfloat16
        )
        resid_back, fore_back = (
            lax.all_to_all(sent_grad, "narrow", split_axis=0, concat_axis=1, tiled=True),
            lax.all_to_all(predict_cotan, "narrow", split_axis=0, concat_axis=1, tiled=True),
        )
        grad_inner_one = column_outer(lift_one_grad, sent_resid)
        grad_inner_back = column_outer(fine_three, back_grad)
        grad_inner_fore = column_outer(fine_three, predict_cotan)
        grad_inner_two = column_outer(own_two_grad, own_fine_one)
        grad_inner_three = column_outer(own_three_grad, own_fine_two)
        resid_grad = resid_back.astype(jnp.float32)
        back_pull = jax.vjp(lambda coef: upsample(coef, length), theta[:, :KB])[1]
        fore_pull = jax.vjp(lambda coef: upsample(coef, ahead), theta[:, KB:])[1]
        back_coef_grad = back_pull(-resid_grad * mask)[0]
        fore_coef_grad = fore_pull(fore_back.astype(jnp.float32))[0]
        theta_grad = jnp.concatenate([back_coef_grad, fore_coef_grad], axis=1).astype(jnp.bfloat16)
        coarse_three_grad = (
            project_rows(theta_grad, weight_basis) * silu_slope(linear_three)
        ).astype(jnp.bfloat16)
        coarse_two_grad = (
            apply_rows(coarse_three_grad, weight_three) * silu_slope(linear_two)
        ).astype(jnp.bfloat16)
        coarse_one_grad = (apply_rows(coarse_two_grad, weight_two) * silu_slope(linear_one)).astype(
            jnp.bfloat16
        )
        pooled_grad = apply_rows(coarse_one_grad, weight_one)
        start_grad = resid_grad * mask + jnp.repeat(pooled_grad, POOL, axis=1) / POOL
        grad_parts.append((start_grad * mask).astype(jnp.bfloat16))
        grad_weight_one = column_outer(coarse_one_grad, pooled)
        grad_weight_two = column_outer(coarse_two_grad, hidden_one)
        grad_weight_three = column_outer(coarse_three_grad, hidden_two)
        grad_weight_basis = column_outer(hidden_three, theta_grad)
        bias_terms = (
            column_sums(coarse_one_grad),
            column_sums(coarse_two_grad),
            column_sums(coarse_three_grad),
            column_sums(theta_grad),
            column_sums(own_one_grad),
            column_sums(own_two_grad),
            column_sums(own_three_grad),
            lax.dynamic_update_slice_in_dim(
                jnp.zeros((length,), jnp.float32), column_sums(back_grad), time_start, 0
            ),
            lax.dynamic_update_slice_in_dim(
                jnp.zeros((ahead,), jnp.float32), column_sums(predict_cotan), predict_onset, 0
            ),
        )
        bias_totals = tuple((total + term for total, term in zip(bias_totals, bias_terms)))
        scattered = (
            lax.psum_scatter(grad_weight_one, ("wide", "narrow"), scatter_dimension=0, tiled=True),
            lax.psum_scatter(grad_weight_two, ("wide", "narrow"), scatter_dimension=0, tiled=True),
            lax.psum_scatter(
                grad_weight_three, ("wide", "narrow"), scatter_dimension=0, tiled=True
            ),
            lax.psum_scatter(
                grad_weight_basis, ("wide", "narrow"), scatter_dimension=0, tiled=True
            ),
            lax.psum_scatter(grad_inner_two, ("wide", "narrow"), scatter_dimension=0, tiled=True),
            lax.psum_scatter(grad_inner_three, ("wide", "narrow"), scatter_dimension=0, tiled=True),
        )
        spread = (
            lax.psum_scatter(
                grad_inner_one.astype(jnp.bfloat16), "wide", scatter_dimension=0, tiled=True
            ).astype(jnp.float32),
            lax.psum_scatter(
                grad_inner_back.astype(jnp.bfloat16), "wide", scatter_dimension=0, tiled=True
            ).astype(jnp.float32),
            lax.psum_scatter(
                grad_inner_fore.astype(jnp.bfloat16), "wide", scatter_dimension=0, tiled=True
            ).astype(jnp.float32),
        )
        totals = tuple((total + term for total, term in zip(totals, scattered)))
        fine_totals = tuple((total + term for total, term in zip(fine_totals, spread)))
    bias_sums = lax.psum(
        (
            bias_totals[0],
            bias_totals[1],
            bias_totals[2],
            bias_totals[3],
            bias_totals[4],
            bias_totals[5],
            bias_totals[6],
            bias_totals[7],
            bias_totals[8],
        ),
        ("wide", "narrow"),
    )
    leftover_signal = jnp.stack(residual_parts, axis=1).reshape(slim_breadth * onsite_tally, piece)
    predicted_future = jnp.stack(predicted_portions, axis=1).reshape(
        slim_breadth * onsite_tally, predicted_portion
    )
    temporal_input_derivative = jnp.concatenate(grad_parts, axis=0)
    return (
        leftover_signal,
        predicted_future,
        temporal_input_derivative,
        totals[0],
        bias_sums[0],
        totals[1],
        bias_sums[1],
        totals[2],
        bias_sums[2],
        totals[3],
        bias_sums[3],
        fine_totals[0],
        bias_sums[4],
        totals[4],
        bias_sums[5],
        totals[5],
        bias_sums[6],
        fine_totals[1],
        bias_sums[7],
        fine_totals[2],
        bias_sums[8],
    )


def fits(nn, nw, series, padding, first, first_bias, *rest):
    hid, length = first_bias.shape[0], series.shape[1]
    paired = all(k & (k - 1) == 0 for k in (nn, nw)) and nw % 2 == 0
    return paired and hid % (16 * nn * nw) == 0 and length % (POOL * nn) == 0 and series.shape[0] % LANE == 0


def solution(mesh):
    both, rows = P(("wide", "narrow"), None), P("wide", "narrow")
    in_specs = (both, P("wide"))
    in_specs += (both, P()) * 4 + (rows, P()) + (both, P()) * 2 + (rows, P()) * 2 + (rows, rows)
    out_specs = (rows, rows, both) + (both, P()) * 4 + (rows, P()) + (both, P()) * 2 + (rows, P()) * 2
    nn, nw = mesh.shape["narrow"], mesh.shape["wide"]

    def body(*args):
        if fits(nn, nw, *args):
            return fast(nn, nw, *args)
        return general(*args)

    return jax.shard_map(body, mesh=mesh, in_specs=in_specs, out_specs=out_specs, check_vma=False)
```

```python
import functools
import types

import jax
import jax.numpy as jnp
import numpy as np
from jax import lax
from jax.experimental import pallas as pl
from jax.experimental.pallas import tpu as pltpu
from jax.sharding import PartitionSpec as P

MESH = pl.DeviceIdType.MESH
POOL = 4
KB = 300
PASSES = 1
LANE = 128
F32 = jnp.float32
BF16 = jnp.bfloat16


def up(value, unit):
    return -(-value // unit) * unit


def interp_table(count, length):
    stride = length // count
    table = np.zeros((count, length), np.float32)
    for t in range(length):
        doubled = 2 * t + 1 - stride
        low = doubled // (2 * stride)
        part = doubled - low * 2 * stride
        table[min(max(low, 0), count - 1), t] += 2 * stride - part
        table[min(max(low + 1, 0), count - 1), t] += part
    return table


def window_tables(nn, length, ahead, back_count, fore_count):
    back, fore = interp_table(back_count, length), interp_table(fore_count, ahead)
    piece, part = length // nn, ahead // nn
    spans = []
    for n in range(nn):
        rows_b = np.nonzero(back[:, n * piece : (n + 1) * piece].any(1))[0]
        rows_f = np.nonzero(fore[:, n * part : (n + 1) * part].any(1))[0]
        spans.append((rows_b, rows_f))
    wide_b = max(len(b) for b, _ in spans)
    wide_f = max(len(f) for _, f in spans)
    width = up(wide_b + wide_f, LANE)
    bw, fw = up(back_count, LANE), up(fore_count, LANE)
    pick = np.zeros((nn, width, bw + fw), np.float32)
    mix_b = np.zeros((nn, piece, width), np.float32)
    mix_f = np.zeros((nn, part, width), np.float32)
    all_f = np.zeros((nn, part, fw), np.float32)
    for n, (rows_b, rows_f) in enumerate(spans):
        all_f[n, :, :fore_count] = fore[:, n * part : (n + 1) * part].T
        for slot, row in enumerate(rows_b):
            pick[n, slot, row] = 1
            mix_b[n, :, slot] = back[row, n * piece : (n + 1) * piece]
        for slot, row in enumerate(rows_f):
            pick[n, wide_b + slot, bw + row] = 1
            mix_f[n, :, wide_b + slot] = fore[row, n * part : (n + 1) * part]
    return wide_b + wide_f, tuple(t.astype(BF16) for t in (pick, mix_b, mix_f, all_f))


class Copy:
    def __init__(self, copy, remote):
        self.copy, self.sent, self.received = copy, False, not remote

    def wait_recv(self):
        if not self.received:
            self.copy.wait_recv()
        self.received = True

    def wait_send(self):
        if not self.sent:
            self.copy.wait_send()
        self.sent = True

    def wait(self):
        if not self.sent:
            self.copy.wait()
        self.sent = True


class Net:
    def __init__(self, sizes, sends, recvs):
        self.nn, self.nc = sizes
        self.sends, self.recvs = sends, recvs
        self.copies = []
        self.w, self.n = lax.axis_index("wide"), lax.axis_index("narrow")
        self.chip, self.core = self.w // 2, self.w % 2

    def chips(self, bit):
        return ((self.chip ^ bit) * 2 + self.core, self.n)

    def narrow(self, bit):
        return (self.w, self.n ^ bit)

    def sibling(self):
        return (self.w ^ 1, self.n)

    def hail(self):
        others = [self.narrow(d) for d in range(1, self.nn)] + [self.chips(b) for b in bits(self.nc)]
        others.append(self.sibling())
        for other in others:
            pl.semaphore_signal(pltpu.get_barrier_semaphore(), 1, device_id=other, device_id_type=MESH)
        self.others = len(others)

    def meet(self):
        pl.semaphore_wait(pltpu.get_barrier_semaphore(), self.others)

    def send(self, src, dst, to):
        k = len(self.copies)
        copy = pltpu.make_async_remote_copy(
            src_ref=src,
            dst_ref=dst,
            send_sem=self.sends.at[k],
            recv_sem=self.recvs.at[k],
            device_id=to,
            device_id_type=MESH,
        )
        copy.start()
        self.copies.append(Copy(copy, True))
        return self.copies[-1]

    def drain(self):
        for copy in self.copies:
            copy.wait_recv()
            copy.wait_send()


def bits(count):
    return [1 << k for k in reversed(range(count.bit_length() - 1))]


class Gather:
    def __init__(self, net, to, order, block, own=None):
        self.net, self.to, self.order, self.block = net, to, order, block
        self.coming = {}
        self.push(0, 0, block(0) if own is None else own)

    def push(self, m, first, src):
        for i in range(first, len(self.order)):
            b = self.order[i]
            self.coming[m | b] = (self.net.send(src, self.block(m), self.to(b)), i)

    def pull(self, m):
        copy, i = self.coming[m]
        copy.wait_recv()
        self.push(m, i + 1, self.block(m))

    def masks(self):
        out = [0]
        for b in self.order:
            out += [m | b for m in out]
        return out[1:]


class Scatter:
    def __init__(self, net, to, order, block, land, add):
        self.net, self.to, self.order, self.block, self.land, self.add = net, to, order, block, land, add
        self.masks = list(range(1 << len(order)))
        self.used = 0
        self.step = 0

    def start(self):
        b = self.order[self.step]
        rest = [m for m in self.masks if not m & b]
        self.pending = []
        for m in rest:
            copy = self.net.send(self.block(m | b), self.land(self.used), self.to(b))
            self.pending.append((copy, m, self.used))
            self.used += 1
        self.masks = rest
        self.step += 1

    def finish(self):
        for copy, m, k in self.pending:
            copy.wait_recv()
            self.add(m, k)

    def last(self):
        ((copy, m, k),) = self.pending
        copy.wait_recv()
        return k


def params(cid):
    return pltpu.CompilerParams(
        collective_id=cid, has_side_effects=True, vmem_limit_bytes=62 << 20
    )


def dot_nt(a, b):
    return lax.dot_general(a, b, (((1,), (1,)), ((), ())), preferred_element_type=F32)


def dot_nn(a, b):
    return lax.dot_general(a, b, (((1,), (0,)), ((), ())), preferred_element_type=F32)


def dot_tn(a, b):
    return lax.dot_general(a, b, (((0,), (0,)), ((), ())), preferred_element_type=F32)


def slope(v):
    s = jax.nn.sigmoid(v)
    return s * (1.0 + v * (1.0 - s))


def pad_to(x, width):
    return jnp.pad(x, ((0, 0), (0, width - x.shape[1])))


def spread_basis(x, back_count, bw, fw):
    return jnp.concatenate([pad_to(x[:, :back_count], bw), pad_to(x[:, back_count:], fw)], axis=1)


def row_loop(total, unit, body):
    def step(i, carry):
        body(pl.multiple_of(i * unit, unit), unit)
        return carry

    lax.fori_loop(0, total // unit, step, 0)
    if total % unit:
        body(total - total % unit, total % unit)


def each(count, body):
    def step(i, carry):
        body(i)
        return carry

    lax.fori_loop(0, count, step, 0)


def whole(c, *refs):
    (
        pads_in, b1, b2, b3, b4, b5, b6, b7, fkb, fob, w1, w2, w3, w4, w5, w6, mix_f_in, all_f_in,
        pick_in, mix_in, series, grad, fut_in, ff, fk, fo,
        left_out, pred_out, tid_out, om, of, ok, oo, obias, chunk_hbm, land_s,
        pick, mix_b, ser, chunk, land_g, bg, fut, wmid, wf, wk, wo, part3, land3, f3a, tw, twa,
        pre, act, pooled, pred, gf, gk, go, cm, cf, ck, co, nm, zm, zf, nf, zk, zo,
        temp, temp2, grads, sfore, pgb, pool, pads, brow, erow, bcol, ecol, bt, bl,
        p1, p2, p3, p4, p5, p6, q0, q1, q2, q3, q4, q5, q6, q7, q8, q9, mix_f, all_f, sends, recvs, own,
    ) = refs
    nn, nc, rows, piece, part, hid, pw, bw = c.nn, c.nc, c.rows, c.piece, c.part, c.hid, c.pw, c.bw
    net = Net((nn, nc), sends, recvs)
    n, chip, core = net.n, net.chip, net.core
    owned = []
    ds = pl.ds
    send = net.send
    near = bits(nn)
    orders = (near, near[::-1])
    far, back_far = bits(nc), bits(nc)[::-1]
    half_lane = [ds(0, c.half), ds(c.half, c.off[-1] - c.half)]
    halves = lambda count: [ds(0, count // 2), ds(count // 2, count // 2)]

    def local(src, dst):
        copy = pltpu.make_async_copy(src, dst, own.at[len(owned)])
        copy.start()
        owned.append(Copy(copy, False))
        return owned[-1]

    def drain():
        for copy in owned:
            copy.wait()
        net.drain()

    def weight(k):
        return wmid[:, :, :, :, c.off[k] : c.off[k + 1]].reshape(hid, c.off[k + 1] - c.off[k])

    def put_weight(k, value):
        width = c.off[k + 1] - c.off[k]
        wmid[:, :, :, :, c.off[k] : c.off[k + 1]] = value.astype(BF16).reshape(nc, 2, nn, c.hs, width)

    def lanes(j):
        return ds(pl.multiple_of(j * rows, LANE), rows)

    def steps(unit, width):
        return lax.broadcasted_iota(jnp.int32, (unit, width), 0)

    def row_mask(j, r, unit):
        return steps(unit, rows) + (j * piece + r) >= pads[:, lanes(n)]

    def activate(k, out):
        def body(r, unit):
            at = ds(r, unit)
            v = pre[k, at, :] + bcol[at, k : k + 1]
            pre[k, at, :] = v
            act[out, at, :] = (v * jax.nn.sigmoid(v)).astype(BF16)

        row_loop(hid, 32, body)

    def sloped(k, out):
        def body(r, unit):
            at = ds(r, unit)
            grads[out, at, :] = (temp[at, :] * slope(pre[k, at, :])).astype(BF16)

        row_loop(hid, 32, body)

    def sums(value):
        return dot_nt(jnp.ones((8, value.shape[1]), BF16), value)[0:1]

    net.hail()
    c_mids = [local(x, y) for x, y in zip((w1, w2, w3, w4, w5, w6), (p1, p2, p3, p4, p5, p6))]
    c_ser = local(series, ser)
    c_bg = local(grad, bg)
    c_fut = local(fut_in, fut)
    c_ff = local(ff, wf.at[n, chip, core])
    c_fk = local(fk, wk.at[chip, core])
    c_fo = local(fo, wo.at[chip, core])
    c_pick = local(pick_in, pick)
    c_mix = local(mix_in, mix_b)
    slot = wmid.at[chip, core, n]
    slot[...] = jnp.zeros_like(slot)
    for copy in c_mids:
        copy.wait()
    for j in range(nn):
        slot[:, j * c.poolw : j * c.poolw + c.pools] = p1[:, j * c.pools : (j + 1) * c.pools]
    for k, w in ((1, p2), (2, p3), (4, p5), (5, p6)):
        slot[:, c.off[k] : c.off[k + 1]] = w[...]
    slot[:, c.off[3] : c.off[3] + c.bcount] = p4[:, : c.bcount]
    slot[:, c.off[3] + bw : c.off[3] + bw + p4.shape[1] - c.bcount] = p4[:, c.bcount :]
    net.meet()

    z_mid = Gather(net, net.chips, far, lambda e: wmid.at[chip ^ e, core, n])

    def gather_mid(e):
        return [
            Gather(net, net.narrow, order, lambda m, h=h: wmid.at[chip ^ e, core, n ^ m, :, h])
            for order, h in zip(orders, half_lane)
        ]

    def pull_first(gathers):
        for g in gathers:
            g.pull(g.masks()[0])

    def pull_rest(gathers):
        for g in gathers:
            for m in g.masks()[1:]:
                g.pull(m)

    n_mid = {0: gather_mid(0)}
    n_ff = [
        Gather(net, net.narrow, order, lambda m, h=h: wf.at[n ^ m, chip, core, h], ff.at[h])
        for order, h in zip(orders, halves(c.hw))
    ]
    c_small = [
        local(x, y)
        for x, y in zip((pads_in, b1, b2, b3, b4, b5, b6, b7, fkb, fob), (q0, q1, q2, q3, q4, q5, q6, q7, q8, q9))
    ]
    c_tables = [local(mix_f_in.at[n], mix_f), local(all_f_in.at[n], all_f)]
    for copy in c_small:
        copy.wait()
    pads[...] = q0[...].reshape(1, nn * rows)
    brow[...] = jnp.zeros_like(brow)
    for k, b in enumerate((q1, q2, q3, q5, q6, q7)):
        brow[k : k + 1, :] = b[...].reshape(1, hid)
    theta_bias = q4[...].reshape(1, q4.shape[0])
    brow[6:7, : c.bcount] = theta_bias[:, : c.bcount]
    brow[6:7, bw : bw + q4.shape[0] - c.bcount] = theta_bias[:, c.bcount :]
    bcol[...] = jnp.transpose(brow[...])
    z_mid.pull(z_mid.masks()[0])
    n_mid[z_mid.masks()[0]] = gather_mid(z_mid.masks()[0])
    z_k = [
        Gather(net, net.chips, far, lambda e: wk.at[chip ^ e, core], fk),
        Gather(net, net.chips, far, lambda e: wo.at[chip ^ e, core], fo),
    ]
    pull_first(n_mid[0])
    for m in z_mid.masks()[1:]:
        z_mid.pull(m)
        n_mid[m] = gather_mid(m)
    pull_first(n_ff)
    erow[...] = jnp.zeros_like(erow)
    for j in range(nn):

        @pl.when(n == j)
        def _(j=j):
            erow[0:1, :piece] = q8[j * piece : (j + 1) * piece].reshape(1, piece)
            erow[0:1, pw : pw + part] = q9[j * part : (j + 1) * part].reshape(1, part)

    ecol[...] = jnp.transpose(erow[...])
    bt[...] = jnp.zeros_like(bt)
    twa[...] = jnp.zeros_like(twa)
    first_step = lax.broadcasted_iota(jnp.int32, (c.poolw, piece), 0) * POOL
    behind = lax.broadcasted_iota(jnp.int32, (c.poolw, piece), 1) - first_step
    pool[...] = jnp.where((behind >= 0) & (behind < POOL), 1.0 / POOL, 0.0).astype(BF16)

    pull_first(z_k)
    others = [m for m in n_mid if m]
    pull_first([g for m in others[:-1] for g in n_mid[m]])
    pull_rest(n_ff)
    c_ff.wait()
    z_f = Gather(net, net.chips, far, lambda e: wf.at[:, chip ^ e, core])
    a_cf = []

    def hand_over(e):
        block = wf.at[:, chip ^ e, core]
        a_cf.append(send(block, block, net.sibling()))

    hand_over(0)
    c_ser.wait()

    def cut_piece(j):
        for r in range(0, piece, 64):
            unit = min(64, piece - r)
            x = ser[j * piece + r : j * piece + r + unit, :]
            chunk[j, r : r + unit, :] = jnp.where(row_mask(j, r, unit), x.astype(F32), 0).astype(BF16)

    for j in range(nn // 2):
        cut_piece(j)
    pull_first(n_mid[others[-1]])
    third = up(piece // 3, 16)
    thirds = [ds(0, third), ds(third, third), ds(2 * third, piece - 2 * third)]
    c_ga = local(grad.at[:, lanes(n)], land_g.at[n])
    a_ga, a_sa = [], []

    def exchange_grad(k):
        h = thirds[k]
        for d in range(1, nn):
            a_ga.append(send(grad.at[h, lanes(n ^ d)], land_g.at[n, h], net.narrow(d)))

    def exchange_series(k):
        h = thirds[k]
        for d in range(1, nn):
            a_sa.append(send(chunk_hbm.at[n ^ d, h], land_s.at[h, lanes(n)], net.narrow(d)))

    exchange_grad(0)

    for j in range(nn // 2, nn):
        cut_piece(j)
    c_chunk = local(chunk, chunk_hbm)
    for j in range(nn):
        pooled[j * c.poolw : (j + 1) * c.poolw, :] = dot_nn(pool[...], chunk[j]).astype(BF16)
    pull_rest(z_k)
    c_fk.wait()
    c_fo.wait()
    a_ck = [send(wk.at[:, core], wk.at[:, core], net.sibling()), send(wo.at[:, core], wo.at[:, core], net.sibling())]
    c_bg.wait()
    c_fut.wait()

    def negate(r, unit):
        at = ds(r, unit)
        mask = steps(unit, nn * rows) + (n * piece + r) >= pads[...]
        bg[at, :] = jnp.where(mask, -bg[at, :].astype(F32), 0).astype(BF16)

    row_loop(piece, 16, negate)
    a_cm = []
    for e in n_mid:
        pull_rest(n_mid[e])
        block = wmid.at[chip ^ e, core]
        a_cm.append(send(block, block, net.sibling()))

    for copy in c_tables:
        copy.wait()
    for copy in a_ck:
        copy.wait_recv()

    def partial(j):
        back = wk[...].reshape(hid, piece)
        fore = wo[...].reshape(hid, part)
        part3[j, :hid, :] = (dot_nn(back, bg[:, lanes(j)]) + dot_nn(fore, fut[:, lanes(j)])).astype(BF16)
        ahead = dot_tn(all_f[...], fut[:, lanes(j)]) * c.scale_f
        part3[j, hid:, :] = ahead[: c.fcount].astype(BF16)

    each(nn, partial)

    def add_part(m, k, h):
        part3[n ^ m, h, :] = (part3[n ^ m, h, :].astype(F32) + land3[k, h, :].astype(F32)).astype(BF16)

    s_part = [
        Scatter(
            net, net.narrow, order,
            lambda m, h=h: part3.at[n ^ m, h],
            lambda k, h=h: land3.at[k, h],
            lambda m, k, h=h: add_part(m, k, h),
        )
        for order, h in zip(orders, halves(hid + c.fcount))
    ]
    for s in s_part:
        s.start()
    exchange_grad(1)

    for copy in a_cm:
        copy.wait_recv()
    pre[0] = dot_nn(weight(0), pooled[...])
    activate(0, 0)
    z_f.pull(z_f.masks()[0])
    hand_over(z_f.masks()[0])
    pre[1] = dot_nn(weight(1), act[0])
    activate(1, 1)
    pre[2] = dot_nn(weight(2), act[1])
    activate(2, 2)
    theta = act.at[6]
    theta[...] = (dot_tn(weight(3), act[2]) + bcol[:, 6:7]).astype(BF16)
    for s in s_part:
        s.finish()
        if s.step < len(near):
            s.start()
    exchange_grad(2)
    c_chunk.wait()

    c_pick.wait()
    c_mix.wait()

    def residual(j):
        tw[j] = dot_nn(pick[j], theta[...]).astype(BF16)
        temp[:piece, :] = dot_nn(mix_b[j], tw[j])

        def body(r, unit):
            at = ds(r, unit)
            x = chunk[j, at, :].astype(F32) - temp[at, :] * c.scale
            chunk[j, at, :] = jnp.where(row_mask(j, r, unit), x, 0).astype(BF16)

        row_loop(piece, 48, body)

    each(nn, residual)
    used = ds(0, c.used)
    twa[n, : c.used, :] = tw[n, : c.used, :]
    for m in z_f.masks()[1:]:
        z_f.pull(m)
        hand_over(m)
    early = len(net.copies)

    for copy in a_cf:
        copy.wait_recv()
    pre[3] = jnp.zeros((hid, rows), F32)

    def lift(j):
        pre[3] += dot_nn(wf[j].reshape(hid, piece), chunk[j])

    each(nn, lift)
    activate(3, 3)
    pre[4] = dot_nn(weight(4), act[3])
    activate(4, 4)
    pre[5] = dot_nn(weight(5), act[4])
    activate(5, 5)
    f3a[:, lanes(n)] = act[5]
    n_f3 = [
        Gather(net, net.narrow, order, lambda m, h=h: f3a.at[h, lanes(n ^ m)], act.at[5, h])
        for order, h in zip(orders, halves(hid))
    ]
    exchange_series(0)

    while s_part[0].step < len(near):
        for s in s_part:
            s.finish()
            s.start()
    k3 = [s.last() for s in s_part]

    def collect(h, k):
        def body(r, unit):
            at = ds(h.start + r, unit)
            total = part3[n, at, :].astype(F32) + land3[k, at, :].astype(F32)
            grads[0, at, :] = (total * slope(pre[5, at, :])).astype(BF16)

        return body

    cut = (hid + c.fcount) // 2
    row_loop(cut, 32, collect(ds(0, cut), k3[0]))
    row_loop(hid - cut, 32, collect(ds(cut, hid - cut), k3[1]))
    sfore[...] = (part3[n, hid:, :].astype(F32) + land3[k3[1], hid:, :].astype(F32)).astype(BF16)
    temp[:hid, :] = dot_tn(weight(5), grads[0])
    sloped(4, 1)
    temp[:hid, :] = dot_tn(weight(4), grads[1])
    sloped(3, 2)

    pull_first(n_f3)
    a_tw = [send(tw.at[n ^ d, used], twa.at[n, used], net.narrow(d)) for d in range(1, nn)]
    exchange_series(1)
    r_cf = []
    for j in range(nn):
        gf[j] = dot_nt(grads[2], chunk[j]).astype(BF16).reshape(nc, 2, c.hw, piece)
        r_cf.append(send(gf.at[j, :, 1 - core], cf.at[j], net.sibling()))

    c_ga.wait()
    for copy in a_ga:
        copy.wait_recv()
    temp2[...] = jnp.zeros_like(temp2)

    def resid_grad(j):
        temp[:piece, :] = dot_tn(wf[j].reshape(hid, piece), grads[2])

        def body(r, unit):
            at = ds(r, unit)
            x = land_g[j, at, :].astype(F32) + temp[at, :]
            land_g[j, at, :] = jnp.where(row_mask(j, r, unit), x, 0).astype(BF16)

        row_loop(piece, 48, body)
        pull = (dot_tn(mix_b[j], land_g[j]) * -c.scale).astype(BF16)
        temp2[...] += dot_tn(pick[j, :, :bw], pull)

    each(nn // 2, resid_grad)
    for j in range(nn):
        r_cf[j].wait_recv()

    def add_f(j):
        for z in range(nc):
            cf[j, z] = (gf[j, z, core].astype(F32) + cf[j, z].astype(F32)).astype(BF16)

    each(nn, add_f)

    def add_zf(e, k):
        def body(j):
            cf[j, chip ^ e] = (cf[j, chip ^ e].astype(F32) + zf[k, j].astype(F32)).astype(BF16)

        each(nn, body)

    r_zf = Scatter(net, net.chips, back_far, lambda e: cf.at[:, chip ^ e], lambda k: zf.at[k], add_zf)
    r_zf.start()
    each(nn - nn // 2, lambda i: resid_grad(i + nn // 2))

    dth = grads.at[3]
    dth[:bw, :] = temp2[...].astype(BF16)
    dth[bw:, :] = jnp.zeros_like(dth[bw:, :])
    dth[bw : bw + c.fcount, :] = sfore[...]
    temp[:hid, :] = dot_nn(weight(3), dth[...])
    sloped(2, 4)
    temp[:hid, :] = dot_tn(weight(2), grads[4])
    sloped(1, 5)
    temp[:hid, :] = dot_tn(weight(1), grads[5])
    sloped(0, 6)
    pgb[...] = dot_tn(weight(0), grads[6]).astype(BF16)
    for copy in net.copies[: early]:
        copy.wait_send()
    put_weight(5, dot_nt(grads[0], act[4]))
    put_weight(4, dot_nt(grads[1], act[3]))
    put_weight(3, dot_nt(act[2], dth[...]))
    put_weight(2, dot_nt(grads[4], act[1]))
    put_weight(1, dot_nt(grads[5], act[0]))
    put_weight(0, dot_nt(grads[6], pooled[...]))
    r_cm = send(wmid.at[:, 1 - core], cm, net.sibling())

    bt[0, ds(4 + n, 1), :piece] = sums(bg[...])
    bt[0, ds(4 + nn + n, 1), :part] = sums(fut[...])
    for k, slot_k in enumerate((6, 5, 4, 3, 2, 1, 0)):
        bt[0, k // 2 : k // 2 + 1, (k % 2) * hid : (k % 2 + 1) * hid] = sums(grads[slot_k])
    travel = [net.sibling()] + [net.narrow(b) for b in near] + [net.chips(b) for b in back_far]
    v_copies = []

    def send_bias():
        k = len(v_copies)
        v_copies.append(send(bt.at[k], bl.at[k], travel[k]))

    def add_bias():
        k = len(v_copies) - 1
        v_copies[k].wait_recv()
        bt[k + 1] = bt[k] + bl[k]

    send_bias()
    pull_rest(n_f3)
    gk[...] = dot_nt(f3a[...], bg[...]).astype(BF16).reshape(nc, 2, c.hw, piece)
    go[...] = dot_nt(f3a[...], fut[...]).astype(BF16).reshape(nc, 2, c.hw, part)
    r_ck = [send(gk.at[:, 1 - core], ck, net.sibling()), send(go.at[:, 1 - core], co, net.sibling())]
    r_cm.wait_recv()
    for z in range(nc):
        cm[z] = (wmid[z, core].astype(F32) + cm[z].astype(F32)).astype(BF16)

    def add_nm(m, k, h):
        cm[:, n ^ m, :, h] = (cm[:, n ^ m, :, h].astype(F32) + nm[k, :, :, h].astype(F32)).astype(BF16)

    r_nm = [
        Scatter(
            net, net.narrow, order,
            lambda m, h=h: cm.at[:, n ^ m, :, h],
            lambda k, h=h: nm.at[k, :, :, h],
            lambda m, k, h=h: add_nm(m, k, h),
        )
        for order, h in zip(orders, half_lane)
    ]
    for s in r_nm:
        s.start()
    exchange_series(2)
    add_bias()
    send_bias()

    for copy in r_ck:
        copy.wait_recv()
    for z in range(nc):
        ck[z] = (gk[z, core].astype(F32) + ck[z].astype(F32)).astype(BF16)
        co[z] = (go[z, core].astype(F32) + co[z].astype(F32)).astype(BF16)

    def add_k(e, k):
        ck[chip ^ e] = (ck[chip ^ e].astype(F32) + zk[k].astype(F32)).astype(BF16)

    def add_o(e, k):
        co[chip ^ e] = (co[chip ^ e].astype(F32) + zo[k].astype(F32)).astype(BF16)

    r_zk = [
        Scatter(net, net.chips, back_far, lambda e: ck.at[chip ^ e], lambda k: zk.at[k], add_k),
        Scatter(net, net.chips, back_far, lambda e: co.at[chip ^ e], lambda k: zo.at[k], add_o),
    ]

    def series_grad(j):
        temp[:piece, :] = dot_tn(pool[...], pgb[j * c.poolw : (j + 1) * c.poolw, :])
        for r in range(0, piece, 64):
            unit = min(64, piece - r)
            x = land_g[j, r : r + unit, :].astype(F32) + temp[r : r + unit, :]
            x = jnp.where(row_mask(j, r, unit), x, 0).astype(BF16)
            ser[j * piece + r : j * piece + r + unit, :] = x

    def outputs(j):
        temp[:piece, :] = dot_nn(mix_b[n], twa[j])

        def first(r, unit):
            at = ds(r, unit)
            x = chunk[j, at, :].astype(F32) - temp[at, :] * c.scale
            chunk[j, at, :] = x.astype(BF16)

        row_loop(piece, 48, first)
        temp[:piece, :] = dot_tn(wk[...].reshape(hid, piece), f3a[:, lanes(j)])

        def second(r, unit):
            at = ds(r, unit)
            x = chunk[j, at, :].astype(F32) - (temp[at, :] + ecol[at, 0:1])
            mask = steps(unit, rows) + (n * piece + r) >= pads[:, lanes(j)]
            chunk[j, at, :] = jnp.where(mask, x, 0).astype(BF16)

        row_loop(piece, 48, second)
        pred[:, lanes(j)] = (
            dot_nn(mix_f[...], twa[j]) * c.scale_f
            + dot_tn(wo[...].reshape(hid, part), f3a[:, lanes(j)])
            + ecol[pw : pw + part, 0:1]
        )

    for j in range(nn // 2):
        series_grad(j)
    r_zf.finish()
    r_zf.start()
    for s in r_zk:
        s.start()
    for j in range(nn // 2, nn):
        series_grad(j)
    c_tid = local(ser, tid_out)
    for s in r_nm:
        s.finish()
        s.start()
    add_bias()
    send_bias()


    def add_nf(m, k, h):
        cf[n ^ m, chip, h, :] = (cf[n ^ m, chip, h, :].astype(F32) + nf[k, h, :].astype(F32)).astype(BF16)

    def add_zm(e, k):
        cm[chip ^ e, n] = (cm[chip ^ e, n].astype(F32) + zm[k].astype(F32)).astype(BF16)

    r_nf = lambda: [
        Scatter(
            net, net.narrow, order,
            lambda m, h=h: cf.at[n ^ m, chip, h],
            lambda k, h=h: nf.at[k, h],
            lambda m, k, h=h: add_nf(m, k, h),
        )
        for order, h in zip(orders, halves(c.hw))
    ]
    r_zm = Scatter(net, net.chips, back_far, lambda e: cm.at[chip ^ e, n], lambda k: zm.at[k], add_zm)
    for copy in a_tw:
        copy.wait_recv()
    r_zf.finish()
    r_nf = r_nf()
    for s in r_nf:
        s.start()
    for s in r_nm:
        s.finish()
    r_zm.start()
    add_bias()
    send_bias()
    for s in r_zk:
        s.finish()
        s.start()
    for copy in a_sa:
        copy.wait_recv()
    c_land = [local(chunk_hbm.at[n], chunk.at[n])]
    c_land += [local(land_s.at[:, lanes(n ^ d)], chunk.at[n ^ d]) for d in range(1, nn)]
    for copy in c_land:
        copy.wait()

    each(nn // 2, outputs)
    for s in r_nf:
        s.finish()
        s.start()
    r_zm.finish()
    r_zm.start()
    add_bias()
    send_bias()
    each(nn - nn // 2, lambda i: outputs(i + nn // 2))
    c_left = [local(chunk.at[j], left_out.at[:, lanes(j)]) for j in range(nn)]
    c_pred = local(pred, pred_out)

    for s in r_zk:
        s.finish()
    ok[...] = ck[chip].astype(F32)
    oo[...] = co[chip].astype(F32)
    for s in r_nf:
        s.finish()
    of[...] = cf[n, chip].astype(F32)
    add_bias()
    obias[...] = bt[len(travel)]
    r_zm.finish()
    om[...] = cm[chip, n].astype(F32)
    drain()


def finish(c, *refs):
    om, of, ok, oo, obias = refs[:5]
    (
        g1, v1, g2, v2, g3, v3, g4, v4, gf, vf1, g5, vf2, g6, vf3, gk, vk, go, vo,
    ) = refs[5:]
    nn, piece, part, hid, bw = c.nn, c.piece, c.part, c.hid, c.bw
    for j in range(nn):
        g1[:, j * c.pools : (j + 1) * c.pools] = om[:, j * c.poolw : j * c.poolw + c.pools]
    for k, g in ((1, g2), (2, g3), (4, g5), (5, g6)):
        g[...] = om[:, c.off[k] : c.off[k + 1]]
    fore = g4.shape[1] - c.bcount
    g4[:, : c.bcount] = om[:, c.off[3] : c.off[3] + c.bcount]
    g4[:, c.bcount :] = om[:, c.off[3] + bw : c.off[3] + bw + fore]
    gf[...] = of[...]
    gk[...] = ok[...]
    go[...] = oo[...]
    for k, v in enumerate((v1, v2, v3, None, vf1, vf2, vf3)):
        if v is not None:
            v[...] = obias[k // 2 : k // 2 + 1, (k % 2) * hid : (k % 2 + 1) * hid].reshape(hid)
    theta = obias[1:2, hid : 2 * hid]
    v4[...] = jnp.concatenate([theta[:, : c.bcount], theta[:, bw : bw + fore]], axis=1).reshape(v4.shape[0])
    vk[...] = jnp.concatenate([obias[4 + j : 5 + j, :piece] for j in range(nn)], axis=1).reshape(vk.shape[0])
    vo[...] = jnp.concatenate([obias[4 + nn + j : 5 + nn + j, :part] for j in range(nn)], axis=1).reshape(vo.shape[0])


def fast(nn, nw, series, padding, *rest):
    (cf, cfb, cs, csb, ct, ctb, cb, cbb, ff, ffb, fs, fsb, ft, ftb, fk, fkb, fo, fob, grad, fut) = rest
    nc = nw // 2
    rows, length = series.shape
    piece, part = grad.shape[1], fut.shape[1]
    ahead = part * nn
    hid = cfb.shape[0]
    hs, hw = hid // (nn * nw), hid // nw
    back_count, fore_count = KB, cbb.shape[0] - KB
    bw, fw = up(back_count, LANE), up(fore_count, LANE)
    used, (pick, mix_b, mix_f, all_f) = window_tables(nn, length, ahead, back_count, fore_count)
    width = pick.shape[1]
    fcount = up(fore_count, 16)
    pools = piece // POOL
    poolw = up(pools, LANE)
    widths = (nn * poolw, hid, hid, bw + fw, hid, hid)
    off = np.concatenate([[0], np.cumsum(widths)]).tolist()
    mw = off[-1]
    pw = up(piece, LANE)
    assert bw + fw == hid
    c = types.SimpleNamespace(
        nn=nn, nc=nc, rows=rows, piece=piece, part=part, hid=hid, hs=hs, hw=hw, pw=pw, bw=bw,
        off=off, poolw=poolw, pools=pools, used=up(used, 16), fcount=fcount,
        bcount=back_count, half=up(mw // 2, LANE),
        scale=1.0 / (2 * (length // back_count)),
        scale_f=1.0 / (2 * (ahead // fore_count)),
    )
    anyspec = pl.BlockSpec(memory_space=pl.ANY)
    vspec = pl.BlockSpec(memory_space=pltpu.VMEM)
    S, V = jax.ShapeDtypeStruct, pltpu.VMEM
    bs = (up(4 + 2 * nn, 8), max(2 * hid, pw))
    stages = 1 + len(bits(nn)) + len(bits(nc))
    gathers = (nc - 1) + 2 * nc * (nn - 1) + 2 * (nn - 1) + 3 * (nc - 1) + 2 + 2 * nc
    ncopies = gathers + 12 * (nn + nc) + 2 * nn * nc
    qw = up(part, LANE)
    scratch = [
        V((nn, width, bw + fw), BF16),
        V((nn, piece, width), BF16),
        V((length, rows), BF16),
        V((nn, piece, rows), BF16),
        V((nn, piece, rows), BF16),
        V((piece, nn * rows), BF16),
        V((part, nn * rows), BF16),
        V((nc, 2, nn, hs, mw), BF16),
        V((nn, nc, 2, hw, piece), BF16),
        V((nc, 2, hw, piece), BF16),
        V((nc, 2, hw, part), BF16),
        V((nn, hid + fcount, rows), BF16),
        V((nn - 1, hid + fcount, rows), BF16),
        V((hid, nn * rows), BF16),
        V((nn, width, rows), BF16),
        V((nn, width, rows), BF16),
        V((6, hid, rows), F32),
        V((7, hid, rows), BF16),
        V((nn * poolw, rows), BF16),
        V((part, nn * rows), F32),
        V((nn, nc, 2, hw, piece), BF16),
        V((nc, 2, hw, piece), BF16),
        V((nc, 2, hw, part), BF16),
        V((nc, nn, hs, mw), BF16),
        V((nn, nc, hw, piece), BF16),
        V((nc, hw, piece), BF16),
        V((nc, hw, part), BF16),
        V((nn - 1, nc, hs, mw), BF16),
        V((nc - 1, hs, mw), BF16),
        V((nc - 1, nn, hw, piece), BF16),
        V((nn - 1, hw, piece), BF16),
        V((nc - 1, hw, piece), BF16),
        V((nc - 1, hw, part), BF16),
        V((max(piece, hid), rows), F32),
        V((bw, rows), F32),
        V((7, hid, rows), BF16),
        V((fcount, rows), BF16),
        V((nn * poolw, rows), BF16),
        V((poolw, piece), BF16),
        V((1, nn * rows), jnp.int32),
        V((8, hid), F32),
        V((8, pw + qw), F32),
        V((hid, 8), F32),
        V((pw + qw, 8), F32),
        V((stages + 1,) + bs, F32),
        V((stages,) + bs, F32),
    ]
    scratch += [V(w.shape, BF16) for w in (cf, cs, ct, cb, fs, ft)]
    scratch += [V(b.shape, b.dtype) for b in (padding, cfb, csb, ctb, cbb, ffb, fsb, ftb, fkb, fob)]
    scratch += [
        V(mix_f.shape[1:], BF16),
        V(all_f.shape[1:], BF16),
        pltpu.SemaphoreType.DMA((ncopies,)),
        pltpu.SemaphoreType.DMA((ncopies,)),
        pltpu.SemaphoreType.DMA((40 + 2 * nn,)),
    ]
    leftover, pred, tid, om, of, ok, oo, obias, _, _ = pl.pallas_call(
        functools.partial(whole, c),
        out_shape=(
            S((piece, nn * rows), BF16),
            S((part, nn * rows), F32),
            S((length, rows), BF16),
            S((hs, mw), F32),
            S((hw, piece), F32),
            S((hw, piece), F32),
            S((hw, part), F32),
            S(bs, F32),
            S((nn, piece, rows), BF16),
            S((piece, nn * rows), BF16),
        ),
        in_specs=[anyspec] * 26,
        out_specs=[anyspec] * 3 + [vspec] * 5 + [anyspec] * 2,
        scratch_shapes=scratch,
        compiler_params=params(0),
    )(
        padding, cfb, csb, ctb, cbb, ffb, fsb, ftb, fkb, fob, cf, cs, ct, cb, fs, ft, mix_f, all_f,
        pick, mix_b, series.T, grad.T, fut.T, ff, fk, fo,
    )
    params_like = (cf, cfb, cs, csb, ct, ctb, cb, cbb, ff, ffb, fs, fsb, ft, ftb, fk, fkb, fo, fob)
    outs = pl.pallas_call(
        functools.partial(finish, c),
        out_shape=tuple(S(p.shape, F32) for p in params_like),
        in_specs=[vspec] * 5,
        out_specs=[vspec] * 18,
    )(om, of, ok, oo, obias)
    return (leftover.T, pred.T, tid.T) + tuple(outs)


def upsample(coef, length):
    coef_count = coef.shape[1]
    stride = length // coef_count
    halfway = stride // 2
    padded = jnp.concatenate([coef[:, :1], coef, coef[:, -1:]], axis=1)
    preceding = jnp.repeat(padded[:, :coef_count], stride, axis=1)
    central = jnp.repeat(padded[:, 1 : coef_count + 1], stride, axis=1)
    following = jnp.repeat(padded[:, 2:], stride, axis=1)
    offsets = jnp.arange(length, dtype=jnp.int32) % stride
    in_front = offsets < halfway
    fraction = (
        jnp.where(in_front, offsets + halfway, offsets - halfway).astype(jnp.float32) + 0.5
    ) / stride
    lower_val = jnp.where(in_front[None, :], preceding, central)
    upper_val = jnp.where(in_front[None, :], central, following)
    return lower_val * (1.0 - fraction) + upper_val * fraction


def silu_slope(value):
    sigma = jax.nn.sigmoid(value)
    return sigma * (1.0 + value * (1.0 - sigma))


def project_rows(rows_in, matrix):
    return lax.dot_general(
        rows_in, matrix, (((1,), (1,)), ((), ())), preferred_element_type=jnp.float32
    )


def apply_rows(rows_in, matrix):
    return jnp.dot(rows_in, matrix, preferred_element_type=jnp.float32)


def column_outer(first_rows, second_rows):
    return lax.dot_general(
        first_rows, second_rows, (((0,), (0,)), ((), ())), preferred_element_type=jnp.float32
    )


def own_slice(values, begin, amount):
    return lax.dynamic_slice_in_dim(values, begin, amount, 0)


def column_sums(values):
    return jnp.sum(values.astype(jnp.float32), axis=0)


def general(
    series,
    padding,
    coarse_first,
    coarse_first_bias,
    coarse_second,
    coarse_second_bias,
    coarse_third,
    coarse_third_bias,
    coarse_basis,
    coarse_basis_bias,
    fine_first,
    fine_first_bias,
    fine_second,
    fine_second_bias,
    fine_third,
    fine_third_bias,
    fine_back,
    fine_back_bias,
    fine_fore,
    detailed_predict_offset,
    grad_resid,
    future_cotangent_array,
):
    slim_breadth = lax.axis_size("narrow")
    slim_position = lax.axis_index("narrow")
    onsite_tally, length = series.shape
    ahead = future_cotangent_array.shape[1] * slim_breadth
    sample_group = onsite_tally // PASSES
    piece = length // slim_breadth
    predicted_portion = ahead // slim_breadth
    group_pads = padding.reshape(slim_breadth, onsite_tally)
    own_pads = lax.dynamic_slice_in_dim(group_pads, slim_position, 1, 0)[0]
    steps_all = jnp.arange(length, dtype=jnp.int32)
    time_start = slim_position * piece
    predict_onset = slim_position * predicted_portion
    steps_piece = time_start + jnp.arange(piece, dtype=jnp.int32)
    back_bias = lax.dynamic_slice_in_dim(fine_back_bias, time_start, piece, 0)
    predict_offset = lax.dynamic_slice_in_dim(
        detailed_predict_offset, predict_onset, predicted_portion, 0
    )
    resid_grid = grad_resid.reshape(slim_breadth, PASSES, sample_group, piece)
    predict_mesh = future_cotangent_array.reshape(
        slim_breadth, PASSES, sample_group, predicted_portion
    )
    own_start = slim_position * sample_group
    coarse_local = (
        coarse_first,
        coarse_second,
        coarse_third,
        coarse_basis,
        fine_second,
        fine_third,
    )
    fine_local = (fine_first, fine_back, fine_fore)
    totals = tuple((jnp.zeros(w.shape, jnp.float32) for w in coarse_local))
    fine_totals = tuple((jnp.zeros(w.shape, jnp.float32) for w in fine_local))
    bias_totals = tuple(
        (
            jnp.zeros(b.shape, jnp.float32)
            for b in (
                coarse_first_bias,
                coarse_second_bias,
                coarse_third_bias,
                coarse_basis_bias,
                fine_first_bias,
                fine_second_bias,
                fine_third_bias,
                fine_back_bias,
                detailed_predict_offset,
            )
        )
    )
    residual_parts = []
    predicted_portions = []
    grad_parts = []
    for iteration_index in range(PASSES):
        shared = (
            lax.all_gather(coarse_first, ("wide", "narrow"), axis=0, tiled=True),
            lax.all_gather(coarse_second, ("wide", "narrow"), axis=0, tiled=True),
            lax.all_gather(coarse_third, ("wide", "narrow"), axis=0, tiled=True),
            lax.all_gather(coarse_basis, ("wide", "narrow"), axis=0, tiled=True),
            lax.all_gather(fine_second, ("wide", "narrow"), axis=0, tiled=True),
            lax.all_gather(fine_third, ("wide", "narrow"), axis=0, tiled=True),
        )
        pieces = (
            lax.all_gather(fine_first, "wide", axis=0, tiled=True),
            lax.all_gather(fine_back, "wide", axis=0, tiled=True),
            lax.all_gather(fine_fore, "wide", axis=0, tiled=True),
        )
        weight_one, weight_two, weight_three, weight_basis, inner_two, inner_three = shared
        inner_one, inner_back, inner_fore = pieces
        lower = iteration_index * sample_group
        mask = (steps_all[None, :] >= own_pads[lower : lower + sample_group, None]).astype(
            jnp.float32
        )
        started = series[lower : lower + sample_group].astype(jnp.float32) * mask
        pooled = jnp.mean(started.reshape(sample_group, length // POOL, POOL), axis=2).astype(
            jnp.bfloat16
        )
        linear_one = project_rows(pooled, weight_one) + coarse_first_bias
        hidden_one = jax.nn.silu(linear_one).astype(jnp.bfloat16)
        linear_two = project_rows(hidden_one, weight_two) + coarse_second_bias
        hidden_two = jax.nn.silu(linear_two).astype(jnp.bfloat16)
        linear_three = project_rows(hidden_two, weight_three) + coarse_third_bias
        hidden_three = jax.nn.silu(linear_three).astype(jnp.bfloat16)
        theta = apply_rows(hidden_three, weight_basis) + coarse_basis_bias
        backcast = upsample(theta[:, :KB], length)
        coarse_fore = upsample(theta[:, KB:], ahead)
        residual_here = (started - backcast) * mask
        sent_resid, sent_fore = (
            lax.all_to_all(
                residual_here.astype(jnp.bfloat16),
                "narrow",
                split_axis=1,
                concat_axis=0,
                tiled=True,
            ),
            lax.all_to_all(
                coarse_fore.astype(jnp.bfloat16), "narrow", split_axis=1, concat_axis=0, tiled=True
            ),
        )
        pads_here = group_pads[:, lower : lower + sample_group].reshape(-1)
        piece_mask = (steps_piece[None, :] >= pads_here[:, None]).astype(jnp.float32)
        first_partial = project_rows(sent_resid, inner_one)
        lift_one = lax.psum(first_partial, "narrow") + fine_first_bias
        fine_one = jax.nn.silu(lift_one).astype(jnp.bfloat16)
        lift_two = project_rows(fine_one, inner_two) + fine_second_bias
        fine_two = jax.nn.silu(lift_two).astype(jnp.bfloat16)
        lift_three = project_rows(fine_two, inner_three) + fine_third_bias
        fine_three = jax.nn.silu(lift_three).astype(jnp.bfloat16)
        coef_back = apply_rows(fine_three, inner_back) + back_bias
        coef_fore = apply_rows(fine_three, inner_fore) + predict_offset
        residual_parts.append(
            ((sent_resid.astype(jnp.float32) - coef_back) * piece_mask)
            .astype(jnp.bfloat16)
            .reshape(slim_breadth, sample_group, piece)
        )
        predicted_portions.append(
            (sent_fore.astype(jnp.float32) + coef_fore).reshape(
                slim_breadth, sample_group, predicted_portion
            )
        )
        out_grad = (
            resid_grid[:, iteration_index]
            .reshape(slim_breadth * sample_group, piece)
            .astype(jnp.float32)
        )
        predict_cotan = predict_mesh[:, iteration_index].reshape(
            slim_breadth * sample_group, predicted_portion
        )
        back_grad = (-out_grad * piece_mask).astype(jnp.bfloat16)
        coef_partial = project_rows(back_grad, inner_back) + project_rows(predict_cotan, inner_fore)
        three_grad = lax.psum(coef_partial, "narrow")
        lift_three_grad = (three_grad * silu_slope(lift_three)).astype(jnp.bfloat16)
        lift_two_grad = (apply_rows(lift_three_grad, inner_three) * silu_slope(lift_two)).astype(
            jnp.bfloat16
        )
        lift_one_grad = (apply_rows(lift_two_grad, inner_two) * silu_slope(lift_one)).astype(
            jnp.bfloat16
        )
        own_one_grad = own_slice(lift_one_grad, own_start, sample_group)
        own_two_grad = own_slice(lift_two_grad, own_start, sample_group)
        own_three_grad = own_slice(lift_three_grad, own_start, sample_group)
        own_fine_one = own_slice(fine_one, own_start, sample_group)
        own_fine_two = own_slice(fine_two, own_start, sample_group)
        sent_grad = (out_grad * piece_mask + apply_rows(lift_one_grad, inner_one)).astype(
            jnp.bfloat16
        )
        resid_back, fore_back = (
            lax.all_to_all(sent_grad, "narrow", split_axis=0, concat_axis=1, tiled=True),
            lax.all_to_all(predict_cotan, "narrow", split_axis=0, concat_axis=1, tiled=True),
        )
        grad_inner_one = column_outer(lift_one_grad, sent_resid)
        grad_inner_back = column_outer(fine_three, back_grad)
        grad_inner_fore = column_outer(fine_three, predict_cotan)
        grad_inner_two = column_outer(own_two_grad, own_fine_one)
        grad_inner_three = column_outer(own_three_grad, own_fine_two)
        resid_grad = resid_back.astype(jnp.float32)
        back_pull = jax.vjp(lambda coef: upsample(coef, length), theta[:, :KB])[1]
        fore_pull = jax.vjp(lambda coef: upsample(coef, ahead), theta[:, KB:])[1]
        back_coef_grad = back_pull(-resid_grad * mask)[0]
        fore_coef_grad = fore_pull(fore_back.astype(jnp.float32))[0]
        theta_grad = jnp.concatenate([back_coef_grad, fore_coef_grad], axis=1).astype(jnp.bfloat16)
        coarse_three_grad = (
            project_rows(theta_grad, weight_basis) * silu_slope(linear_three)
        ).astype(jnp.bfloat16)
        coarse_two_grad = (
            apply_rows(coarse_three_grad, weight_three) * silu_slope(linear_two)
        ).astype(jnp.bfloat16)
        coarse_one_grad = (apply_rows(coarse_two_grad, weight_two) * silu_slope(linear_one)).astype(
            jnp.bfloat16
        )
        pooled_grad = apply_rows(coarse_one_grad, weight_one)
        start_grad = resid_grad * mask + jnp.repeat(pooled_grad, POOL, axis=1) / POOL
        grad_parts.append((start_grad * mask).astype(jnp.bfloat16))
        grad_weight_one = column_outer(coarse_one_grad, pooled)
        grad_weight_two = column_outer(coarse_two_grad, hidden_one)
        grad_weight_three = column_outer(coarse_three_grad, hidden_two)
        grad_weight_basis = column_outer(hidden_three, theta_grad)
        bias_terms = (
            column_sums(coarse_one_grad),
            column_sums(coarse_two_grad),
            column_sums(coarse_three_grad),
            column_sums(theta_grad),
            column_sums(own_one_grad),
            column_sums(own_two_grad),
            column_sums(own_three_grad),
            lax.dynamic_update_slice_in_dim(
                jnp.zeros((length,), jnp.float32), column_sums(back_grad), time_start, 0
            ),
            lax.dynamic_update_slice_in_dim(
                jnp.zeros((ahead,), jnp.float32), column_sums(predict_cotan), predict_onset, 0
            ),
        )
        bias_totals = tuple((total + term for total, term in zip(bias_totals, bias_terms)))
        scattered = (
            lax.psum_scatter(grad_weight_one, ("wide", "narrow"), scatter_dimension=0, tiled=True),
            lax.psum_scatter(grad_weight_two, ("wide", "narrow"), scatter_dimension=0, tiled=True),
            lax.psum_scatter(
                grad_weight_three, ("wide", "narrow"), scatter_dimension=0, tiled=True
            ),
            lax.psum_scatter(
                grad_weight_basis, ("wide", "narrow"), scatter_dimension=0, tiled=True
            ),
            lax.psum_scatter(grad_inner_two, ("wide", "narrow"), scatter_dimension=0, tiled=True),
            lax.psum_scatter(grad_inner_three, ("wide", "narrow"), scatter_dimension=0, tiled=True),
        )
        spread = (
            lax.psum_scatter(
                grad_inner_one.astype(jnp.bfloat16), "wide", scatter_dimension=0, tiled=True
            ).astype(jnp.float32),
            lax.psum_scatter(
                grad_inner_back.astype(jnp.bfloat16), "wide", scatter_dimension=0, tiled=True
            ).astype(jnp.float32),
            lax.psum_scatter(
                grad_inner_fore.astype(jnp.bfloat16), "wide", scatter_dimension=0, tiled=True
            ).astype(jnp.float32),
        )
        totals = tuple((total + term for total, term in zip(totals, scattered)))
        fine_totals = tuple((total + term for total, term in zip(fine_totals, spread)))
    bias_sums = lax.psum(
        (
            bias_totals[0],
            bias_totals[1],
            bias_totals[2],
            bias_totals[3],
            bias_totals[4],
            bias_totals[5],
            bias_totals[6],
            bias_totals[7],
            bias_totals[8],
        ),
        ("wide", "narrow"),
    )
    leftover_signal = jnp.stack(residual_parts, axis=1).reshape(slim_breadth * onsite_tally, piece)
    predicted_future = jnp.stack(predicted_portions, axis=1).reshape(
        slim_breadth * onsite_tally, predicted_portion
    )
    temporal_input_derivative = jnp.concatenate(grad_parts, axis=0)
    return (
        leftover_signal,
        predicted_future,
        temporal_input_derivative,
        totals[0],
        bias_sums[0],
        totals[1],
        bias_sums[1],
        totals[2],
        bias_sums[2],
        totals[3],
        bias_sums[3],
        fine_totals[0],
        bias_sums[4],
        totals[4],
        bias_sums[5],
        totals[5],
        bias_sums[6],
        fine_totals[1],
        bias_sums[7],
        fine_totals[2],
        bias_sums[8],
    )


def fits(nn, nw, series, padding, first, first_bias, *rest):
    hid, length = first_bias.shape[0], series.shape[1]
    paired = all(k & (k - 1) == 0 for k in (nn, nw)) and nw % 2 == 0
    paired = paired and len(bits(nn)) == 2 and len(bits(nw // 2)) == 2
    return paired and hid % (16 * nn * nw) == 0 and length % (POOL * nn) == 0 and series.shape[0] % LANE == 0


def solution(mesh):
    both, rows = P(("wide", "narrow"), None), P("wide", "narrow")
    in_specs = (both, P("wide"))
    in_specs += (both, P()) * 4 + (rows, P()) + (both, P()) * 2 + (rows, P()) * 2 + (rows, rows)
    out_specs = (rows, rows, both) + (both, P()) * 4 + (rows, P()) + (both, P()) * 2 + (rows, P()) * 2
    nn, nw = mesh.shape["narrow"], mesh.shape["wide"]

    def body(*args):
        if fits(nn, nw, *args):
            return fast(nn, nw, *args)
        return general(*args)

    return jax.shard_map(body, mesh=mesh, in_specs=in_specs, out_specs=out_specs, check_vma=False)
```

```python
import functools
import types

import jax
import jax.numpy as jnp
import numpy as np
from jax import lax
from jax.experimental import pallas as pl
from jax.experimental.pallas import tpu as pltpu
from jax.sharding import PartitionSpec as P

MESH = pl.DeviceIdType.MESH
POOL = 4
KB = 300
PASSES = 1
LANE = 128
F32 = jnp.float32
BF16 = jnp.bfloat16


def up(value, unit):
    return -(-value // unit) * unit


def interp_table(count, length):
    stride = length // count
    table = np.zeros((count, length), np.float32)
    for t in range(length):
        doubled = 2 * t + 1 - stride
        low = doubled // (2 * stride)
        part = doubled - low * 2 * stride
        table[min(max(low, 0), count - 1), t] += 2 * stride - part
        table[min(max(low + 1, 0), count - 1), t] += part
    return table


def window_tables(nn, length, ahead, back_count, fore_count):
    back, fore = interp_table(back_count, length), interp_table(fore_count, ahead)
    piece, part = length // nn, ahead // nn
    spans = []
    for n in range(nn):
        rows_b = np.nonzero(back[:, n * piece : (n + 1) * piece].any(1))[0]
        rows_f = np.nonzero(fore[:, n * part : (n + 1) * part].any(1))[0]
        spans.append((rows_b, rows_f))
    wide_b = max(len(b) for b, _ in spans)
    wide_f = max(len(f) for _, f in spans)
    width = up(wide_b + wide_f, LANE)
    bw, fw = up(back_count, LANE), up(fore_count, LANE)
    pick = np.zeros((nn, width, bw + fw), np.float32)
    mix_b = np.zeros((nn, piece, width), np.float32)
    mix_f = np.zeros((nn, part, width), np.float32)
    all_f = np.zeros((nn, part, fw), np.float32)
    for n, (rows_b, rows_f) in enumerate(spans):
        all_f[n, :, :fore_count] = fore[:, n * part : (n + 1) * part].T
        for slot, row in enumerate(rows_b):
            pick[n, slot, row] = 1
            mix_b[n, :, slot] = back[row, n * piece : (n + 1) * piece]
        for slot, row in enumerate(rows_f):
            pick[n, wide_b + slot, bw + row] = 1
            mix_f[n, :, wide_b + slot] = fore[row, n * part : (n + 1) * part]
    return wide_b + wide_f, tuple(t.astype(BF16) for t in (pick, mix_b, mix_f, all_f))


class Copy:
    def __init__(self, copy, remote):
        self.copy, self.sent, self.received = copy, False, not remote

    def wait_recv(self):
        if not self.received:
            self.copy.wait_recv()
        self.received = True

    def wait_send(self):
        if not self.sent:
            self.copy.wait_send()
        self.sent = True

    def wait(self):
        if not self.sent:
            self.copy.wait()
        self.sent = True


class Net:
    def __init__(self, sizes, sends, recvs):
        self.nn, self.nc = sizes
        self.sends, self.recvs = sends, recvs
        self.copies = []
        self.w, self.n = lax.axis_index("wide"), lax.axis_index("narrow")
        self.chip, self.core = self.w // 2, self.w % 2

    def chips(self, bit):
        return ((self.chip ^ bit) * 2 + self.core, self.n)

    def narrow(self, bit):
        return (self.w, self.n ^ bit)

    def sibling(self):
        return (self.w ^ 1, self.n)

    def hail(self):
        others = [self.narrow(d) for d in range(1, self.nn)] + [self.chips(b) for b in bits(self.nc)]
        others.append(self.sibling())
        for other in others:
            pl.semaphore_signal(pltpu.get_barrier_semaphore(), 1, device_id=other, device_id_type=MESH)
        self.others = len(others)

    def meet(self):
        pl.semaphore_wait(pltpu.get_barrier_semaphore(), self.others)

    def send(self, src, dst, to):
        k = len(self.copies)
        copy = pltpu.make_async_remote_copy(
            src_ref=src,
            dst_ref=dst,
            send_sem=self.sends.at[k],
            recv_sem=self.recvs.at[k],
            device_id=to,
            device_id_type=MESH,
        )
        copy.start()
        self.copies.append(Copy(copy, True))
        return self.copies[-1]

    def drain(self):
        for copy in self.copies:
            copy.wait_recv()
            copy.wait_send()


def bits(count):
    return [1 << k for k in reversed(range(count.bit_length() - 1))]


class Gather:
    def __init__(self, net, to, order, block, own=None):
        self.net, self.to, self.order, self.block = net, to, order, block
        self.coming = {}
        self.push(0, 0, block(0) if own is None else own)

    def push(self, m, first, src):
        for i in range(first, len(self.order)):
            b = self.order[i]
            self.coming[m | b] = (self.net.send(src, self.block(m), self.to(b)), i)

    def pull(self, m):
        copy, i = self.coming[m]
        copy.wait_recv()
        self.push(m, i + 1, self.block(m))

    def masks(self):
        out = [0]
        for b in self.order:
            out += [m | b for m in out]
        return out[1:]


class Scatter:
    def __init__(self, net, to, order, block, land, add):
        self.net, self.to, self.order, self.block, self.land, self.add = net, to, order, block, land, add
        self.masks = list(range(1 << len(order)))
        self.used = 0
        self.step = 0

    def start(self):
        b = self.order[self.step]
        rest = [m for m in self.masks if not m & b]
        self.pending = []
        for m in rest:
            copy = self.net.send(self.block(m | b), self.land(self.used), self.to(b))
            self.pending.append((copy, m, self.used))
            self.used += 1
        self.masks = rest
        self.step += 1

    def finish(self):
        for copy, m, k in self.pending:
            copy.wait_recv()
            self.add(m, k)

    def last(self):
        ((copy, m, k),) = self.pending
        copy.wait_recv()
        return k


def params(cid):
    return pltpu.CompilerParams(
        collective_id=cid, has_side_effects=True, vmem_limit_bytes=62 << 20
    )


def dot_nt(a, b):
    return lax.dot_general(a, b, (((1,), (1,)), ((), ())), preferred_element_type=F32)


def dot_nn(a, b):
    return lax.dot_general(a, b, (((1,), (0,)), ((), ())), preferred_element_type=F32)


def dot_tn(a, b):
    return lax.dot_general(a, b, (((0,), (0,)), ((), ())), preferred_element_type=F32)


def slope(v):
    s = jax.nn.sigmoid(v)
    return s * (1.0 + v * (1.0 - s))


def pad_to(x, width):
    return jnp.pad(x, ((0, 0), (0, width - x.shape[1])))


def spread_basis(x, back_count, bw, fw):
    return jnp.concatenate([pad_to(x[:, :back_count], bw), pad_to(x[:, back_count:], fw)], axis=1)


def row_loop(total, unit, body):
    def step(i, carry):
        body(pl.multiple_of(i * unit, unit), unit)
        return carry

    lax.fori_loop(0, total // unit, step, 0)
    if total % unit:
        body(total - total % unit, total % unit)


def each(count, body):
    def step(i, carry):
        body(i)
        return carry

    lax.fori_loop(0, count, step, 0)


def whole(c, *refs):
    (
        pads_in, b1, b2, b3, b4, b5, b6, b7, fkb, fob, w1, w2, w3, w4, w5, w6, mix_f_in, all_f_in,
        pick_in, mix_in, series, grad, fut_in, ff, fk, fo,
        left_out, pred_out, tid_out, om, of, ok, oo, obias, chunk_hbm, land_s,
        pick, mix_b, ser, chunk, land_g, bg, fut, wmid, wf, wk, wo, part3, land3, f3a, tw, twa,
        pre, act, pooled, pred, gf, gk, go, cm, cf, ck, co, nm, zm, zi, ni, zf, nf, zk, zo,
        temp, temp3, temp4, temp2, grads, sfore, pgb, pool, pads, brow, erow, bcol, ecol, bt, bl,
        p1, p2, p3, p4, p5, p6, q0, q1, q2, q3, q4, q5, q6, q7, q8, q9, mix_f, all_f, sends, recvs, own,
    ) = refs
    nn, nc, rows, piece, part, hid, pw, bw = c.nn, c.nc, c.rows, c.piece, c.part, c.hid, c.pw, c.bw
    net = Net((nn, nc), sends, recvs)
    n, chip, core = net.n, net.chip, net.core
    owned = []
    ds = pl.ds
    send = net.send
    near = bits(nn)
    orders = (near, near[::-1])
    far, back_far = bits(nc), bits(nc)[::-1]
    half_lane = [ds(0, c.half), ds(c.half, c.off[-1] - c.half)]
    half_outer = [ds(0, c.off[4] // 2), ds(c.off[4] // 2, c.off[4] // 2)]
    halves = lambda count: [ds(0, count // 2), ds(count // 2, count // 2)]

    def local(src, dst):
        copy = pltpu.make_async_copy(src, dst, own.at[len(owned)])
        copy.start()
        owned.append(Copy(copy, False))
        return owned[-1]

    def drain():
        for copy in owned:
            copy.wait()
        net.drain()

    def weight(k):
        return wmid[:, :, :, :, c.off[k] : c.off[k + 1]].reshape(hid, c.off[k + 1] - c.off[k])

    def put_weight(k, value):
        width = c.off[k + 1] - c.off[k]
        wmid[:, :, :, :, c.off[k] : c.off[k + 1]] = value.astype(BF16).reshape(nc, 2, nn, c.hs, width)

    def lanes(j):
        return ds(pl.multiple_of(j * rows, LANE), rows)

    def steps(unit, width):
        return lax.broadcasted_iota(jnp.int32, (unit, width), 0)

    def row_mask(j, r, unit):
        return steps(unit, rows) + (j * piece + r) >= pads[:, lanes(n)]

    def settle(k, r, value, out):
        v = value + bcol[r, k : k + 1]
        pre[k, r, :] = v
        act[out, r, :] = (v * jax.nn.sigmoid(v)).astype(BF16)

    tall = 2 * c.hw
    bands = [ds(z * tall, tall) for z in range(nc)]

    def weight_rows(k, z):
        return wmid[z, :, :, :, c.off[k] : c.off[k + 1]].reshape(tall, c.off[k + 1] - c.off[k])

    def weight_columns(k, r):
        return wmid[:, :, :, :, c.off[k] + r.start : c.off[k] + r.start + r.size].reshape(hid, r.size)

    def layer(k, x, out):
        for z, r in enumerate(bands):
            settle(k, r, dot_nn(weight_rows(k, z), x[...]), out)

    def layer_back(k, x, j, out):
        for r in bands:
            grads[out, r, :] = (dot_tn(weight_columns(k, r), x[...]) * slope(pre[j, r, :])).astype(BF16)

    def sums(value):
        return dot_nt(jnp.ones((8, value.shape[1]), BF16), value)[0:1]

    net.hail()
    c_mids = [local(x, y) for x, y in zip((w1, w2, w3, w4, w5, w6), (p1, p2, p3, p4, p5, p6))]
    c_ser = local(series, ser)
    c_bg = local(grad, bg)
    c_fut = local(fut_in, fut)
    c_ff = local(ff, wf.at[n, chip, core])
    c_fk = local(fk, wk.at[chip, core])
    c_fo = local(fo, wo.at[chip, core])
    c_pick = local(pick_in, pick)
    c_mix = local(mix_in, mix_b)
    slot = wmid.at[chip, core, n]
    slot[...] = jnp.zeros_like(slot)
    for copy in c_mids:
        copy.wait()
    for j in range(nn):
        slot[:, j * c.poolw : j * c.poolw + c.pools] = p1[:, j * c.pools : (j + 1) * c.pools]
    for k, w in ((1, p2), (2, p3), (4, p5), (5, p6)):
        slot[:, c.off[k] : c.off[k + 1]] = w[...]
    slot[:, c.off[3] : c.off[3] + c.bcount] = p4[:, : c.bcount]
    slot[:, c.off[3] + bw : c.off[3] + bw + p4.shape[1] - c.bcount] = p4[:, c.bcount :]
    net.meet()
    z_mid = Gather(net, net.chips, far, lambda e: wmid.at[chip ^ e, core, n])

    def gather_mid(e):
        return [
            Gather(net, net.narrow, order, lambda m, h=h: wmid.at[chip ^ e, core, n ^ m, :, h])
            for order, h in zip(orders, half_lane)
        ]

    def pull_first(gathers):
        for g in gathers:
            g.pull(g.masks()[0])

    def pull_rest(gathers):
        for g in gathers:
            for m in g.masks()[1:]:
                g.pull(m)

    n_mid = {0: gather_mid(0)}
    n_ff = [
        Gather(net, net.narrow, order, lambda m, h=h: wf.at[n ^ m, chip, core, h], ff.at[h])
        for order, h in zip(orders, halves(c.hw))
    ]
    cuts = list(range(0, piece, up(piece // 4, LANE))) + [piece]
    cuts = [ds(a, b - a) for a, b in zip(cuts[:-1], cuts[1:])]
    c_ga = local(grad.at[:, lanes(n)], land_g.at[n])
    a_ga, a_sa = [], []

    def exchange_grad(k):
        h = cuts[k]
        for d in range(1, nn):
            a_ga.append(send(grad.at[h, lanes(n ^ d)], land_g.at[n, h], net.narrow(d)))

    def exchange_series(k):
        h = cuts[k]
        for d in range(1, nn):
            a_sa.append(send(chunk_hbm.at[n ^ d, h], land_s.at[h, lanes(n)], net.narrow(d)))

    exchange_grad(3)
    c_small = [
        local(x, y)
        for x, y in zip((pads_in, b1, b2, b3, b4, b5, b6, b7, fkb, fob), (q0, q1, q2, q3, q4, q5, q6, q7, q8, q9))
    ]
    c_tables = [local(mix_f_in.at[n], mix_f), local(all_f_in.at[n], all_f)]
    for copy in c_small:
        copy.wait()
    pads[...] = q0[...].reshape(1, nn * rows)
    brow[...] = jnp.zeros_like(brow)
    for k, b in enumerate((q1, q2, q3, q5, q6, q7)):
        brow[k : k + 1, :] = b[...].reshape(1, hid)
    theta_bias = q4[...].reshape(1, q4.shape[0])
    brow[6:7, : c.bcount] = theta_bias[:, : c.bcount]
    brow[6:7, bw : bw + q4.shape[0] - c.bcount] = theta_bias[:, c.bcount :]
    bcol[...] = jnp.transpose(brow[...])
    z_mid.pull(z_mid.masks()[0])
    n_mid[z_mid.masks()[0]] = gather_mid(z_mid.masks()[0])
    z_k = [
        Gather(net, net.chips, far, lambda e: wk.at[chip ^ e, core], fk),
        Gather(net, net.chips, far, lambda e: wo.at[chip ^ e, core], fo),
    ]
    pull_first(n_mid[0])
    for m in z_mid.masks()[1:]:
        z_mid.pull(m)
        n_mid[m] = gather_mid(m)
    pull_first(n_ff)
    erow[...] = jnp.zeros_like(erow)
    for j in range(nn):

        @pl.when(n == j)
        def _(j=j):
            erow[0:1, :piece] = q8[j * piece : (j + 1) * piece].reshape(1, piece)
            erow[0:1, pw : pw + part] = q9[j * part : (j + 1) * part].reshape(1, part)

    ecol[...] = jnp.transpose(erow[...])
    bt[...] = jnp.zeros_like(bt)
    twa[...] = jnp.zeros_like(twa)
    first_step = lax.broadcasted_iota(jnp.int32, (c.poolw, piece), 0) * POOL
    behind = lax.broadcasted_iota(jnp.int32, (c.poolw, piece), 1) - first_step
    pool[...] = jnp.where((behind >= 0) & (behind < POOL), 1.0 / POOL, 0.0).astype(BF16)
    pull_first(z_k)
    others = [m for m in n_mid if m]
    pull_first([g for m in others[:-1] for g in n_mid[m]])
    pull_rest(n_ff)
    c_ff.wait()
    z_f = Gather(net, net.chips, far, lambda e: wf.at[:, chip ^ e, core])
    a_cf = []

    def hand_over(e):
        block = wf.at[:, chip ^ e, core]
        a_cf.append(send(block, block, net.sibling()))

    hand_over(0)
    c_ser.wait()

    def cut_piece(j):
        for r in range(0, piece, 64):
            unit = min(64, piece - r)
            x = ser[j * piece + r : j * piece + r + unit, :]
            chunk[j, r : r + unit, :] = jnp.where(row_mask(j, r, unit), x.astype(F32), 0).astype(BF16)

    for j in range(nn // 2):
        cut_piece(j)
    pull_first(n_mid[others[-1]])
    exchange_grad(0)
    for j in range(nn // 2, nn):
        cut_piece(j)
    c_chunk = [local(chunk, chunk_hbm), local(chunk.at[n], land_s.at[:, lanes(n)])]
    for j in range(nn):
        pooled[j * c.poolw : (j + 1) * c.poolw, :] = dot_nn(pool[...], chunk[j]).astype(BF16)
    pull_rest(z_k)
    c_fk.wait()
    c_fo.wait()
    a_ck = [send(wk.at[:, core], wk.at[:, core], net.sibling()), send(wo.at[:, core], wo.at[:, core], net.sibling())]
    c_bg.wait()
    c_fut.wait()

    def negate(r, unit):
        at = ds(r, unit)
        mask = steps(unit, nn * rows) + (n * piece + r) >= pads[...]
        bg[at, :] = jnp.where(mask, -bg[at, :].astype(F32), 0).astype(BF16)

    row_loop(piece, 16, negate)
    a_cm = []
    for e in n_mid:
        pull_rest(n_mid[e])
        block = wmid.at[chip ^ e, core]
        a_cm.append(send(block, block, net.sibling()))
    for copy in c_tables:
        copy.wait()
    for copy in a_ck:
        copy.wait_recv()

    def partial(j):
        back = wk[...].reshape(hid, piece)
        fore = wo[...].reshape(hid, part)
        part3[j, :hid, :] = (dot_nn(back, bg[:, lanes(j)]) + dot_nn(fore, fut[:, lanes(j)])).astype(BF16)
        ahead = dot_tn(all_f[...], fut[:, lanes(j)]) * c.scale_f
        part3[j, hid:, :] = ahead[: c.fcount].astype(BF16)

    each(nn, partial)

    def add_part(m, k, h):
        part3[n ^ m, h, :] = (part3[n ^ m, h, :].astype(F32) + land3[k, h, :].astype(F32)).astype(BF16)

    s_part = [
        Scatter(
            net, net.narrow, order,
            lambda m, h=h: part3.at[n ^ m, h],
            lambda k, h=h: land3.at[k, h],
            lambda m, k, h=h: add_part(m, k, h),
        )
        for order, h in zip(orders, halves(hid + c.fcount))
    ]
    for s in s_part:
        s.start()
    exchange_grad(1)
    for copy in a_cm:
        copy.wait_recv()
    layer(0, pooled, 0)
    z_f.pull(z_f.masks()[0])
    hand_over(z_f.masks()[0])
    layer(1, act.at[0], 1)
    layer(2, act.at[1], 2)
    theta = act.at[6]
    for r in bands:
        theta[r, :] = (dot_tn(weight_columns(3, r), act[2]) + bcol[r, 6:7]).astype(BF16)
    for s in s_part:
        s.finish()
        if s.step < len(near):
            s.start()
    exchange_grad(2)
    for copy in c_chunk:
        copy.wait()
    c_pick.wait()
    c_mix.wait()

    def residual(j):
        tw[j] = dot_nn(pick[j], theta[...]).astype(BF16)
        temp[:piece, :] = dot_nn(mix_b[j], tw[j])

        def body(r, unit):
            at = ds(r, unit)
            x = chunk[j, at, :].astype(F32) - temp[at, :] * c.scale
            chunk[j, at, :] = jnp.where(row_mask(j, r, unit), x, 0).astype(BF16)

        row_loop(piece, 144, body)

    each(nn, residual)
    used = ds(0, c.used)
    twa[used, lanes(n)] = tw[n, : c.used, :]
    for m in z_f.masks()[1:]:
        z_f.pull(m)
        hand_over(m)
    early = len(net.copies)
    for copy in a_cf:
        copy.wait_recv()
    for z, r in enumerate(bands):
        total = dot_nn(wf[0, z].reshape(tall, piece), chunk[0])
        for j in range(1, nn):
            total += dot_nn(wf[j, z].reshape(tall, piece), chunk[j])
        settle(3, r, total, 3)
    layer(4, act.at[3], 4)
    layer(5, act.at[4], 5)
    f3a[:, lanes(n)] = act[5]
    n_f3 = [
        Gather(net, net.narrow, order, lambda m, h=h: f3a.at[h, lanes(n ^ m)], act.at[5, h])
        for order, h in zip(orders, halves(hid))
    ]
    a_tw = [send(tw.at[n ^ d, used], twa.at[used, lanes(n)], net.narrow(d)) for d in range(1, nn)]
    while s_part[0].step < len(near):
        for s in s_part:
            s.finish()
            s.start()
    k3 = [s.last() for s in s_part]

    def collect(h, k):
        def body(r, unit):
            at = ds(h.start + r, unit)
            total = part3[n, at, :].astype(F32) + land3[k, at, :].astype(F32)
            grads[0, at, :] = (total * slope(pre[5, at, :])).astype(BF16)

        return body

    cut = (hid + c.fcount) // 2
    row_loop(cut, 96, collect(ds(0, cut), k3[0]))
    row_loop(hid - cut, 96, collect(ds(cut, hid - cut), k3[1]))
    sfore[...] = (part3[n, hid:, :].astype(F32) + land3[k3[1], hid:, :].astype(F32)).astype(BF16)
    layer_back(5, grads.at[0], 4, 1)
    layer_back(4, grads.at[1], 3, 2)
    r_cf = []
    for j in range(nn):
        gf[j] = dot_nt(grads[2], chunk[j]).astype(BF16).reshape(nc, 2, c.hw, piece)
        r_cf.append(send(gf.at[j, :, 1 - core], cf.at[j], net.sibling()))
    for copy in net.copies[:early]:
        copy.wait_send()
    put_weight(5, dot_nt(grads[0], act[4]))
    put_weight(4, dot_nt(grads[1], act[3]))
    inner, outer = ds(c.off[4], c.off[-1] - c.off[4]), ds(0, c.off[4])
    r_ci = send(wmid.at[:, 1 - core, :, :, inner], cm.at[:, :, :, inner], net.sibling())

    def add_f(j):
        for z in range(nc):
            cf[j, z] = (gf[j, z, core].astype(F32) + cf[j, z].astype(F32)).astype(BF16)

    for j in range(nn):
        r_cf[j].wait_recv()
    each(nn, add_f)

    def add_zf(e, k):
        def body(j):
            cf[j, chip ^ e] = (cf[j, chip ^ e].astype(F32) + zf[k, j].astype(F32)).astype(BF16)

        each(nn, body)

    r_zf = Scatter(net, net.chips, back_far, lambda e: cf.at[:, chip ^ e], lambda k: zf.at[k], add_zf)
    r_zf.start()
    pull_first(n_f3)
    exchange_series(0)
    r_ci.wait_recv()
    for z in range(nc):
        both = wmid[z, core, :, :, inner].astype(F32) + cm[z, :, :, inner].astype(F32)
        cm[z, :, :, inner] = both.astype(BF16)

    def add_zi(e, k):
        both = cm[chip ^ e, :, :, inner].astype(F32) + zi[k].astype(F32)
        cm[chip ^ e, :, :, inner] = both.astype(BF16)

    def add_ni(m, k):
        both = cm[chip, n ^ m, :, inner].astype(F32) + ni[k].astype(F32)
        cm[chip, n ^ m, :, inner] = both.astype(BF16)

    r_zi = Scatter(net, net.chips, back_far, lambda e: cm.at[chip ^ e, :, :, inner], lambda k: zi.at[k], add_zi)
    r_zi.start()
    c_ga.wait()
    for copy in a_ga:
        copy.wait_recv()
    temp2[...] = jnp.zeros_like(temp2)

    def resid_grad(j):
        temp[:piece, :] = dot_tn(wf[j].reshape(hid, piece), grads[2])

        def body(r, unit):
            at = ds(r, unit)
            x = land_g[j, at, :].astype(F32) + temp[at, :]
            land_g[j, at, :] = jnp.where(row_mask(j, r, unit), x, 0).astype(BF16)

        row_loop(piece, 144, body)
        pull = (dot_tn(mix_b[j], land_g[j]) * -c.scale).astype(BF16)
        temp2[...] += dot_tn(pick[j, :, :bw], pull)

    each(nn, resid_grad)
    dth = grads.at[3]
    dth[:bw, :] = temp2[...].astype(BF16)
    dth[bw:, :] = jnp.zeros_like(dth[bw:, :])
    dth[bw : bw + c.fcount, :] = sfore[...]
    for z, r in enumerate(bands):
        grads[4, r, :] = (dot_nn(weight_rows(3, z), dth[...]) * slope(pre[2, r, :])).astype(BF16)
    layer_back(2, grads.at[4], 1, 5)
    layer_back(1, grads.at[5], 0, 6)
    pgb[...] = dot_tn(weight(0), grads[6]).astype(BF16)
    put_weight(3, dot_nt(act[2], dth[...]))
    put_weight(2, dot_nt(grads[4], act[1]))
    put_weight(1, dot_nt(grads[5], act[0]))
    put_weight(0, dot_nt(grads[6], pooled[...]))
    r_cm = send(wmid.at[:, 1 - core, :, :, outer], cm.at[:, :, :, outer], net.sibling())
    bt[0, ds(4 + n, 1), :piece] = sums(bg[...])
    bt[0, ds(4 + n, 1), pw : pw + part] = sums(fut[...])
    for k, slot_k in enumerate((6, 5, 4, 3, 2, 1, 0)):
        bt[0, k // 2 : k // 2 + 1, (k % 2) * hid : (k % 2 + 1) * hid] = sums(grads[slot_k])
    travel = [net.sibling()] + [net.narrow(b) for b in near] + [net.chips(b) for b in back_far]
    v_copies = []

    def send_bias():
        k = len(v_copies)
        v_copies.append(send(bt.at[k], bl.at[k], travel[k]))

    def add_bias():
        k = len(v_copies) - 1
        v_copies[k].wait_recv()
        bt[k + 1] = bt[k] + bl[k]

    send_bias()
    r_cm.wait_recv()
    for z in range(nc):
        both = wmid[z, core, :, :, outer].astype(F32) + cm[z, :, :, outer].astype(F32)
        cm[z, :, :, outer] = both.astype(BF16)

    def add_nm(m, k, h):
        cm[:, n ^ m, :, h] = (cm[:, n ^ m, :, h].astype(F32) + nm[k, :, :, h].astype(F32)).astype(BF16)

    r_nm = [
        Scatter(
            net, net.narrow, order,
            lambda m, h=h: cm.at[:, n ^ m, :, h],
            lambda k, h=h: nm.at[k, :, :, h],
            lambda m, k, h=h: add_nm(m, k, h),
        )
        for order, h in zip(orders, half_outer)
    ]
    for s in r_nm:
        s.start()
    exchange_series(1)
    add_bias()
    send_bias()
    pull_rest(n_f3)
    gk[...] = dot_nt(f3a[...], bg[...]).astype(BF16).reshape(nc, 2, c.hw, piece)
    go[...] = dot_nt(f3a[...], fut[...]).astype(BF16).reshape(nc, 2, c.hw, part)
    r_ck = [send(gk.at[:, 1 - core], ck, net.sibling()), send(go.at[:, 1 - core], co, net.sibling())]
    r_zf.finish()
    r_zf.start()
    r_zi.finish()
    r_zi.start()
    for copy in r_ck:
        copy.wait_recv()
    for z in range(nc):
        ck[z] = (gk[z, core].astype(F32) + ck[z].astype(F32)).astype(BF16)
        co[z] = (go[z, core].astype(F32) + co[z].astype(F32)).astype(BF16)

    def add_k(e, k):
        ck[chip ^ e] = (ck[chip ^ e].astype(F32) + zk[k].astype(F32)).astype(BF16)

    def add_o(e, k):
        co[chip ^ e] = (co[chip ^ e].astype(F32) + zo[k].astype(F32)).astype(BF16)

    r_zk = [
        Scatter(net, net.chips, back_far, lambda e: ck.at[chip ^ e], lambda k: zk.at[k], add_k),
        Scatter(net, net.chips, back_far, lambda e: co.at[chip ^ e], lambda k: zo.at[k], add_o),
    ]

    def series_grad(j):
        temp[:piece, :] = dot_tn(pool[...], pgb[j * c.poolw : (j + 1) * c.poolw, :])
        for r in range(0, piece, 64):
            unit = min(64, piece - r)
            x = land_g[j, r : r + unit, :].astype(F32) + temp[r : r + unit, :]
            x = jnp.where(row_mask(j, r, unit), x, 0).astype(BF16)
            ser[j * piece + r : j * piece + r + unit, :] = x

    def outputs(k):
        h = cuts[k]
        for copy in a_sa[k * (nn - 1) : (k + 1) * (nn - 1)]:
            copy.wait_recv()
        local(land_s.at[h], bg.at[h]).wait()
        stop = h.start + h.size
        marks = [r for r in range(h.start, stop, LANE) if stop - r >= LANE // 2] + [stop]
        for low, high in zip(marks[:-1], marks[1:]):
            temp3[: high - low, :] = dot_nn(mix_b[n, low:high, :], twa[...])
            temp4[: high - low, :] = dot_tn(wk[:, :, :, low:high].reshape(hid, high - low), f3a[...])

            def body(r, unit, low=low):
                at, here = ds(low + r, unit), ds(r, unit)
                x = (bg[at, :].astype(F32) - temp3[here, :] * c.scale).astype(BF16).astype(F32)
                x = x - (temp4[here, :] + ecol[at, 0:1])
                mask = steps(unit, nn * rows) + (n * piece + low + r) >= pads[...]
                bg[at, :] = jnp.where(mask, x, 0).astype(BF16)

            row_loop(high - low, 32, body)
        local(bg.at[h], left_out.at[h])

    def forecast():
        fore = dot_nn(mix_f[...], twa[...]) * c.scale_f
        pred[...] = fore + dot_tn(wo[...].reshape(hid, part), f3a[...]) + ecol[pw : pw + part, 0:1]

    def add_nf(m, k, h):
        cf[n ^ m, chip, h, :] = (cf[n ^ m, chip, h, :].astype(F32) + nf[k, h, :].astype(F32)).astype(BF16)

    def add_zm(e, k):
        both = cm[chip ^ e, n, :, outer].astype(F32) + zm[k].astype(F32)
        cm[chip ^ e, n, :, outer] = both.astype(BF16)

    r_zm = Scatter(net, net.chips, back_far, lambda e: cm.at[chip ^ e, n, :, outer], lambda k: zm.at[k], add_zm)
    r_nf = [
        Scatter(
            net, net.narrow, order,
            lambda m, h=h: cf.at[n ^ m, chip, h],
            lambda k, h=h: nf.at[k, h],
            lambda m, k, h=h: add_nf(m, k, h),
        )
        for order, h in zip(orders, halves(c.hw))
    ]
    for s in r_zk:
        s.start()
    for s in r_nm:
        s.finish()
        s.start()
    add_bias()
    send_bias()
    exchange_series(2)
    r_zi.finish()
    r_ni = Scatter(net, net.narrow, near, lambda m: cm.at[chip, n ^ m, :, inner], lambda k: ni.at[k], add_ni)
    r_ni.start()
    for j in range(nn // 2):
        series_grad(j)
    r_zf.finish()
    for s in r_nf:
        s.start()
    for s in r_nm:
        s.finish()
    r_zm.start()
    add_bias()
    send_bias()
    exchange_series(3)
    for j in range(nn // 2, nn):
        series_grad(j)
    c_tid = local(ser, tid_out)
    for copy in a_tw:
        copy.wait_recv()
    forecast()
    c_pred = local(pred, pred_out)
    for s in r_zk:
        s.finish()
        s.start()
    outputs(0)
    for s in r_nf:
        s.finish()
        s.start()
    r_ni.finish()
    r_ni.start()
    outputs(1)
    r_zm.finish()
    r_zm.start()
    add_bias()
    send_bias()
    outputs(2)
    outputs(3)
    for s in r_zk:
        s.finish()
    ok[...] = ck[chip].astype(F32)
    oo[...] = co[chip].astype(F32)
    r_ni.finish()
    for s in r_nf:
        s.finish()
    of[...] = cf[n, chip].astype(F32)
    add_bias()
    obias[...] = bt[len(travel)]
    r_zm.finish()
    om[...] = cm[chip, n].astype(F32)
    drain()


def finish(c, *refs):
    large_in, small_in, large_out, small_out = refs[:3], refs[3:8], refs[8:11], refs[11:29]
    held, (om, of, ok, oo, obias), given, sems = refs[29:32], refs[32:37], refs[37:55], refs[55]
    g1, v1, g2, v2, g3, v3, g4, v4, gf, vf1, g5, vf2, g6, vf3, gk, vk, go, vo = given
    arriving = [
        pltpu.make_async_copy(src, dst, sems.at[24 + k])
        for k, (src, dst) in enumerate(zip(small_in, (om, of, ok, oo, obias)))
    ]
    leaving = [
        pltpu.make_async_copy(src, dst, sems.at[29 + k]) for k, (src, dst) in enumerate(zip(given, small_out))
    ]
    for copy in arriving:
        copy.start()
    pieces = []
    for a, (src, via, dst) in enumerate(zip(large_in, held, large_out)):
        size = up(-(-src.shape[0] // 4), 16)
        for b, r in enumerate(range(0, src.shape[0], size)):
            h = pl.ds(r, min(size, src.shape[0] - r))
            k = 8 * a + 2 * b
            pieces.append(
                (
                    pltpu.make_async_copy(src.at[h], via.at[h], sems.at[k]),
                    pltpu.make_async_copy(via.at[h], dst.at[h], sems.at[k + 1]),
                )
            )
    for inward, outward in pieces:
        inward.start()
    for copy in arriving:
        copy.wait()
    nn, piece, part, hid, bw = c.nn, c.piece, c.part, c.hid, c.bw
    for j in range(nn):
        g1[:, j * c.pools : (j + 1) * c.pools] = om[:, j * c.poolw : j * c.poolw + c.pools]
    for k, g in ((1, g2), (2, g3), (4, g5), (5, g6)):
        g[...] = om[:, c.off[k] : c.off[k + 1]]
    fore = g4.shape[1] - c.bcount
    g4[:, : c.bcount] = om[:, c.off[3] : c.off[3] + c.bcount]
    g4[:, c.bcount :] = om[:, c.off[3] + bw : c.off[3] + bw + fore]
    gf[...] = of[...]
    gk[...] = ok[...]
    go[...] = oo[...]
    for k, v in enumerate((v1, v2, v3, None, vf1, vf2, vf3)):
        if v is not None:
            v[...] = obias[k // 2 : k // 2 + 1, (k % 2) * hid : (k % 2 + 1) * hid].reshape(hid)
    theta = obias[1:2, hid : 2 * hid]
    v4[...] = jnp.concatenate([theta[:, : c.bcount], theta[:, bw : bw + fore]], axis=1).reshape(v4.shape[0])
    vk[...] = jnp.concatenate([obias[4 + j : 5 + j, :piece] for j in range(nn)], axis=1).reshape(vk.shape[0])
    vo[...] = jnp.concatenate([obias[4 + j : 5 + j, c.pw : c.pw + part] for j in range(nn)], axis=1).reshape(vo.shape[0])
    for copy in leaving:
        copy.start()
    for inward, outward in pieces:
        inward.wait()
        outward.start()
    for inward, outward in pieces:
        outward.wait()
    for copy in leaving:
        copy.wait()


def fast(nn, nw, series, padding, *rest):
    (cf, cfb, cs, csb, ct, ctb, cb, cbb, ff, ffb, fs, fsb, ft, ftb, fk, fkb, fo, fob, grad, fut) = rest
    nc = nw // 2
    rows, length = series.shape
    piece, part = grad.shape[1], fut.shape[1]
    ahead = part * nn
    hid = cfb.shape[0]
    hs, hw = hid // (nn * nw), hid // nw
    back_count, fore_count = KB, cbb.shape[0] - KB
    bw, fw = up(back_count, LANE), up(fore_count, LANE)
    used, (pick, mix_b, mix_f, all_f) = window_tables(nn, length, ahead, back_count, fore_count)
    width = pick.shape[1]
    fcount = up(fore_count, 16)
    pools = piece // POOL
    poolw = up(pools, LANE)
    widths = (nn * poolw, hid, hid, bw + fw, hid, hid)
    off = np.concatenate([[0], np.cumsum(widths)]).tolist()
    mw = off[-1]
    pw = up(piece, LANE)
    assert bw + fw == hid
    c = types.SimpleNamespace(
        nn=nn, nc=nc, rows=rows, piece=piece, part=part, hid=hid, hs=hs, hw=hw, pw=pw, bw=bw,
        off=off, poolw=poolw, pools=pools, used=up(used, 16), fcount=fcount,
        bcount=back_count, half=up(mw // 2, LANE),
        scale=1.0 / (2 * (length // back_count)),
        scale_f=1.0 / (2 * (ahead // fore_count)),
    )
    anyspec = pl.BlockSpec(memory_space=pl.ANY)
    vspec = pl.BlockSpec(memory_space=pltpu.VMEM)
    S, V = jax.ShapeDtypeStruct, pltpu.VMEM
    bs = (up(4 + nn, 8), max(2 * hid, pw + up(part, LANE)))
    stages = 1 + len(bits(nn)) + len(bits(nc))
    gathers = (nc - 1) + 2 * nc * (nn - 1) + 2 * (nn - 1) + 3 * (nc - 1) + 2 + 2 * nc
    ncopies = gathers + 12 * (nn + nc) + 2 * nn * nc
    qw = up(part, LANE)
    scratch = [
        V((nn, width, bw + fw), BF16),
        V((nn, piece, width), BF16),
        V((length, rows), BF16),
        V((nn, piece, rows), BF16),
        V((nn, piece, rows), BF16),
        V((piece, nn * rows), BF16),
        V((part, nn * rows), BF16),
        V((nc, 2, nn, hs, mw), BF16),
        V((nn, nc, 2, hw, piece), BF16),
        V((nc, 2, hw, piece), BF16),
        V((nc, 2, hw, part), BF16),
        V((nn, hid + fcount, rows), BF16),
        V((nn - 1, hid + fcount, rows), BF16),
        V((hid, nn * rows), BF16),
        V((nn, width, rows), BF16),
        V((width, nn * rows), BF16),
        V((6, hid, rows), F32),
        V((7, hid, rows), BF16),
        V((nn * poolw, rows), BF16),
        V((part, nn * rows), F32),
        V((nn, nc, 2, hw, piece), BF16),
        V((nc, 2, hw, piece), BF16),
        V((nc, 2, hw, part), BF16),
        V((nc, nn, hs, mw), BF16),
        V((nn, nc, hw, piece), BF16),
        V((nc, hw, piece), BF16),
        V((nc, hw, part), BF16),
        V((nn - 1, nc, hs, off[4]), BF16),
        V((nc - 1, hs, off[4]), BF16),
        V((nc - 1, nn, hs, mw - off[4]), BF16),
        V((nn - 1, hs, mw - off[4]), BF16),
        V((nc - 1, nn, hw, piece), BF16),
        V((nn - 1, hw, piece), BF16),
        V((nc - 1, hw, piece), BF16),
        V((nc - 1, hw, part), BF16),
        V((piece, rows), F32),
        V((LANE + up(piece % LANE, 16), nn * rows), F32),
        V((LANE + up(piece % LANE, 16), nn * rows), F32),
        V((bw, rows), F32),
        V((7, hid, rows), BF16),
        V((fcount, rows), BF16),
        V((nn * poolw, rows), BF16),
        V((poolw, piece), BF16),
        V((1, nn * rows), jnp.int32),
        V((8, hid), F32),
        V((8, pw + qw), F32),
        V((hid, 8), F32),
        V((pw + qw, 8), F32),
        V((stages + 1,) + bs, F32),
        V((stages,) + bs, F32),
    ]
    scratch += [V(w.shape, BF16) for w in (cf, cs, ct, cb, fs, ft)]
    scratch += [V(b.shape, b.dtype) for b in (padding, cfb, csb, ctb, cbb, ffb, fsb, ftb, fkb, fob)]
    scratch += [
        V(mix_f.shape[1:], BF16),
        V(all_f.shape[1:], BF16),
        pltpu.SemaphoreType.DMA((ncopies,)),
        pltpu.SemaphoreType.DMA((ncopies,)),
        pltpu.SemaphoreType.DMA((40 + 8 * nn,)),
    ]
    leftover, pred, tid, om, of, ok, oo, obias, _, _ = pl.pallas_call(
        functools.partial(whole, c),
        out_shape=(
            S((piece, nn * rows), BF16),
            S((part, nn * rows), F32),
            S((length, rows), BF16),
            S((hs, mw), F32),
            S((hw, piece), F32),
            S((hw, piece), F32),
            S((hw, part), F32),
            S(bs, F32),
            S((nn, piece, rows), BF16),
            S((piece, nn * rows), BF16),
        ),
        in_specs=[anyspec] * 26,
        out_specs=[anyspec] * 3 + [vspec] * 5 + [anyspec] * 2,
        scratch_shapes=scratch,
        compiler_params=params(0),
    )(
        padding, cfb, csb, ctb, cbb, ffb, fsb, ftb, fkb, fob, cf, cs, ct, cb, fs, ft, mix_f, all_f,
        pick, mix_b, series.T, grad.T, fut.T, ff, fk, fo,
    )
    params_like = (cf, cfb, cs, csb, ct, ctb, cb, cbb, ff, ffb, fs, fsb, ft, ftb, fk, fkb, fo, fob)
    outs = pl.pallas_call(
        functools.partial(finish, c),
        out_shape=tuple(S(x.shape, x.dtype) for x in (leftover, pred, tid))
        + tuple(S(p.shape, F32) for p in params_like),
        in_specs=[anyspec] * 8,
        out_specs=[anyspec] * 21,
        scratch_shapes=[V(x.shape, x.dtype) for x in (leftover, pred, tid, om, of, ok, oo, obias)]
        + [V(p.shape, F32) for p in params_like]
        + [pltpu.SemaphoreType.DMA((48,))],
        compiler_params=pltpu.CompilerParams(vmem_limit_bytes=60 << 20),
    )(leftover, pred, tid, om, of, ok, oo, obias)
    return (outs[0].T, outs[1].T, outs[2].T) + tuple(outs[3:])


def upsample(coef, length):
    coef_count = coef.shape[1]
    stride = length // coef_count
    halfway = stride // 2
    padded = jnp.concatenate([coef[:, :1], coef, coef[:, -1:]], axis=1)
    preceding = jnp.repeat(padded[:, :coef_count], stride, axis=1)
    central = jnp.repeat(padded[:, 1 : coef_count + 1], stride, axis=1)
    following = jnp.repeat(padded[:, 2:], stride, axis=1)
    offsets = jnp.arange(length, dtype=jnp.int32) % stride
    in_front = offsets < halfway
    fraction = (
        jnp.where(in_front, offsets + halfway, offsets - halfway).astype(jnp.float32) + 0.5
    ) / stride
    lower_val = jnp.where(in_front[None, :], preceding, central)
    upper_val = jnp.where(in_front[None, :], central, following)
    return lower_val * (1.0 - fraction) + upper_val * fraction


def silu_slope(value):
    sigma = jax.nn.sigmoid(value)
    return sigma * (1.0 + value * (1.0 - sigma))


def project_rows(rows_in, matrix):
    return lax.dot_general(
        rows_in, matrix, (((1,), (1,)), ((), ())), preferred_element_type=jnp.float32
    )


def apply_rows(rows_in, matrix):
    return jnp.dot(rows_in, matrix, preferred_element_type=jnp.float32)


def column_outer(first_rows, second_rows):
    return lax.dot_general(
        first_rows, second_rows, (((0,), (0,)), ((), ())), preferred_element_type=jnp.float32
    )


def own_slice(values, begin, amount):
    return lax.dynamic_slice_in_dim(values, begin, amount, 0)


def column_sums(values):
    return jnp.sum(values.astype(jnp.float32), axis=0)


def general(
    series,
    padding,
    coarse_first,
    coarse_first_bias,
    coarse_second,
    coarse_second_bias,
    coarse_third,
    coarse_third_bias,
    coarse_basis,
    coarse_basis_bias,
    fine_first,
    fine_first_bias,
    fine_second,
    fine_second_bias,
    fine_third,
    fine_third_bias,
    fine_back,
    fine_back_bias,
    fine_fore,
    detailed_predict_offset,
    grad_resid,
    future_cotangent_array,
):
    slim_breadth = lax.axis_size("narrow")
    slim_position = lax.axis_index("narrow")
    onsite_tally, length = series.shape
    ahead = future_cotangent_array.shape[1] * slim_breadth
    sample_group = onsite_tally // PASSES
    piece = length // slim_breadth
    predicted_portion = ahead // slim_breadth
    group_pads = padding.reshape(slim_breadth, onsite_tally)
    own_pads = lax.dynamic_slice_in_dim(group_pads, slim_position, 1, 0)[0]
    steps_all = jnp.arange(length, dtype=jnp.int32)
    time_start = slim_position * piece
    predict_onset = slim_position * predicted_portion
    steps_piece = time_start + jnp.arange(piece, dtype=jnp.int32)
    back_bias = lax.dynamic_slice_in_dim(fine_back_bias, time_start, piece, 0)
    predict_offset = lax.dynamic_slice_in_dim(
        detailed_predict_offset, predict_onset, predicted_portion, 0
    )
    resid_grid = grad_resid.reshape(slim_breadth, PASSES, sample_group, piece)
    predict_mesh = future_cotangent_array.reshape(
        slim_breadth, PASSES, sample_group, predicted_portion
    )
    own_start = slim_position * sample_group
    coarse_local = (
        coarse_first,
        coarse_second,
        coarse_third,
        coarse_basis,
        fine_second,
        fine_third,
    )
    fine_local = (fine_first, fine_back, fine_fore)
    totals = tuple((jnp.zeros(w.shape, jnp.float32) for w in coarse_local))
    fine_totals = tuple((jnp.zeros(w.shape, jnp.float32) for w in fine_local))
    bias_totals = tuple(
        (
            jnp.zeros(b.shape, jnp.float32)
            for b in (
                coarse_first_bias,
                coarse_second_bias,
                coarse_third_bias,
                coarse_basis_bias,
                fine_first_bias,
                fine_second_bias,
                fine_third_bias,
                fine_back_bias,
                detailed_predict_offset,
            )
        )
    )
    residual_parts = []
    predicted_portions = []
    grad_parts = []
    for iteration_index in range(PASSES):
        shared = (
            lax.all_gather(coarse_first, ("wide", "narrow"), axis=0, tiled=True),
            lax.all_gather(coarse_second, ("wide", "narrow"), axis=0, tiled=True),
            lax.all_gather(coarse_third, ("wide", "narrow"), axis=0, tiled=True),
            lax.all_gather(coarse_basis, ("wide", "narrow"), axis=0, tiled=True),
            lax.all_gather(fine_second, ("wide", "narrow"), axis=0, tiled=True),
            lax.all_gather(fine_third, ("wide", "narrow"), axis=0, tiled=True),
        )
        pieces = (
            lax.all_gather(fine_first, "wide", axis=0, tiled=True),
            lax.all_gather(fine_back, "wide", axis=0, tiled=True),
            lax.all_gather(fine_fore, "wide", axis=0, tiled=True),
        )
        weight_one, weight_two, weight_three, weight_basis, inner_two, inner_three = shared
        inner_one, inner_back, inner_fore = pieces
        lower = iteration_index * sample_group
        mask = (steps_all[None, :] >= own_pads[lower : lower + sample_group, None]).astype(
            jnp.float32
        )
        started = series[lower : lower + sample_group].astype(jnp.float32) * mask
        pooled = jnp.mean(started.reshape(sample_group, length // POOL, POOL), axis=2).astype(
            jnp.bfloat16
        )
        linear_one = project_rows(pooled, weight_one) + coarse_first_bias
        hidden_one = jax.nn.silu(linear_one).astype(jnp.bfloat16)
        linear_two = project_rows(hidden_one, weight_two) + coarse_second_bias
        hidden_two = jax.nn.silu(linear_two).astype(jnp.bfloat16)
        linear_three = project_rows(hidden_two, weight_three) + coarse_third_bias
        hidden_three = jax.nn.silu(linear_three).astype(jnp.bfloat16)
        theta = apply_rows(hidden_three, weight_basis) + coarse_basis_bias
        backcast = upsample(theta[:, :KB], length)
        coarse_fore = upsample(theta[:, KB:], ahead)
        residual_here = (started - backcast) * mask
        sent_resid, sent_fore = (
            lax.all_to_all(
                residual_here.astype(jnp.bfloat16),
                "narrow",
                split_axis=1,
                concat_axis=0,
                tiled=True,
            ),
            lax.all_to_all(
                coarse_fore.astype(jnp.bfloat16), "narrow", split_axis=1, concat_axis=0, tiled=True
            ),
        )
        pads_here = group_pads[:, lower : lower + sample_group].reshape(-1)
        piece_mask = (steps_piece[None, :] >= pads_here[:, None]).astype(jnp.float32)
        first_partial = project_rows(sent_resid, inner_one)
        lift_one = lax.psum(first_partial, "narrow") + fine_first_bias
        fine_one = jax.nn.silu(lift_one).astype(jnp.bfloat16)
        lift_two = project_rows(fine_one, inner_two) + fine_second_bias
        fine_two = jax.nn.silu(lift_two).astype(jnp.bfloat16)
        lift_three = project_rows(fine_two, inner_three) + fine_third_bias
        fine_three = jax.nn.silu(lift_three).astype(jnp.bfloat16)
        coef_back = apply_rows(fine_three, inner_back) + back_bias
        coef_fore = apply_rows(fine_three, inner_fore) + predict_offset
        residual_parts.append(
            ((sent_resid.astype(jnp.float32) - coef_back) * piece_mask)
            .astype(jnp.bfloat16)
            .reshape(slim_breadth, sample_group, piece)
        )
        predicted_portions.append(
            (sent_fore.astype(jnp.float32) + coef_fore).reshape(
                slim_breadth, sample_group, predicted_portion
            )
        )
        out_grad = (
            resid_grid[:, iteration_index]
            .reshape(slim_breadth * sample_group, piece)
            .astype(jnp.float32)
        )
        predict_cotan = predict_mesh[:, iteration_index].reshape(
            slim_breadth * sample_group, predicted_portion
        )
        back_grad = (-out_grad * piece_mask).astype(jnp.bfloat16)
        coef_partial = project_rows(back_grad, inner_back) + project_rows(predict_cotan, inner_fore)
        three_grad = lax.psum(coef_partial, "narrow")
        lift_three_grad = (three_grad * silu_slope(lift_three)).astype(jnp.bfloat16)
        lift_two_grad = (apply_rows(lift_three_grad, inner_three) * silu_slope(lift_two)).astype(
            jnp.bfloat16
        )
        lift_one_grad = (apply_rows(lift_two_grad, inner_two) * silu_slope(lift_one)).astype(
            jnp.bfloat16
        )
        own_one_grad = own_slice(lift_one_grad, own_start, sample_group)
        own_two_grad = own_slice(lift_two_grad, own_start, sample_group)
        own_three_grad = own_slice(lift_three_grad, own_start, sample_group)
        own_fine_one = own_slice(fine_one, own_start, sample_group)
        own_fine_two = own_slice(fine_two, own_start, sample_group)
        sent_grad = (out_grad * piece_mask + apply_rows(lift_one_grad, inner_one)).astype(
            jnp.bfloat16
        )
        resid_back, fore_back = (
            lax.all_to_all(sent_grad, "narrow", split_axis=0, concat_axis=1, tiled=True),
            lax.all_to_all(predict_cotan, "narrow", split_axis=0, concat_axis=1, tiled=True),
        )
        grad_inner_one = column_outer(lift_one_grad, sent_resid)
        grad_inner_back = column_outer(fine_three, back_grad)
        grad_inner_fore = column_outer(fine_three, predict_cotan)
        grad_inner_two = column_outer(own_two_grad, own_fine_one)
        grad_inner_three = column_outer(own_three_grad, own_fine_two)
        resid_grad = resid_back.astype(jnp.float32)
        back_pull = jax.vjp(lambda coef: upsample(coef, length), theta[:, :KB])[1]
        fore_pull = jax.vjp(lambda coef: upsample(coef, ahead), theta[:, KB:])[1]
        back_coef_grad = back_pull(-resid_grad * mask)[0]
        fore_coef_grad = fore_pull(fore_back.astype(jnp.float32))[0]
        theta_grad = jnp.concatenate([back_coef_grad, fore_coef_grad], axis=1).astype(jnp.bfloat16)
        coarse_three_grad = (
            project_rows(theta_grad, weight_basis) * silu_slope(linear_three)
        ).astype(jnp.bfloat16)
        coarse_two_grad = (
            apply_rows(coarse_three_grad, weight_three) * silu_slope(linear_two)
        ).astype(jnp.bfloat16)
        coarse_one_grad = (apply_rows(coarse_two_grad, weight_two) * silu_slope(linear_one)).astype(
            jnp.bfloat16
        )
        pooled_grad = apply_rows(coarse_one_grad, weight_one)
        start_grad = resid_grad * mask + jnp.repeat(pooled_grad, POOL, axis=1) / POOL
        grad_parts.append((start_grad * mask).astype(jnp.bfloat16))
        grad_weight_one = column_outer(coarse_one_grad, pooled)
        grad_weight_two = column_outer(coarse_two_grad, hidden_one)
        grad_weight_three = column_outer(coarse_three_grad, hidden_two)
        grad_weight_basis = column_outer(hidden_three, theta_grad)
        bias_terms = (
            column_sums(coarse_one_grad),
            column_sums(coarse_two_grad),
            column_sums(coarse_three_grad),
            column_sums(theta_grad),
            column_sums(own_one_grad),
            column_sums(own_two_grad),
            column_sums(own_three_grad),
            lax.dynamic_update_slice_in_dim(
                jnp.zeros((length,), jnp.float32), column_sums(back_grad), time_start, 0
            ),
            lax.dynamic_update_slice_in_dim(
                jnp.zeros((ahead,), jnp.float32), column_sums(predict_cotan), predict_onset, 0
            ),
        )
        bias_totals = tuple((total + term for total, term in zip(bias_totals, bias_terms)))
        scattered = (
            lax.psum_scatter(grad_weight_one, ("wide", "narrow"), scatter_dimension=0, tiled=True),
            lax.psum_scatter(grad_weight_two, ("wide", "narrow"), scatter_dimension=0, tiled=True),
            lax.psum_scatter(
                grad_weight_three, ("wide", "narrow"), scatter_dimension=0, tiled=True
            ),
            lax.psum_scatter(
                grad_weight_basis, ("wide", "narrow"), scatter_dimension=0, tiled=True
            ),
            lax.psum_scatter(grad_inner_two, ("wide", "narrow"), scatter_dimension=0, tiled=True),
            lax.psum_scatter(grad_inner_three, ("wide", "narrow"), scatter_dimension=0, tiled=True),
        )
        spread = (
            lax.psum_scatter(
                grad_inner_one.astype(jnp.bfloat16), "wide", scatter_dimension=0, tiled=True
            ).astype(jnp.float32),
            lax.psum_scatter(
                grad_inner_back.astype(jnp.bfloat16), "wide", scatter_dimension=0, tiled=True
            ).astype(jnp.float32),
            lax.psum_scatter(
                grad_inner_fore.astype(jnp.bfloat16), "wide", scatter_dimension=0, tiled=True
            ).astype(jnp.float32),
        )
        totals = tuple((total + term for total, term in zip(totals, scattered)))
        fine_totals = tuple((total + term for total, term in zip(fine_totals, spread)))
    bias_sums = lax.psum(
        (
            bias_totals[0],
            bias_totals[1],
            bias_totals[2],
            bias_totals[3],
            bias_totals[4],
            bias_totals[5],
            bias_totals[6],
            bias_totals[7],
            bias_totals[8],
        ),
        ("wide", "narrow"),
    )
    leftover_signal = jnp.stack(residual_parts, axis=1).reshape(slim_breadth * onsite_tally, piece)
    predicted_future = jnp.stack(predicted_portions, axis=1).reshape(
        slim_breadth * onsite_tally, predicted_portion
    )
    temporal_input_derivative = jnp.concatenate(grad_parts, axis=0)
    return (
        leftover_signal,
        predicted_future,
        temporal_input_derivative,
        totals[0],
        bias_sums[0],
        totals[1],
        bias_sums[1],
        totals[2],
        bias_sums[2],
        totals[3],
        bias_sums[3],
        fine_totals[0],
        bias_sums[4],
        totals[4],
        bias_sums[5],
        totals[5],
        bias_sums[6],
        fine_totals[1],
        bias_sums[7],
        fine_totals[2],
        bias_sums[8],
    )


def fits(nn, nw, series, padding, first, first_bias, *rest):
    hid, length = first_bias.shape[0], series.shape[1]
    paired = all(k & (k - 1) == 0 for k in (nn, nw)) and nw % 2 == 0
    paired = paired and len(bits(nn)) == 2 and len(bits(nw // 2)) == 2
    return paired and hid % (16 * nn * nw) == 0 and length % (POOL * nn) == 0 and series.shape[0] % LANE == 0


def solution(mesh):
    both, rows = P(("wide", "narrow"), None), P("wide", "narrow")
    in_specs = (both, P("wide"))
    in_specs += (both, P()) * 4 + (rows, P()) + (both, P()) * 2 + (rows, P()) * 2 + (rows, rows)
    out_specs = (rows, rows, both) + (both, P()) * 4 + (rows, P()) + (both, P()) * 2 + (rows, P()) * 2
    nn, nw = mesh.shape["narrow"], mesh.shape["wide"]

    def body(*args):
        if fits(nn, nw, *args):
            return fast(nn, nw, *args)
        return general(*args)

    return jax.shard_map(body, mesh=mesh, in_specs=in_specs, out_specs=out_specs, check_vma=False)
```

```python
import functools
import types

import jax
import jax.numpy as jnp
import numpy as np
from jax import lax
from jax.experimental import pallas as pl
from jax.experimental.pallas import tpu as pltpu
from jax.sharding import PartitionSpec as P

MESH = pl.DeviceIdType.MESH
POOL = 4
KB = 300
PASSES = 1
LANE = 128
F32 = jnp.float32
BF16 = jnp.bfloat16


def up(value, unit):
    return -(-value // unit) * unit


def interp_table(count, length):
    stride = length // count
    table = np.zeros((count, length), np.float32)
    for t in range(length):
        doubled = 2 * t + 1 - stride
        low = doubled // (2 * stride)
        part = doubled - low * 2 * stride
        table[min(max(low, 0), count - 1), t] += 2 * stride - part
        table[min(max(low + 1, 0), count - 1), t] += part
    return table


def window_tables(nn, length, ahead, back_count, fore_count):
    back, fore = interp_table(back_count, length), interp_table(fore_count, ahead)
    piece, part = length // nn, ahead // nn
    spans = []
    for n in range(nn):
        rows_b = np.nonzero(back[:, n * piece : (n + 1) * piece].any(1))[0]
        rows_f = np.nonzero(fore[:, n * part : (n + 1) * part].any(1))[0]
        spans.append((rows_b, rows_f))
    wide_b = max(len(b) for b, _ in spans)
    wide_f = max(len(f) for _, f in spans)
    width = up(wide_b + wide_f, LANE)
    bw, fw = up(back_count, LANE), up(fore_count, LANE)
    pick = np.zeros((nn, width, bw + fw), np.float32)
    mix_b = np.zeros((nn, piece, width), np.float32)
    mix_f = np.zeros((nn, part, width), np.float32)
    all_f = np.zeros((nn, part, fw), np.float32)
    for n, (rows_b, rows_f) in enumerate(spans):
        all_f[n, :, :fore_count] = fore[:, n * part : (n + 1) * part].T
        for slot, row in enumerate(rows_b):
            pick[n, slot, row] = 1
            mix_b[n, :, slot] = back[row, n * piece : (n + 1) * piece]
        for slot, row in enumerate(rows_f):
            pick[n, wide_b + slot, bw + row] = 1
            mix_f[n, :, wide_b + slot] = fore[row, n * part : (n + 1) * part]
    return wide_b + wide_f, tuple(t.astype(BF16) for t in (pick, mix_b, mix_f, all_f))


class Copy:
    def __init__(self, copy, remote):
        self.copy, self.sent, self.received = copy, False, not remote

    def wait_recv(self):
        if not self.received:
            self.copy.wait_recv()
        self.received = True

    def wait_send(self):
        if not self.sent:
            self.copy.wait_send()
        self.sent = True

    def wait(self):
        if not self.sent:
            self.copy.wait()
        self.sent = True


class Net:
    def __init__(self, sizes, sends, recvs):
        self.nn, self.nc = sizes
        self.sends, self.recvs = sends, recvs
        self.copies = []
        self.w, self.n = lax.axis_index("wide"), lax.axis_index("narrow")
        self.chip, self.core = self.w // 2, self.w % 2

    def chips(self, bit):
        return ((self.chip ^ bit) * 2 + self.core, self.n)

    def narrow(self, bit):
        return (self.w, self.n ^ bit)

    def sibling(self):
        return (self.w ^ 1, self.n)

    def hail(self):
        others = [self.narrow(d) for d in range(1, self.nn)] + [self.chips(b) for b in bits(self.nc)]
        others.append(self.sibling())
        for other in others:
            pl.semaphore_signal(pltpu.get_barrier_semaphore(), 1, device_id=other, device_id_type=MESH)
        self.others = len(others)

    def meet(self):
        pl.semaphore_wait(pltpu.get_barrier_semaphore(), self.others)

    def send(self, src, dst, to):
        k = len(self.copies)
        copy = pltpu.make_async_remote_copy(
            src_ref=src,
            dst_ref=dst,
            send_sem=self.sends.at[k],
            recv_sem=self.recvs.at[k],
            device_id=to,
            device_id_type=MESH,
        )
        copy.start()
        self.copies.append(Copy(copy, True))
        return self.copies[-1]

    def drain(self):
        for copy in self.copies:
            copy.wait_recv()
            copy.wait_send()


def bits(count):
    return [1 << k for k in reversed(range(count.bit_length() - 1))]


class Gather:
    def __init__(self, net, to, order, block, own=None):
        self.net, self.to, self.order, self.block = net, to, order, block
        self.coming = {}
        self.push(0, 0, block(0) if own is None else own)

    def push(self, m, first, src):
        for i in range(first, len(self.order)):
            b = self.order[i]
            self.coming[m | b] = (self.net.send(src, self.block(m), self.to(b)), i)

    def pull(self, m):
        copy, i = self.coming[m]
        copy.wait_recv()
        self.push(m, i + 1, self.block(m))

    def masks(self):
        out = [0]
        for b in self.order:
            out += [m | b for m in out]
        return out[1:]


class Scatter:
    def __init__(self, net, to, order, block, land, add):
        self.net, self.to, self.order, self.block, self.land, self.add = net, to, order, block, land, add
        self.masks = list(range(1 << len(order)))
        self.used = 0
        self.step = 0

    def start(self):
        b = self.order[self.step]
        rest = [m for m in self.masks if not m & b]
        self.pending = []
        for m in rest:
            copy = self.net.send(self.block(m | b), self.land(self.used), self.to(b))
            self.pending.append((copy, m, self.used))
            self.used += 1
        self.masks = rest
        self.step += 1

    def finish(self):
        for copy, m, k in self.pending:
            copy.wait_recv()
            self.add(m, k)

    def last(self):
        ((copy, m, k),) = self.pending
        copy.wait_recv()
        return k


def params(cid):
    return pltpu.CompilerParams(
        collective_id=cid, has_side_effects=True, vmem_limit_bytes=62 << 20
    )


def dot_nt(a, b):
    return lax.dot_general(a, b, (((1,), (1,)), ((), ())), preferred_element_type=F32)


def dot_nn(a, b):
    return lax.dot_general(a, b, (((1,), (0,)), ((), ())), preferred_element_type=F32)


def dot_tn(a, b):
    return lax.dot_general(a, b, (((0,), (0,)), ((), ())), preferred_element_type=F32)


def slope(v):
    s = jax.nn.sigmoid(v)
    return s * (1.0 + v * (1.0 - s))


def pad_to(x, width):
    return jnp.pad(x, ((0, 0), (0, width - x.shape[1])))


def spread_basis(x, back_count, bw, fw):
    return jnp.concatenate([pad_to(x[:, :back_count], bw), pad_to(x[:, back_count:], fw)], axis=1)


def row_loop(total, unit, body):
    def step(i, carry):
        body(pl.multiple_of(i * unit, unit), unit)
        return carry

    lax.fori_loop(0, total // unit, step, 0)
    if total % unit:
        body(total - total % unit, total % unit)


def each(count, body):
    def step(i, carry):
        body(i)
        return carry

    lax.fori_loop(0, count, step, 0)


def whole(c, *refs):
    (
        pads_in, b1, b2, b3, b4, b5, b6, b7, fkb, fob, w1, w2, w3, w4, w5, w6, mix_f_in, all_f_in,
        pick_in, mix_in, series, grad, fut_in, ff, fk, fo,
        left_out, pred_out, tid_out, om, of, ok, oo, obias, chunk_hbm, land_s,
        pick, mix_b, ser, chunk, land_g, bg, fut, wmid, wf, wk, wo, part3, land3, f3a, tw, twa,
        pre, act, pooled, pred, gf, gk, go, cm, cf, ck, co, nm, zm, zi, ni, zf, nf, zk, zo,
        temp, temp3, temp4, temp2, grads, sfore, pgb, pool, pads, brow, erow, bcol, ecol, bt, bl,
        p1, p2, p3, p4, p5, p6, q0, q1, q2, q3, q4, q5, q6, q7, q8, q9, mix_f, all_f, sends, recvs, own,
    ) = refs
    nn, nc, rows, piece, part, hid, pw, bw = c.nn, c.nc, c.rows, c.piece, c.part, c.hid, c.pw, c.bw
    net = Net((nn, nc), sends, recvs)
    n, chip, core = net.n, net.chip, net.core
    owned = []
    ds = pl.ds
    send = net.send
    near = bits(nn)
    orders = (near, near[::-1])
    far, back_far = bits(nc), bits(nc)[::-1]
    half_lane = [ds(0, c.half), ds(c.half, c.off[-1] - c.half)]
    half_outer = [ds(0, c.off[4] // 2), ds(c.off[4] // 2, c.off[4] // 2)]
    halves = lambda count: [ds(0, count // 2), ds(count // 2, count // 2)]

    def local(src, dst):
        copy = pltpu.make_async_copy(src, dst, own.at[len(owned)])
        copy.start()
        owned.append(Copy(copy, False))
        return owned[-1]

    def drain():
        for copy in owned:
            copy.wait()
        net.drain()

    def weight(k):
        return wmid[:, :, :, :, c.off[k] : c.off[k + 1]].reshape(hid, c.off[k + 1] - c.off[k])

    def put_weight(k, value):
        width = c.off[k + 1] - c.off[k]
        wmid[:, :, :, :, c.off[k] : c.off[k + 1]] = value.astype(BF16).reshape(nc, 2, nn, c.hs, width)

    def lanes(j):
        return ds(pl.multiple_of(j * rows, LANE), rows)

    def steps(unit, width):
        return lax.broadcasted_iota(jnp.int32, (unit, width), 0)

    def row_mask(j, r, unit):
        return steps(unit, rows) + (j * piece + r) >= pads[:, lanes(n)]

    def settle(k, r, value, out):
        v = value + bcol[r, k : k + 1]
        pre[k, r, :] = v
        act[out, r, :] = (v * jax.nn.sigmoid(v)).astype(BF16)

    tall = 2 * c.hw
    bands = [ds(z * tall, tall) for z in range(nc)]

    def weight_rows(k, z):
        return wmid[z, :, :, :, c.off[k] : c.off[k + 1]].reshape(tall, c.off[k + 1] - c.off[k])

    def weight_columns(k, r):
        return wmid[:, :, :, :, c.off[k] + r.start : c.off[k] + r.start + r.size].reshape(hid, r.size)

    def layer(k, x, out):
        for z, r in enumerate(bands):
            settle(k, r, dot_nn(weight_rows(k, z), x[...]), out)

    def layer_back(k, x, j, out):
        for r in bands:
            grads[out, r, :] = (dot_tn(weight_columns(k, r), x[...]) * slope(pre[j, r, :])).astype(BF16)

    def sums(value):
        return dot_nt(jnp.ones((8, value.shape[1]), BF16), value)[0:1]

    net.hail()
    c_mids = [local(x, y) for x, y in zip((w1, w2, w3, w4, w5, w6), (p1, p2, p3, p4, p5, p6))]
    c_ff = local(ff, wf.at[n, chip, core])
    c_fk = local(fk, wk.at[chip, core])
    c_fo = local(fo, wo.at[chip, core])
    slot = wmid.at[chip, core, n]
    slot[...] = jnp.zeros_like(slot)
    for copy in c_mids:
        copy.wait()
    for j in range(nn):
        slot[:, j * c.poolw : j * c.poolw + c.pools] = p1[:, j * c.pools : (j + 1) * c.pools]
    for k, w in ((1, p2), (2, p3), (4, p5), (5, p6)):
        slot[:, c.off[k] : c.off[k + 1]] = w[...]
    slot[:, c.off[3] : c.off[3] + c.bcount] = p4[:, : c.bcount]
    slot[:, c.off[3] + bw : c.off[3] + bw + p4.shape[1] - c.bcount] = p4[:, c.bcount :]
    net.meet()
    z_mid = Gather(net, net.chips, far, lambda e: wmid.at[chip ^ e, core, n])

    def gather_mid(e):
        return [
            Gather(net, net.narrow, order, lambda m, h=h: wmid.at[chip ^ e, core, n ^ m, :, h])
            for order, h in zip(orders, half_lane)
        ]

    def pull_first(gathers):
        for g in gathers:
            g.pull(g.masks()[0])

    def pull_rest(gathers):
        for g in gathers:
            for m in g.masks()[1:]:
                g.pull(m)

    n_mid = {0: gather_mid(0)}
    n_ff = [
        Gather(net, net.narrow, order, lambda m, h=h: wf.at[n ^ m, chip, core, h], ff.at[h])
        for order, h in zip(orders, halves(c.hw))
    ]
    c_ser = local(series, ser)
    c_bg = local(grad, bg)
    c_fut = local(fut_in, fut)
    c_pick = local(pick_in, pick)
    c_mix = local(mix_in, mix_b)
    cuts = list(range(0, piece, up(piece // 4, LANE))) + [piece]
    cuts = [ds(a, b - a) for a, b in zip(cuts[:-1], cuts[1:])]
    starts = [0, 2 * LANE, 3 * LANE, 5 * LANE, 6 * LANE, piece]
    parts = [ds(a, b - a) for a, b in zip(starts[:-1], starts[1:])]
    c_ga = local(grad.at[:, lanes(n)], land_g.at[n])
    a_ga, a_sa = [], []

    def exchange_grad(k):
        h = cuts[k]
        for d in range(1, nn):
            a_ga.append(send(grad.at[h, lanes(n ^ d)], land_g.at[n, h], net.narrow(d)))

    def exchange_series(k):
        h = parts[k]
        for d in range(1, nn):
            a_sa.append(send(chunk_hbm.at[n ^ d, h], land_s.at[h, lanes(n)], net.narrow(d)))

    c_small = [
        local(x, y)
        for x, y in zip((pads_in, b1, b2, b3, b4, b5, b6, b7, fkb, fob), (q0, q1, q2, q3, q4, q5, q6, q7, q8, q9))
    ]
    c_tables = [local(mix_f_in.at[n], mix_f), local(all_f_in.at[n], all_f)]
    for copy in c_small:
        copy.wait()
    pads[...] = q0[...].reshape(1, nn * rows)
    brow[...] = jnp.zeros_like(brow)
    for k, b in enumerate((q1, q2, q3, q5, q6, q7)):
        brow[k : k + 1, :] = b[...].reshape(1, hid)
    theta_bias = q4[...].reshape(1, q4.shape[0])
    brow[6:7, : c.bcount] = theta_bias[:, : c.bcount]
    brow[6:7, bw : bw + q4.shape[0] - c.bcount] = theta_bias[:, c.bcount :]
    bcol[...] = jnp.transpose(brow[...])
    exchange_grad(3)
    z_mid.pull(z_mid.masks()[0])
    n_mid[z_mid.masks()[0]] = gather_mid(z_mid.masks()[0])
    z_k = [
        Gather(net, net.chips, far, lambda e: wk.at[chip ^ e, core], fk),
        Gather(net, net.chips, far, lambda e: wo.at[chip ^ e, core], fo),
    ]
    pull_first(n_ff)
    pull_first(n_mid[0])
    for m in z_mid.masks()[1:]:
        z_mid.pull(m)
        n_mid[m] = gather_mid(m)
    erow[...] = jnp.zeros_like(erow)
    for j in range(nn):

        @pl.when(n == j)
        def _(j=j):
            erow[0:1, :piece] = q8[j * piece : (j + 1) * piece].reshape(1, piece)
            erow[0:1, pw : pw + part] = q9[j * part : (j + 1) * part].reshape(1, part)

    ecol[...] = jnp.transpose(erow[...])
    bt[...] = jnp.zeros_like(bt)
    twa[...] = jnp.zeros_like(twa)
    first_step = lax.broadcasted_iota(jnp.int32, (c.poolw, piece), 0) * POOL
    behind = lax.broadcasted_iota(jnp.int32, (c.poolw, piece), 1) - first_step
    pool[...] = jnp.where((behind >= 0) & (behind < POOL), 1.0 / POOL, 0.0).astype(BF16)
    pull_first(z_k)
    others = z_mid.masks()
    for m in others[:-1]:
        pull_first(n_mid[m])
    pull_rest(n_ff)
    c_ff.wait()
    z_f = [Gather(net, net.chips, far, lambda e, j=j: wf.at[j, chip ^ e, core]) for j in range(nn)]
    a_cf = []

    def hand_over(j, e):
        block = wf.at[j, chip ^ e, core]
        a_cf.append(send(block, block, net.sibling()))

    for j in range(nn):
        hand_over(j, 0)
    c_ser.wait()

    def cut_piece(j):
        for r in range(0, piece, 64):
            unit = min(64, piece - r)
            x = ser[j * piece + r : j * piece + r + unit, :]
            chunk[j, r : r + unit, :] = jnp.where(row_mask(j, r, unit), x.astype(F32), 0).astype(BF16)

    for j in range(nn // 2):
        cut_piece(j)
    pull_first(n_mid[others[-1]])
    cut_piece(nn // 2)
    exchange_grad(0)
    for j in range(nn // 2 + 1, nn):
        cut_piece(j)
    c_chunk = [local(chunk, chunk_hbm), local(chunk.at[n], land_s.at[:, lanes(n)])]
    for j in range(nn):
        pooled[j * c.poolw : (j + 1) * c.poolw, :] = dot_nn(pool[...], chunk[j]).astype(BF16)
    pull_rest(z_k)
    c_fk.wait()
    c_fo.wait()
    a_ck = [send(wk.at[:, core], wk.at[:, core], net.sibling()), send(wo.at[:, core], wo.at[:, core], net.sibling())]
    c_bg.wait()
    c_fut.wait()

    def negate(r, unit):
        at = ds(r, unit)
        mask = steps(unit, nn * rows) + (n * piece + r) >= pads[...]
        bg[at, :] = jnp.where(mask, -bg[at, :].astype(F32), 0).astype(BF16)

    row_loop(piece, 16, negate)
    for copy in c_tables:
        copy.wait()
    for copy in a_ck:
        copy.wait_recv()

    def partial(j):
        back = wk[...].reshape(hid, piece)
        fore = wo[...].reshape(hid, part)
        part3[j, :hid, :] = (dot_nn(back, bg[:, lanes(j)]) + dot_nn(fore, fut[:, lanes(j)])).astype(BF16)
        ahead = dot_tn(all_f[...], fut[:, lanes(j)]) * c.scale_f
        part3[j, hid:, :] = ahead[: c.fcount].astype(BF16)

    each(nn, partial)

    def add_part(m, k, h):
        part3[n ^ m, h, :] = (part3[n ^ m, h, :].astype(F32) + land3[k, h, :].astype(F32)).astype(BF16)

    s_part = [
        Scatter(
            net, net.narrow, order,
            lambda m, h=h: part3.at[n ^ m, h],
            lambda k, h=h: land3.at[k, h],
            lambda m, k, h=h: add_part(m, k, h),
        )
        for order, h in zip(orders, halves(hid + c.fcount))
    ]
    for s in s_part:
        s.start()
    bt[0, ds(4 + n, 1), :piece] = sums(bg[...])
    bt[0, ds(4 + n, 1), pw : pw + part] = sums(fut[...])
    exchange_grad(1)
    for j, g in enumerate(z_f):
        g.pull(g.masks()[0])
        hand_over(j, g.masks()[0])
    a_cm = []
    for e in n_mid:
        pull_rest(n_mid[e])
        block = wmid.at[chip ^ e, core]
        a_cm.append(send(block, block, net.sibling()))
    for copy in a_cm:
        copy.wait_recv()
    layer(0, pooled, 0)
    layer(1, act.at[0], 1)
    layer(2, act.at[1], 2)
    theta = act.at[6]
    for r in bands:
        theta[r, :] = (dot_tn(weight_columns(3, r), act[2]) + bcol[r, 6:7]).astype(BF16)
    for s in s_part:
        s.finish()
        if s.step < len(near):
            s.start()
    for copy in c_chunk:
        copy.wait()
    c_pick.wait()
    c_mix.wait()

    def residual(j):
        tw[j] = dot_nn(pick[j], theta[...]).astype(BF16)
        temp[:piece, :] = dot_nn(mix_b[j], tw[j])

        def body(r, unit):
            at = ds(r, unit)
            x = chunk[j, at, :].astype(F32) - temp[at, :] * c.scale
            chunk[j, at, :] = jnp.where(row_mask(j, r, unit), x, 0).astype(BF16)

        row_loop(piece, 144, body)

    each(nn, residual)
    exchange_grad(2)
    used = ds(0, c.used)
    twa[used, lanes(n)] = tw[n, : c.used, :]
    for m in z_f[0].masks()[1:]:
        for j, g in enumerate(z_f):
            g.pull(m)
            hand_over(j, m)
    early = len(net.copies)
    for copy in a_cf[:-nn]:
        copy.wait_recv()
    for j in range(nn):
        a_cf[j - nn].wait_recv()
        for z, r in enumerate(bands):
            total = dot_nn(wf[j, z].reshape(tall, piece), chunk[j])
            if j:
                total += pre[3, r, :]
            if j < nn - 1:
                pre[3, r, :] = total
            else:
                settle(3, r, total, 3)
    layer(4, act.at[3], 4)
    layer(5, act.at[4], 5)
    f3a[:, lanes(n)] = act[5]
    n_f3 = [
        Gather(net, net.narrow, order, lambda m, h=h: f3a.at[h, lanes(n ^ m)], act.at[5, h])
        for order, h in zip(orders, halves(hid))
    ]
    while s_part[0].step < len(near):
        for s in s_part:
            s.finish()
            s.start()
    k3 = [s.last() for s in s_part]

    def collect(h, k):
        def body(r, unit):
            at = ds(h.start + r, unit)
            total = part3[n, at, :].astype(F32) + land3[k, at, :].astype(F32)
            grads[0, at, :] = (total * slope(pre[5, at, :])).astype(BF16)

        return body

    cut = (hid + c.fcount) // 2
    row_loop(cut, 96, collect(ds(0, cut), k3[0]))
    row_loop(hid - cut, 96, collect(ds(cut, hid - cut), k3[1]))
    sfore[...] = (part3[n, hid:, :].astype(F32) + land3[k3[1], hid:, :].astype(F32)).astype(BF16)
    layer_back(5, grads.at[0], 4, 1)
    layer_back(4, grads.at[1], 3, 2)
    a_tw = [send(tw.at[n ^ d, used], twa.at[used, lanes(n)], net.narrow(d)) for d in range(1, nn)]
    r_cf = []
    for j in range(nn):
        gf[j] = dot_nt(grads[2], chunk[j]).astype(BF16).reshape(nc, 2, c.hw, piece)
        r_cf.append(send(gf.at[j, :, 1 - core], cf.at[j], net.sibling()))

    def add_f(j):
        for z in range(nc):
            cf[j, z] = (gf[j, z, core].astype(F32) + cf[j, z].astype(F32)).astype(BF16)

    def add_zf(j, e, k):
        cf[j, chip ^ e] = (cf[j, chip ^ e].astype(F32) + zf[k, j].astype(F32)).astype(BF16)

    def forward_f(j):
        r_zf[j].finish()
        r_zf[j].start()

    r_zf = [
        Scatter(
            net, net.chips, back_far,
            lambda e, j=j: cf.at[j, chip ^ e],
            lambda k, j=j: zf.at[k, j],
            lambda e, k, j=j: add_zf(j, e, k),
        )
        for j in range(nn)
    ]
    for j in range(nn):
        r_cf[j].wait_recv()
        add_f(j)
        r_zf[j].start()
    for copy in net.copies[:early]:
        copy.wait_send()
    put_weight(5, dot_nt(grads[0], act[4]))
    put_weight(4, dot_nt(grads[1], act[3]))
    inner, outer = ds(c.off[4], c.off[-1] - c.off[4]), ds(0, c.off[4])
    r_ci = send(wmid.at[:, 1 - core, :, :, inner], cm.at[:, :, :, inner], net.sibling())
    c_ga.wait()
    for copy in a_ga:
        copy.wait_recv()
    temp2[...] = jnp.zeros_like(temp2)

    def resid_grad(j):
        temp[:piece, :] = dot_tn(wf[j].reshape(hid, piece), grads[2])

        def body(r, unit):
            at = ds(r, unit)
            x = land_g[j, at, :].astype(F32) + temp[at, :]
            land_g[j, at, :] = jnp.where(row_mask(j, r, unit), x, 0).astype(BF16)

        row_loop(piece, 144, body)
        pull = (dot_tn(mix_b[j], land_g[j]) * -c.scale).astype(BF16)
        temp2[...] += dot_tn(pick[j, :, :bw], pull)

    each(nn // 2, resid_grad)
    pull_first(n_f3)
    r_ci.wait_recv()
    for z in range(nc):
        both = wmid[z, core, :, :, inner].astype(F32) + cm[z, :, :, inner].astype(F32)
        cm[z, :, :, inner] = both.astype(BF16)

    def add_zi(e, k):
        both = cm[chip ^ e, :, :, inner].astype(F32) + zi[k].astype(F32)
        cm[chip ^ e, :, :, inner] = both.astype(BF16)

    def add_ni(m, k):
        both = cm[chip, n ^ m, :, inner].astype(F32) + ni[k].astype(F32)
        cm[chip, n ^ m, :, inner] = both.astype(BF16)

    r_zi = Scatter(net, net.chips, back_far, lambda e: cm.at[chip ^ e, :, :, inner], lambda k: zi.at[k], add_zi)
    r_zi.start()
    exchange_series(0)
    each(nn - nn // 2, lambda i: resid_grad(i + nn // 2))
    dth = grads.at[3]
    dth[:bw, :] = temp2[...].astype(BF16)
    dth[bw:, :] = jnp.zeros_like(dth[bw:, :])
    dth[bw : bw + c.fcount, :] = sfore[...]
    for z, r in enumerate(bands):
        grads[4, r, :] = (dot_nn(weight_rows(3, z), dth[...]) * slope(pre[2, r, :])).astype(BF16)
    layer_back(2, grads.at[4], 1, 5)
    layer_back(1, grads.at[5], 0, 6)
    forward_f(0)
    pgb[...] = dot_tn(weight(0), grads[6]).astype(BF16)
    put_weight(3, dot_nt(act[2], dth[...]))
    put_weight(2, dot_nt(grads[4], act[1]))
    put_weight(1, dot_nt(grads[5], act[0]))
    put_weight(0, dot_nt(grads[6], pooled[...]))
    r_cm = send(wmid.at[:, 1 - core, :, :, outer], cm.at[:, :, :, outer], net.sibling())
    forward_f(1)
    for k, slot_k in enumerate((6, 5, 4, 3, 2, 1, 0)):
        bt[0, k // 2 : k // 2 + 1, (k % 2) * hid : (k % 2 + 1) * hid] = sums(grads[slot_k])
    travel = [net.sibling()] + [net.narrow(b) for b in near] + [net.chips(b) for b in back_far]
    v_copies = []

    def send_bias():
        k = len(v_copies)
        v_copies.append(send(bt.at[k], bl.at[k], travel[k]))

    def add_bias():
        k = len(v_copies) - 1
        v_copies[k].wait_recv()
        bt[k + 1] = bt[k] + bl[k]

    send_bias()
    pull_rest(n_f3)
    gk[...] = dot_nt(f3a[...], bg[...]).astype(BF16).reshape(nc, 2, c.hw, piece)
    r_cm.wait_recv()
    for z in range(nc):
        both = wmid[z, core, :, :, outer].astype(F32) + cm[z, :, :, outer].astype(F32)
        cm[z, :, :, outer] = both.astype(BF16)

    def add_nm(m, k, h):
        cm[:, n ^ m, :, h] = (cm[:, n ^ m, :, h].astype(F32) + nm[k, :, :, h].astype(F32)).astype(BF16)

    r_nm = [
        Scatter(
            net, net.narrow, order,
            lambda m, h=h: cm.at[:, n ^ m, :, h],
            lambda k, h=h: nm.at[k, :, :, h],
            lambda m, k, h=h: add_nm(m, k, h),
        )
        for order, h in zip(orders, half_outer)
    ]
    for s in r_nm:
        s.start()
    add_bias()
    send_bias()
    exchange_series(1)
    go[...] = dot_nt(f3a[...], fut[...]).astype(BF16).reshape(nc, 2, c.hw, part)
    r_ck = [send(gk.at[:, 1 - core], ck, net.sibling()), send(go.at[:, 1 - core], co, net.sibling())]
    def add_k(e, k):
        ck[chip ^ e] = (ck[chip ^ e].astype(F32) + zk[k].astype(F32)).astype(BF16)

    def add_o(e, k):
        co[chip ^ e] = (co[chip ^ e].astype(F32) + zo[k].astype(F32)).astype(BF16)

    r_zk = [
        Scatter(net, net.chips, back_far, lambda e: ck.at[chip ^ e], lambda k: zk.at[k], add_k),
        Scatter(net, net.chips, back_far, lambda e: co.at[chip ^ e], lambda k: zo.at[k], add_o),
    ]

    def series_grad(j):
        temp[:piece, :] = dot_tn(pool[...], pgb[j * c.poolw : (j + 1) * c.poolw, :])
        for r in range(0, piece, 64):
            unit = min(64, piece - r)
            x = land_g[j, r : r + unit, :].astype(F32) + temp[r : r + unit, :]
            x = jnp.where(row_mask(j, r, unit), x, 0).astype(BF16)
            ser[j * piece + r : j * piece + r + unit, :] = x

    def outputs(k):
        h = parts[k]
        for copy in a_sa[k * (nn - 1) : (k + 1) * (nn - 1)]:
            copy.wait_recv()
        local(land_s.at[h], bg.at[h]).wait()
        stop = h.start + h.size
        marks = [r for r in range(h.start, stop, LANE) if stop - r >= LANE // 2] + [stop]
        for low, high in zip(marks[:-1], marks[1:]):
            temp3[: high - low, :] = dot_nn(mix_b[n, low:high, :], twa[...])
            temp4[: high - low, :] = dot_tn(wk[:, :, :, low:high].reshape(hid, high - low), f3a[...])

            def body(r, unit, low=low):
                at, here = ds(low + r, unit), ds(r, unit)
                x = (bg[at, :].astype(F32) - temp3[here, :] * c.scale).astype(BF16).astype(F32)
                x = x - (temp4[here, :] + ecol[at, 0:1])
                mask = steps(unit, nn * rows) + (n * piece + low + r) >= pads[...]
                bg[at, :] = jnp.where(mask, x, 0).astype(BF16)

            row_loop(high - low, 32, body)
        local(bg.at[h], left_out.at[h])

    def forecast():
        fore = dot_nn(mix_f[...], twa[...]) * c.scale_f
        pred[...] = fore + dot_tn(wo[...].reshape(hid, part), f3a[...]) + ecol[pw : pw + part, 0:1]

    def add_nf(m, k, h):
        cf[n ^ m, chip, h, :] = (cf[n ^ m, chip, h, :].astype(F32) + nf[k, h, :].astype(F32)).astype(BF16)

    def add_zm(e, k):
        both = cm[chip ^ e, n, :, outer].astype(F32) + zm[k].astype(F32)
        cm[chip ^ e, n, :, outer] = both.astype(BF16)

    r_zm = Scatter(net, net.chips, back_far, lambda e: cm.at[chip ^ e, n, :, outer], lambda k: zm.at[k], add_zm)
    r_nf = [
        Scatter(
            net, net.narrow, order,
            lambda m, h=h: cf.at[n ^ m, chip, h],
            lambda k, h=h: nf.at[k, h],
            lambda m, k, h=h: add_nf(m, k, h),
        )
        for order, h in zip(orders, halves(c.hw))
    ]
    series_grad(0)
    forward_f(2)
    for j in range(1, nn - 1):
        series_grad(j)
    for j in range(3, nn):
        forward_f(j)
    for copy in r_ck:
        copy.wait_recv()
    for z in range(nc):
        ck[z] = (gk[z, core].astype(F32) + ck[z].astype(F32)).astype(BF16)
        co[z] = (go[z, core].astype(F32) + co[z].astype(F32)).astype(BF16)
    for s in r_nm:
        s.finish()
        s.start()
    add_bias()
    send_bias()
    series_grad(nn - 1)
    exchange_series(2)
    c_tid = local(ser, tid_out)
    for copy in a_tw:
        copy.wait_recv()
    forecast()
    c_pred = local(pred, pred_out)
    outputs(0)
    for s in r_nm:
        s.finish()
    r_zm.start()
    add_bias()
    send_bias()
    for s in r_zk:
        s.start()
    r_zi.finish()
    r_zi.start()
    for s in r_zf:
        s.finish()
    for s in r_nf:
        s.start()
    outputs(1)
    exchange_series(3)
    exchange_series(4)
    r_zm.finish()
    r_zm.start()
    add_bias()
    send_bias()
    outputs(2)
    for s in r_zk:
        s.finish()
        s.start()
    for s in r_nf:
        s.finish()
        s.start()
    r_zi.finish()
    r_ni = Scatter(net, net.narrow, near, lambda m: cm.at[chip, n ^ m, :, inner], lambda k: ni.at[k], add_ni)
    r_ni.start()
    add_bias()
    obias[...] = bt[len(travel)]
    outputs(3)
    r_zm.finish()
    outputs(4)
    r_ni.finish()
    r_ni.start()
    for s in r_nf:
        s.finish()
    of[...] = cf[n, chip].astype(F32)
    for s in r_zk:
        s.finish()
    ok[...] = ck[chip].astype(F32)
    oo[...] = co[chip].astype(F32)
    r_ni.finish()
    om[...] = cm[chip, n].astype(F32)
    drain()
    assert len(net.copies) <= sends.shape[0] and len(owned) <= own.shape[0]


def finish(c, *refs):
    large_in, small_in, large_out, small_out = refs[:3], refs[3:8], refs[8:11], refs[11:29]
    held, (om, of, ok, oo, obias), given, sems = refs[29:32], refs[32:37], refs[37:55], refs[55]
    g1, v1, g2, v2, g3, v3, g4, v4, gf, vf1, g5, vf2, g6, vf3, gk, vk, go, vo = given
    arriving = [
        pltpu.make_async_copy(src, dst, sems.at[48 + k])
        for k, (src, dst) in enumerate(zip(small_in, (om, of, ok, oo, obias)))
    ]
    leaving = [
        pltpu.make_async_copy(src, dst, sems.at[53 + k]) for k, (src, dst) in enumerate(zip(given, small_out))
    ]
    for copy in arriving:
        copy.start()
    pieces = []
    for a, (src, via, dst) in enumerate(zip(large_in, held, large_out)):
        size = up(-(-src.shape[0] // 8), 16)
        for b, r in enumerate(range(0, src.shape[0], size)):
            h = pl.ds(r, min(size, src.shape[0] - r))
            k = 16 * a + 2 * b
            pieces.append(
                (
                    pltpu.make_async_copy(src.at[h], via.at[h], sems.at[k]),
                    pltpu.make_async_copy(via.at[h], dst.at[h], sems.at[k + 1]),
                )
            )
    for inward, outward in pieces:
        inward.start()
    for copy in arriving:
        copy.wait()
    nn, piece, part, hid, bw = c.nn, c.piece, c.part, c.hid, c.bw
    for j in range(nn):
        g1[:, j * c.pools : (j + 1) * c.pools] = om[:, j * c.poolw : j * c.poolw + c.pools]
    for k, g in ((1, g2), (2, g3), (4, g5), (5, g6)):
        g[...] = om[:, c.off[k] : c.off[k + 1]]
    fore = g4.shape[1] - c.bcount
    g4[:, : c.bcount] = om[:, c.off[3] : c.off[3] + c.bcount]
    g4[:, c.bcount :] = om[:, c.off[3] + bw : c.off[3] + bw + fore]
    gf[...] = of[...]
    gk[...] = ok[...]
    go[...] = oo[...]
    for k, v in enumerate((v1, v2, v3, None, vf1, vf2, vf3)):
        if v is not None:
            v[...] = obias[k // 2 : k // 2 + 1, (k % 2) * hid : (k % 2 + 1) * hid].reshape(hid)
    theta = obias[1:2, hid : 2 * hid]
    v4[...] = jnp.concatenate([theta[:, : c.bcount], theta[:, bw : bw + fore]], axis=1).reshape(v4.shape[0])
    vk[...] = jnp.concatenate([obias[4 + j : 5 + j, :piece] for j in range(nn)], axis=1).reshape(vk.shape[0])
    vo[...] = jnp.concatenate([obias[4 + j : 5 + j, c.pw : c.pw + part] for j in range(nn)], axis=1).reshape(vo.shape[0])
    for copy in leaving:
        copy.start()
    for inward, outward in pieces:
        inward.wait()
        outward.start()
    for inward, outward in pieces:
        outward.wait()
    for copy in leaving:
        copy.wait()


def fast(nn, nw, series, padding, *rest):
    (cf, cfb, cs, csb, ct, ctb, cb, cbb, ff, ffb, fs, fsb, ft, ftb, fk, fkb, fo, fob, grad, fut) = rest
    nc = nw // 2
    rows, length = series.shape
    piece, part = grad.shape[1], fut.shape[1]
    ahead = part * nn
    hid = cfb.shape[0]
    hs, hw = hid // (nn * nw), hid // nw
    back_count, fore_count = KB, cbb.shape[0] - KB
    bw, fw = up(back_count, LANE), up(fore_count, LANE)
    used, (pick, mix_b, mix_f, all_f) = window_tables(nn, length, ahead, back_count, fore_count)
    width = pick.shape[1]
    fcount = up(fore_count, 16)
    pools = piece // POOL
    poolw = up(pools, LANE)
    widths = (nn * poolw, hid, hid, bw + fw, hid, hid)
    off = np.concatenate([[0], np.cumsum(widths)]).tolist()
    mw = off[-1]
    pw = up(piece, LANE)
    assert bw + fw == hid
    c = types.SimpleNamespace(
        nn=nn, nc=nc, rows=rows, piece=piece, part=part, hid=hid, hs=hs, hw=hw, pw=pw, bw=bw,
        off=off, poolw=poolw, pools=pools, used=up(used, 16), fcount=fcount,
        bcount=back_count, half=up(mw // 2, LANE),
        scale=1.0 / (2 * (length // back_count)),
        scale_f=1.0 / (2 * (ahead // fore_count)),
    )
    anyspec = pl.BlockSpec(memory_space=pl.ANY)
    vspec = pl.BlockSpec(memory_space=pltpu.VMEM)
    S, V = jax.ShapeDtypeStruct, pltpu.VMEM
    bs = (up(4 + nn, 8), max(2 * hid, pw + up(part, LANE)))
    stages = 1 + len(bits(nn)) + len(bits(nc))
    gathers = (nc - 1) + 2 * nc * (nn - 1) + 2 * (nn - 1) + 3 * (nc - 1) + 2 + 2 * nc
    ncopies = gathers + 12 * (nn + nc) + 6 * nn * nc
    qw = up(part, LANE)
    scratch = [
        V((nn, width, bw + fw), BF16),
        V((nn, piece, width), BF16),
        V((length, rows), BF16),
        V((nn, piece, rows), BF16),
        V((nn, piece, rows), BF16),
        V((piece, nn * rows), BF16),
        V((part, nn * rows), BF16),
        V((nc, 2, nn, hs, mw), BF16),
        V((nn, nc, 2, hw, piece), BF16),
        V((nc, 2, hw, piece), BF16),
        V((nc, 2, hw, part), BF16),
        V((nn, hid + fcount, rows), BF16),
        V((nn - 1, hid + fcount, rows), BF16),
        V((hid, nn * rows), BF16),
        V((nn, width, rows), BF16),
        V((width, nn * rows), BF16),
        V((6, hid, rows), F32),
        V((7, hid, rows), BF16),
        V((nn * poolw, rows), BF16),
        V((part, nn * rows), F32),
        V((nn, nc, 2, hw, piece), BF16),
        V((nc, 2, hw, piece), BF16),
        V((nc, 2, hw, part), BF16),
        V((nc, nn, hs, mw), BF16),
        V((nn, nc, hw, piece), BF16),
        V((nc, hw, piece), BF16),
        V((nc, hw, part), BF16),
        V((nn - 1, nc, hs, off[4]), BF16),
        V((nc - 1, hs, off[4]), BF16),
        V((nc - 1, nn, hs, mw - off[4]), BF16),
        V((nn - 1, hs, mw - off[4]), BF16),
        V((nc - 1, nn, hw, piece), BF16),
        V((nn - 1, hw, piece), BF16),
        V((nc - 1, hw, piece), BF16),
        V((nc - 1, hw, part), BF16),
        V((piece, rows), F32),
        V((LANE + up(piece % LANE, 16), nn * rows), F32),
        V((LANE + up(piece % LANE, 16), nn * rows), F32),
        V((bw, rows), F32),
        V((7, hid, rows), BF16),
        V((fcount, rows), BF16),
        V((nn * poolw, rows), BF16),
        V((poolw, piece), BF16),
        V((1, nn * rows), jnp.int32),
        V((8, hid), F32),
        V((8, pw + qw), F32),
        V((hid, 8), F32),
        V((pw + qw, 8), F32),
        V((stages + 1,) + bs, F32),
        V((stages,) + bs, F32),
    ]
    scratch += [V(w.shape, BF16) for w in (cf, cs, ct, cb, fs, ft)]
    scratch += [V(b.shape, b.dtype) for b in (padding, cfb, csb, ctb, cbb, ffb, fsb, ftb, fkb, fob)]
    scratch += [
        V(mix_f.shape[1:], BF16),
        V(all_f.shape[1:], BF16),
        pltpu.SemaphoreType.DMA((ncopies,)),
        pltpu.SemaphoreType.DMA((ncopies,)),
        pltpu.SemaphoreType.DMA((40 + 8 * nn,)),
    ]
    leftover, pred, tid, om, of, ok, oo, obias, _, _ = pl.pallas_call(
        functools.partial(whole, c),
        out_shape=(
            S((piece, nn * rows), BF16),
            S((part, nn * rows), F32),
            S((length, rows), BF16),
            S((hs, mw), F32),
            S((hw, piece), F32),
            S((hw, piece), F32),
            S((hw, part), F32),
            S(bs, F32),
            S((nn, piece, rows), BF16),
            S((piece, nn * rows), BF16),
        ),
        in_specs=[anyspec] * 26,
        out_specs=[anyspec] * 3 + [vspec] * 5 + [anyspec] * 2,
        scratch_shapes=scratch,
        compiler_params=params(0),
    )(
        padding, cfb, csb, ctb, cbb, ffb, fsb, ftb, fkb, fob, cf, cs, ct, cb, fs, ft, mix_f, all_f,
        pick, mix_b, series.T, grad.T, fut.T, ff, fk, fo,
    )
    params_like = (cf, cfb, cs, csb, ct, ctb, cb, cbb, ff, ffb, fs, fsb, ft, ftb, fk, fkb, fo, fob)
    outs = pl.pallas_call(
        functools.partial(finish, c),
        out_shape=tuple(S(x.shape, x.dtype) for x in (leftover, pred, tid))
        + tuple(S(p.shape, F32) for p in params_like),
        in_specs=[anyspec] * 8,
        out_specs=[anyspec] * 21,
        scratch_shapes=[V(x.shape, x.dtype) for x in (leftover, pred, tid, om, of, ok, oo, obias)]
        + [V(p.shape, F32) for p in params_like]
        + [pltpu.SemaphoreType.DMA((72,))],
        compiler_params=pltpu.CompilerParams(vmem_limit_bytes=60 << 20),
    )(leftover, pred, tid, om, of, ok, oo, obias)
    return (outs[0].T, outs[1].T, outs[2].T) + tuple(outs[3:])


def upsample(coef, length):
    coef_count = coef.shape[1]
    stride = length // coef_count
    halfway = stride // 2
    padded = jnp.concatenate([coef[:, :1], coef, coef[:, -1:]], axis=1)
    preceding = jnp.repeat(padded[:, :coef_count], stride, axis=1)
    central = jnp.repeat(padded[:, 1 : coef_count + 1], stride, axis=1)
    following = jnp.repeat(padded[:, 2:], stride, axis=1)
    offsets = jnp.arange(length, dtype=jnp.int32) % stride
    in_front = offsets < halfway
    fraction = (
        jnp.where(in_front, offsets + halfway, offsets - halfway).astype(jnp.float32) + 0.5
    ) / stride
    lower_val = jnp.where(in_front[None, :], preceding, central)
    upper_val = jnp.where(in_front[None, :], central, following)
    return lower_val * (1.0 - fraction) + upper_val * fraction


def silu_slope(value):
    sigma = jax.nn.sigmoid(value)
    return sigma * (1.0 + value * (1.0 - sigma))


def project_rows(rows_in, matrix):
    return lax.dot_general(
        rows_in, matrix, (((1,), (1,)), ((), ())), preferred_element_type=jnp.float32
    )


def apply_rows(rows_in, matrix):
    return jnp.dot(rows_in, matrix, preferred_element_type=jnp.float32)


def column_outer(first_rows, second_rows):
    return lax.dot_general(
        first_rows, second_rows, (((0,), (0,)), ((), ())), preferred_element_type=jnp.float32
    )


def own_slice(values, begin, amount):
    return lax.dynamic_slice_in_dim(values, begin, amount, 0)


def column_sums(values):
    return jnp.sum(values.astype(jnp.float32), axis=0)


def general(
    series,
    padding,
    coarse_first,
    coarse_first_bias,
    coarse_second,
    coarse_second_bias,
    coarse_third,
    coarse_third_bias,
    coarse_basis,
    coarse_basis_bias,
    fine_first,
    fine_first_bias,
    fine_second,
    fine_second_bias,
    fine_third,
    fine_third_bias,
    fine_back,
    fine_back_bias,
    fine_fore,
    detailed_predict_offset,
    grad_resid,
    future_cotangent_array,
):
    slim_breadth = lax.axis_size("narrow")
    slim_position = lax.axis_index("narrow")
    onsite_tally, length = series.shape
    ahead = future_cotangent_array.shape[1] * slim_breadth
    sample_group = onsite_tally // PASSES
    piece = length // slim_breadth
    predicted_portion = ahead // slim_breadth
    group_pads = padding.reshape(slim_breadth, onsite_tally)
    own_pads = lax.dynamic_slice_in_dim(group_pads, slim_position, 1, 0)[0]
    steps_all = jnp.arange(length, dtype=jnp.int32)
    time_start = slim_position * piece
    predict_onset = slim_position * predicted_portion
    steps_piece = time_start + jnp.arange(piece, dtype=jnp.int32)
    back_bias = lax.dynamic_slice_in_dim(fine_back_bias, time_start, piece, 0)
    predict_offset = lax.dynamic_slice_in_dim(
        detailed_predict_offset, predict_onset, predicted_portion, 0
    )
    resid_grid = grad_resid.reshape(slim_breadth, PASSES, sample_group, piece)
    predict_mesh = future_cotangent_array.reshape(
        slim_breadth, PASSES, sample_group, predicted_portion
    )
    own_start = slim_position * sample_group
    coarse_local = (
        coarse_first,
        coarse_second,
        coarse_third,
        coarse_basis,
        fine_second,
        fine_third,
    )
    fine_local = (fine_first, fine_back, fine_fore)
    totals = tuple((jnp.zeros(w.shape, jnp.float32) for w in coarse_local))
    fine_totals = tuple((jnp.zeros(w.shape, jnp.float32) for w in fine_local))
    bias_totals = tuple(
        (
            jnp.zeros(b.shape, jnp.float32)
            for b in (
                coarse_first_bias,
                coarse_second_bias,
                coarse_third_bias,
                coarse_basis_bias,
                fine_first_bias,
                fine_second_bias,
                fine_third_bias,
                fine_back_bias,
                detailed_predict_offset,
            )
        )
    )
    residual_parts = []
    predicted_portions = []
    grad_parts = []
    for iteration_index in range(PASSES):
        shared = (
            lax.all_gather(coarse_first, ("wide", "narrow"), axis=0, tiled=True),
            lax.all_gather(coarse_second, ("wide", "narrow"), axis=0, tiled=True),
            lax.all_gather(coarse_third, ("wide", "narrow"), axis=0, tiled=True),
            lax.all_gather(coarse_basis, ("wide", "narrow"), axis=0, tiled=True),
            lax.all_gather(fine_second, ("wide", "narrow"), axis=0, tiled=True),
            lax.all_gather(fine_third, ("wide", "narrow"), axis=0, tiled=True),
        )
        pieces = (
            lax.all_gather(fine_first, "wide", axis=0, tiled=True),
            lax.all_gather(fine_back, "wide", axis=0, tiled=True),
            lax.all_gather(fine_fore, "wide", axis=0, tiled=True),
        )
        weight_one, weight_two, weight_three, weight_basis, inner_two, inner_three = shared
        inner_one, inner_back, inner_fore = pieces
        lower = iteration_index * sample_group
        mask = (steps_all[None, :] >= own_pads[lower : lower + sample_group, None]).astype(
            jnp.float32
        )
        started = series[lower : lower + sample_group].astype(jnp.float32) * mask
        pooled = jnp.mean(started.reshape(sample_group, length // POOL, POOL), axis=2).astype(
            jnp.bfloat16
        )
        linear_one = project_rows(pooled, weight_one) + coarse_first_bias
        hidden_one = jax.nn.silu(linear_one).astype(jnp.bfloat16)
        linear_two = project_rows(hidden_one, weight_two) + coarse_second_bias
        hidden_two = jax.nn.silu(linear_two).astype(jnp.bfloat16)
        linear_three = project_rows(hidden_two, weight_three) + coarse_third_bias
        hidden_three = jax.nn.silu(linear_three).astype(jnp.bfloat16)
        theta = apply_rows(hidden_three, weight_basis) + coarse_basis_bias
        backcast = upsample(theta[:, :KB], length)
        coarse_fore = upsample(theta[:, KB:], ahead)
        residual_here = (started - backcast) * mask
        sent_resid, sent_fore = (
            lax.all_to_all(
                residual_here.astype(jnp.bfloat16),
                "narrow",
                split_axis=1,
                concat_axis=0,
                tiled=True,
            ),
            lax.all_to_all(
                coarse_fore.astype(jnp.bfloat16), "narrow", split_axis=1, concat_axis=0, tiled=True
            ),
        )
        pads_here = group_pads[:, lower : lower + sample_group].reshape(-1)
        piece_mask = (steps_piece[None, :] >= pads_here[:, None]).astype(jnp.float32)
        first_partial = project_rows(sent_resid, inner_one)
        lift_one = lax.psum(first_partial, "narrow") + fine_first_bias
        fine_one = jax.nn.silu(lift_one).astype(jnp.bfloat16)
        lift_two = project_rows(fine_one, inner_two) + fine_second_bias
        fine_two = jax.nn.silu(lift_two).astype(jnp.bfloat16)
        lift_three = project_rows(fine_two, inner_three) + fine_third_bias
        fine_three = jax.nn.silu(lift_three).astype(jnp.bfloat16)
        coef_back = apply_rows(fine_three, inner_back) + back_bias
        coef_fore = apply_rows(fine_three, inner_fore) + predict_offset
        residual_parts.append(
            ((sent_resid.astype(jnp.float32) - coef_back) * piece_mask)
            .astype(jnp.bfloat16)
            .reshape(slim_breadth, sample_group, piece)
        )
        predicted_portions.append(
            (sent_fore.astype(jnp.float32) + coef_fore).reshape(
                slim_breadth, sample_group, predicted_portion
            )
        )
        out_grad = (
            resid_grid[:, iteration_index]
            .reshape(slim_breadth * sample_group, piece)
            .astype(jnp.float32)
        )
        predict_cotan = predict_mesh[:, iteration_index].reshape(
            slim_breadth * sample_group, predicted_portion
        )
        back_grad = (-out_grad * piece_mask).astype(jnp.bfloat16)
        coef_partial = project_rows(back_grad, inner_back) + project_rows(predict_cotan, inner_fore)
        three_grad = lax.psum(coef_partial, "narrow")
        lift_three_grad = (three_grad * silu_slope(lift_three)).astype(jnp.bfloat16)
        lift_two_grad = (apply_rows(lift_three_grad, inner_three) * silu_slope(lift_two)).astype(
            jnp.bfloat16
        )
        lift_one_grad = (apply_rows(lift_two_grad, inner_two) * silu_slope(lift_one)).astype(
            jnp.bfloat16
        )
        own_one_grad = own_slice(lift_one_grad, own_start, sample_group)
        own_two_grad = own_slice(lift_two_grad, own_start, sample_group)
        own_three_grad = own_slice(lift_three_grad, own_start, sample_group)
        own_fine_one = own_slice(fine_one, own_start, sample_group)
        own_fine_two = own_slice(fine_two, own_start, sample_group)
        sent_grad = (out_grad * piece_mask + apply_rows(lift_one_grad, inner_one)).astype(
            jnp.bfloat16
        )
        resid_back, fore_back = (
            lax.all_to_all(sent_grad, "narrow", split_axis=0, concat_axis=1, tiled=True),
            lax.all_to_all(predict_cotan, "narrow", split_axis=0, concat_axis=1, tiled=True),
        )
        grad_inner_one = column_outer(lift_one_grad, sent_resid)
        grad_inner_back = column_outer(fine_three, back_grad)
        grad_inner_fore = column_outer(fine_three, predict_cotan)
        grad_inner_two = column_outer(own_two_grad, own_fine_one)
        grad_inner_three = column_outer(own_three_grad, own_fine_two)
        resid_grad = resid_back.astype(jnp.float32)
        back_pull = jax.vjp(lambda coef: upsample(coef, length), theta[:, :KB])[1]
        fore_pull = jax.vjp(lambda coef: upsample(coef, ahead), theta[:, KB:])[1]
        back_coef_grad = back_pull(-resid_grad * mask)[0]
        fore_coef_grad = fore_pull(fore_back.astype(jnp.float32))[0]
        theta_grad = jnp.concatenate([back_coef_grad, fore_coef_grad], axis=1).astype(jnp.bfloat16)
        coarse_three_grad = (
            project_rows(theta_grad, weight_basis) * silu_slope(linear_three)
        ).astype(jnp.bfloat16)
        coarse_two_grad = (
            apply_rows(coarse_three_grad, weight_three) * silu_slope(linear_two)
        ).astype(jnp.bfloat16)
        coarse_one_grad = (apply_rows(coarse_two_grad, weight_two) * silu_slope(linear_one)).astype(
            jnp.bfloat16
        )
        pooled_grad = apply_rows(coarse_one_grad, weight_one)
        start_grad = resid_grad * mask + jnp.repeat(pooled_grad, POOL, axis=1) / POOL
        grad_parts.append((start_grad * mask).astype(jnp.bfloat16))
        grad_weight_one = column_outer(coarse_one_grad, pooled)
        grad_weight_two = column_outer(coarse_two_grad, hidden_one)
        grad_weight_three = column_outer(coarse_three_grad, hidden_two)
        grad_weight_basis = column_outer(hidden_three, theta_grad)
        bias_terms = (
            column_sums(coarse_one_grad),
            column_sums(coarse_two_grad),
            column_sums(coarse_three_grad),
            column_sums(theta_grad),
            column_sums(own_one_grad),
            column_sums(own_two_grad),
            column_sums(own_three_grad),
            lax.dynamic_update_slice_in_dim(
                jnp.zeros((length,), jnp.float32), column_sums(back_grad), time_start, 0
            ),
            lax.dynamic_update_slice_in_dim(
                jnp.zeros((ahead,), jnp.float32), column_sums(predict_cotan), predict_onset, 0
            ),
        )
        bias_totals = tuple((total + term for total, term in zip(bias_totals, bias_terms)))
        scattered = (
            lax.psum_scatter(grad_weight_one, ("wide", "narrow"), scatter_dimension=0, tiled=True),
            lax.psum_scatter(grad_weight_two, ("wide", "narrow"), scatter_dimension=0, tiled=True),
            lax.psum_scatter(
                grad_weight_three, ("wide", "narrow"), scatter_dimension=0, tiled=True
            ),
            lax.psum_scatter(
                grad_weight_basis, ("wide", "narrow"), scatter_dimension=0, tiled=True
            ),
            lax.psum_scatter(grad_inner_two, ("wide", "narrow"), scatter_dimension=0, tiled=True),
            lax.psum_scatter(grad_inner_three, ("wide", "narrow"), scatter_dimension=0, tiled=True),
        )
        spread = (
            lax.psum_scatter(
                grad_inner_one.astype(jnp.bfloat16), "wide", scatter_dimension=0, tiled=True
            ).astype(jnp.float32),
            lax.psum_scatter(
                grad_inner_back.astype(jnp.bfloat16), "wide", scatter_dimension=0, tiled=True
            ).astype(jnp.float32),
            lax.psum_scatter(
                grad_inner_fore.astype(jnp.bfloat16), "wide", scatter_dimension=0, tiled=True
            ).astype(jnp.float32),
        )
        totals = tuple((total + term for total, term in zip(totals, scattered)))
        fine_totals = tuple((total + term for total, term in zip(fine_totals, spread)))
    bias_sums = lax.psum(
        (
            bias_totals[0],
            bias_totals[1],
            bias_totals[2],
            bias_totals[3],
            bias_totals[4],
            bias_totals[5],
            bias_totals[6],
            bias_totals[7],
            bias_totals[8],
        ),
        ("wide", "narrow"),
    )
    leftover_signal = jnp.stack(residual_parts, axis=1).reshape(slim_breadth * onsite_tally, piece)
    predicted_future = jnp.stack(predicted_portions, axis=1).reshape(
        slim_breadth * onsite_tally, predicted_portion
    )
    temporal_input_derivative = jnp.concatenate(grad_parts, axis=0)
    return (
        leftover_signal,
        predicted_future,
        temporal_input_derivative,
        totals[0],
        bias_sums[0],
        totals[1],
        bias_sums[1],
        totals[2],
        bias_sums[2],
        totals[3],
        bias_sums[3],
        fine_totals[0],
        bias_sums[4],
        totals[4],
        bias_sums[5],
        totals[5],
        bias_sums[6],
        fine_totals[1],
        bias_sums[7],
        fine_totals[2],
        bias_sums[8],
    )


def fits(nn, nw, series, padding, first, first_bias, *rest):
    hid, length = first_bias.shape[0], series.shape[1]
    paired = all(k & (k - 1) == 0 for k in (nn, nw)) and nw % 2 == 0
    paired = paired and len(bits(nn)) == 2 and len(bits(nw // 2)) == 2
    paired = paired and length > 6 * LANE * nn
    return paired and hid % (16 * nn * nw) == 0 and length % (POOL * nn) == 0 and series.shape[0] % LANE == 0


def solution(mesh):
    both, rows = P(("wide", "narrow"), None), P("wide", "narrow")
    in_specs = (both, P("wide"))
    in_specs += (both, P()) * 4 + (rows, P()) + (both, P()) * 2 + (rows, P()) * 2 + (rows, rows)
    out_specs = (rows, rows, both) + (both, P()) * 4 + (rows, P()) + (both, P()) * 2 + (rows, P()) * 2
    nn, nw = mesh.shape["narrow"], mesh.shape["wide"]

    def body(*args):
        if fits(nn, nw, *args):
            return fast(nn, nw, *args)
        return general(*args)

    return jax.shard_map(body, mesh=mesh, in_specs=in_specs, out_specs=out_specs, check_vma=False)
```

```python
import functools
import types

import jax
import jax.numpy as jnp
import numpy as np
from jax import lax
from jax.experimental import pallas as pl
from jax.experimental.pallas import tpu as pltpu
from jax.sharding import PartitionSpec as P

MESH = pl.DeviceIdType.MESH
POOL = 4
KB = 300
PASSES = 1
LANE = 128
F32 = jnp.float32
BF16 = jnp.bfloat16


def up(value, unit):
    return -(-value // unit) * unit


def interp_table(count, length):
    stride = length // count
    table = np.zeros((count, length), np.float32)
    for t in range(length):
        doubled = 2 * t + 1 - stride
        low = doubled // (2 * stride)
        part = doubled - low * 2 * stride
        table[min(max(low, 0), count - 1), t] += 2 * stride - part
        table[min(max(low + 1, 0), count - 1), t] += part
    return table


def window_tables(nn, length, ahead, back_count, fore_count):
    back, fore = interp_table(back_count, length), interp_table(fore_count, ahead)
    piece, part = length // nn, ahead // nn
    spans = []
    for n in range(nn):
        rows_b = np.nonzero(back[:, n * piece : (n + 1) * piece].any(1))[0]
        rows_f = np.nonzero(fore[:, n * part : (n + 1) * part].any(1))[0]
        spans.append((rows_b, rows_f))
    wide_b = max(len(b) for b, _ in spans)
    wide_f = max(len(f) for _, f in spans)
    width = up(wide_b + wide_f, LANE)
    bw, fw = up(back_count, LANE), up(fore_count, LANE)
    pick = np.zeros((nn, width, bw + fw), np.float32)
    mix_b = np.zeros((nn, piece, width), np.float32)
    mix_f = np.zeros((nn, part, width), np.float32)
    all_f = np.zeros((nn, part, fw), np.float32)
    for n, (rows_b, rows_f) in enumerate(spans):
        all_f[n, :, :fore_count] = fore[:, n * part : (n + 1) * part].T
        for slot, row in enumerate(rows_b):
            pick[n, slot, row] = 1
            mix_b[n, :, slot] = back[row, n * piece : (n + 1) * piece]
        for slot, row in enumerate(rows_f):
            pick[n, wide_b + slot, bw + row] = 1
            mix_f[n, :, wide_b + slot] = fore[row, n * part : (n + 1) * part]
    return wide_b + wide_f, tuple(t.astype(BF16) for t in (pick, mix_b, mix_f, all_f))


class Copy:
    def __init__(self, copy, remote):
        self.copy, self.sent, self.received = copy, False, not remote

    def wait_recv(self):
        if not self.received:
            self.copy.wait_recv()
        self.received = True

    def wait_send(self):
        if not self.sent:
            self.copy.wait_send()
        self.sent = True

    def wait(self):
        if not self.sent:
            self.copy.wait()
        self.sent = True


class Net:
    def __init__(self, sizes, sends, recvs):
        self.nn, self.nc = sizes
        self.sends, self.recvs = sends, recvs
        self.copies = []
        self.w, self.n = lax.axis_index("wide"), lax.axis_index("narrow")
        self.chip, self.core = self.w // 2, self.w % 2

    def chips(self, bit):
        return ((self.chip ^ bit) * 2 + self.core, self.n)

    def narrow(self, bit):
        return (self.w, self.n ^ bit)

    def sibling(self):
        return (self.w ^ 1, self.n)

    def hail(self):
        others = [self.narrow(d) for d in range(1, self.nn)] + [self.chips(b) for b in bits(self.nc)]
        others.append(self.sibling())
        for other in others:
            pl.semaphore_signal(pltpu.get_barrier_semaphore(), 1, device_id=other, device_id_type=MESH)
        self.others = len(others)

    def meet(self):
        pl.semaphore_wait(pltpu.get_barrier_semaphore(), self.others)

    def send(self, src, dst, to):
        k = len(self.copies)
        copy = pltpu.make_async_remote_copy(
            src_ref=src,
            dst_ref=dst,
            send_sem=self.sends.at[k],
            recv_sem=self.recvs.at[k],
            device_id=to,
            device_id_type=MESH,
        )
        copy.start()
        self.copies.append(Copy(copy, True))
        return self.copies[-1]

    def drain(self):
        for copy in self.copies:
            copy.wait_recv()
            copy.wait_send()


def bits(count):
    return [1 << k for k in reversed(range(count.bit_length() - 1))]


class Gather:
    def __init__(self, net, to, order, block, own=None):
        self.net, self.to, self.order, self.block = net, to, order, block
        self.coming = {}
        self.push(0, 0, block(0) if own is None else own)

    def push(self, m, first, src):
        for i in range(first, len(self.order)):
            b = self.order[i]
            self.coming[m | b] = (self.net.send(src, self.block(m), self.to(b)), i)

    def pull(self, m):
        copy, i = self.coming[m]
        copy.wait_recv()
        self.push(m, i + 1, self.block(m))

    def masks(self):
        out = [0]
        for b in self.order:
            out += [m | b for m in out]
        return out[1:]


class Scatter:
    def __init__(self, net, to, order, block, land, add):
        self.net, self.to, self.order, self.block, self.land, self.add = net, to, order, block, land, add
        self.masks = list(range(1 << len(order)))
        self.used = 0
        self.step = 0

    def start(self):
        b = self.order[self.step]
        rest = [m for m in self.masks if not m & b]
        self.pending = []
        for m in rest:
            copy = self.net.send(self.block(m | b), self.land(self.used), self.to(b))
            self.pending.append((copy, m, self.used))
            self.used += 1
        self.masks = rest
        self.step += 1

    def finish(self):
        for copy, m, k in self.pending:
            copy.wait_recv()
            self.add(m, k)

    def last(self):
        ((copy, m, k),) = self.pending
        copy.wait_recv()
        return k


def params(cid):
    return pltpu.CompilerParams(
        collective_id=cid, has_side_effects=True, vmem_limit_bytes=62 << 20
    )


def dot_nt(a, b):
    return lax.dot_general(a, b, (((1,), (1,)), ((), ())), preferred_element_type=F32)


def dot_nn(a, b):
    return lax.dot_general(a, b, (((1,), (0,)), ((), ())), preferred_element_type=F32)


def dot_tn(a, b):
    return lax.dot_general(a, b, (((0,), (0,)), ((), ())), preferred_element_type=F32)


def slope(v):
    s = jax.nn.sigmoid(v)
    return s * (1.0 + v * (1.0 - s))


def pad_to(x, width):
    return jnp.pad(x, ((0, 0), (0, width - x.shape[1])))


def spread_basis(x, back_count, bw, fw):
    return jnp.concatenate([pad_to(x[:, :back_count], bw), pad_to(x[:, back_count:], fw)], axis=1)


def row_loop(total, unit, body):
    def step(i, carry):
        body(pl.multiple_of(i * unit, unit), unit)
        return carry

    lax.fori_loop(0, total // unit, step, 0)
    if total % unit:
        body(total - total % unit, total % unit)


def each(count, body):
    def step(i, carry):
        body(i)
        return carry

    lax.fori_loop(0, count, step, 0)


def whole(c, *refs):
    (
        pads_in, b1, b2, b3, b4, b5, b6, b7, fkb, fob, w1, w2, w3, w4, w5, w6, mix_f_in, all_f_in,
        pick_in, mix_in, series, grad, fut_in, ff, fk, fo,
        left_out, pred_out, tid_out, om, of, ok, oo, obias, chunk_hbm, land_s,
        pick, mix_b, ser, chunk, land_g, bg, fut, wmid, wf, wk, wo, part3, land3, f3a, tw, twa,
        pre, act, pooled, pred, gf, gk, go, cm, cf, ck, co, nm, zm, zi, ni, zf, nf, zk, zo,
        temp, temp3, temp4, temp2, grads, sfore, pgb, pool, pads, brow, erow, bcol, ecol, bt, bl,
        p1, p2, p3, p4, p5, p6, q0, q1, q2, q3, q4, q5, q6, q7, q8, q9, mix_f, all_f, sends, recvs, own,
    ) = refs
    nn, nc, rows, piece, part, hid, pw, bw = c.nn, c.nc, c.rows, c.piece, c.part, c.hid, c.pw, c.bw
    net = Net((nn, nc), sends, recvs)
    n, chip, core = net.n, net.chip, net.core
    owned = []
    ds = pl.ds
    send = net.send
    near = bits(nn)
    orders = (near, near[::-1])
    far, back_far = bits(nc), bits(nc)[::-1]
    half_lane = [ds(0, c.half), ds(c.half, c.off[-1] - c.half)]
    half_outer = [ds(0, c.off[4] // 2), ds(c.off[4] // 2, c.off[4] // 2)]
    halves = lambda count: [ds(0, count // 2), ds(count // 2, count // 2)]

    def local(src, dst):
        copy = pltpu.make_async_copy(src, dst, own.at[len(owned)])
        copy.start()
        owned.append(Copy(copy, False))
        return owned[-1]

    def drain():
        for copy in owned:
            copy.wait()
        net.drain()

    def weight(k):
        return wmid[:, :, :, :, c.off[k] : c.off[k + 1]].reshape(hid, c.off[k + 1] - c.off[k])

    def put_weight(k, value):
        width = c.off[k + 1] - c.off[k]
        wmid[:, :, :, :, c.off[k] : c.off[k + 1]] = value.astype(BF16).reshape(nc, 2, nn, c.hs, width)

    def lanes(j):
        return ds(pl.multiple_of(j * rows, LANE), rows)

    def steps(unit, width):
        return lax.broadcasted_iota(jnp.int32, (unit, width), 0)

    def row_mask(j, r, unit):
        return steps(unit, rows) + (j * piece + r) >= pads[:, lanes(n)]

    def settle(k, r, value, out):
        v = value + bcol[r, k : k + 1]
        pre[k, r, :] = v
        act[out, r, :] = (v * jax.nn.sigmoid(v)).astype(BF16)

    tall = 2 * c.hw
    bands = [ds(z * tall, tall) for z in range(nc)]

    def weight_rows(k, z):
        return wmid[z, :, :, :, c.off[k] : c.off[k + 1]].reshape(tall, c.off[k + 1] - c.off[k])

    def weight_columns(k, r):
        return wmid[:, :, :, :, c.off[k] + r.start : c.off[k] + r.start + r.size].reshape(hid, r.size)

    def layer(k, x, out):
        for z, r in enumerate(bands):
            settle(k, r, dot_nn(weight_rows(k, z), x[...]), out)

    def layer_back(k, x, j, out):
        for r in bands:
            grads[out, r, :] = (dot_tn(weight_columns(k, r), x[...]) * slope(pre[j, r, :])).astype(BF16)

    def sums(value):
        return dot_nt(jnp.ones((8, value.shape[1]), BF16), value)[0:1]

    net.hail()
    c_mids = [local(x, y) for x, y in zip((w1, w2, w3, w4, w5, w6), (p1, p2, p3, p4, p5, p6))]
    c_ff = local(ff, wf.at[n, chip, core])
    c_fk = local(fk, wk.at[chip, core])
    c_fo = local(fo, wo.at[chip, core])
    slot = wmid.at[chip, core, n]
    slot[...] = jnp.zeros_like(slot)
    for copy in c_mids:
        copy.wait()
    for j in range(nn):
        slot[:, j * c.poolw : j * c.poolw + c.pools] = p1[:, j * c.pools : (j + 1) * c.pools]
    for k, w in ((1, p2), (2, p3), (4, p5), (5, p6)):
        slot[:, c.off[k] : c.off[k + 1]] = w[...]
    slot[:, c.off[3] : c.off[3] + c.bcount] = p4[:, : c.bcount]
    slot[:, c.off[3] + bw : c.off[3] + bw + p4.shape[1] - c.bcount] = p4[:, c.bcount :]
    net.meet()
    z_mid = Gather(net, net.chips, far, lambda e: wmid.at[chip ^ e, core, n])

    def gather_mid(e):
        return [
            Gather(net, net.narrow, order, lambda m, h=h: wmid.at[chip ^ e, core, n ^ m, :, h])
            for order, h in zip(orders, half_lane)
        ]

    def pull_first(gathers):
        for g in gathers:
            g.pull(g.masks()[0])

    def pull_rest(gathers):
        for g in gathers:
            for m in g.masks()[1:]:
                g.pull(m)

    n_mid = {0: gather_mid(0)}
    n_ff = [
        Gather(net, net.narrow, order, lambda m, h=h: wf.at[n ^ m, chip, core, h], ff.at[h])
        for order, h in zip(orders, halves(c.hw))
    ]
    c_ser = local(series, ser)
    c_bg = local(grad, bg)
    c_fut = local(fut_in, fut)
    c_pick = local(pick_in, pick)
    c_mix = local(mix_in, mix_b)
    cuts = list(range(0, piece, up(piece // 4, LANE))) + [piece]
    cuts = [ds(a, b - a) for a, b in zip(cuts[:-1], cuts[1:])]
    starts = [0, 2 * LANE, 3 * LANE, 5 * LANE, 6 * LANE, piece]
    parts = [ds(a, b - a) for a, b in zip(starts[:-1], starts[1:])]
    c_ga = local(grad.at[:, lanes(n)], land_g.at[n])
    a_ga, a_sa = [], []

    def exchange_grad(k):
        h = cuts[k]
        for d in range(1, nn):
            a_ga.append(send(grad.at[h, lanes(n ^ d)], land_g.at[n, h], net.narrow(d)))

    def exchange_series(k):
        h = parts[k]
        for d in range(1, nn):
            a_sa.append(send(chunk_hbm.at[n ^ d, h], land_s.at[h, lanes(n)], net.narrow(d)))

    c_small = [
        local(x, y)
        for x, y in zip((pads_in, b1, b2, b3, b4, b5, b6, b7, fkb, fob), (q0, q1, q2, q3, q4, q5, q6, q7, q8, q9))
    ]
    c_tables = [local(mix_f_in.at[n], mix_f), local(all_f_in.at[n], all_f)]
    for copy in c_small:
        copy.wait()
    pads[...] = q0[...].reshape(1, nn * rows)
    brow[...] = jnp.zeros_like(brow)
    for k, b in enumerate((q1, q2, q3, q5, q6, q7)):
        brow[k : k + 1, :] = b[...].reshape(1, hid)
    theta_bias = q4[...].reshape(1, q4.shape[0])
    brow[6:7, : c.bcount] = theta_bias[:, : c.bcount]
    brow[6:7, bw : bw + q4.shape[0] - c.bcount] = theta_bias[:, c.bcount :]
    bcol[...] = jnp.transpose(brow[...])
    exchange_grad(3)
    z_mid.pull(z_mid.masks()[0])
    n_mid[z_mid.masks()[0]] = gather_mid(z_mid.masks()[0])
    z_k = [
        Gather(net, net.chips, far, lambda e: wk.at[chip ^ e, core], fk),
        Gather(net, net.chips, far, lambda e: wo.at[chip ^ e, core], fo),
    ]
    pull_first(n_ff)
    pull_first(n_mid[0])
    for m in z_mid.masks()[1:]:
        z_mid.pull(m)
        n_mid[m] = gather_mid(m)
    erow[...] = jnp.zeros_like(erow)
    for j in range(nn):

        @pl.when(n == j)
        def _(j=j):
            erow[0:1, :piece] = q8[j * piece : (j + 1) * piece].reshape(1, piece)
            erow[0:1, pw : pw + part] = q9[j * part : (j + 1) * part].reshape(1, part)

    ecol[...] = jnp.transpose(erow[...])
    bt[...] = jnp.zeros_like(bt)
    twa[...] = jnp.zeros_like(twa)
    first_step = lax.broadcasted_iota(jnp.int32, (c.poolw, piece), 0) * POOL
    behind = lax.broadcasted_iota(jnp.int32, (c.poolw, piece), 1) - first_step
    pool[...] = jnp.where((behind >= 0) & (behind < POOL), 1.0 / POOL, 0.0).astype(BF16)
    pull_first(z_k)
    others = z_mid.masks()
    for m in others[:-1]:
        pull_first(n_mid[m])
    pull_rest(n_ff)
    c_ff.wait()
    z_f = [Gather(net, net.chips, far, lambda e, j=j: wf.at[j, chip ^ e, core]) for j in range(nn)]
    a_cf = []

    def hand_over(j, e):
        block = wf.at[j, chip ^ e, core]
        a_cf.append(send(block, block, net.sibling()))

    for j in range(nn):
        hand_over(j, 0)
    c_ser.wait()

    def cut_piece(j):
        for r in range(0, piece, 64):
            unit = min(64, piece - r)
            x = ser[j * piece + r : j * piece + r + unit, :]
            chunk[j, r : r + unit, :] = jnp.where(row_mask(j, r, unit), x.astype(F32), 0).astype(BF16)

    for j in range(nn // 2):
        cut_piece(j)
    pull_first(n_mid[others[-1]])
    cut_piece(nn // 2)
    exchange_grad(0)
    for j in range(nn // 2 + 1, nn):
        cut_piece(j)
    c_chunk = [local(chunk, chunk_hbm), local(chunk.at[n], land_s.at[:, lanes(n)])]
    for j in range(nn):
        pooled[j * c.poolw : (j + 1) * c.poolw, :] = dot_nn(pool[...], chunk[j]).astype(BF16)
    pull_rest(z_k)
    c_fk.wait()
    c_fo.wait()
    a_ck = [send(wk.at[:, core], wk.at[:, core], net.sibling()), send(wo.at[:, core], wo.at[:, core], net.sibling())]
    c_bg.wait()
    c_fut.wait()

    def negate(r, unit):
        at = ds(r, unit)
        mask = steps(unit, nn * rows) + (n * piece + r) >= pads[...]
        bg[at, :] = jnp.where(mask, -bg[at, :].astype(F32), 0).astype(BF16)

    row_loop(piece, 16, negate)
    for copy in c_tables:
        copy.wait()
    for copy in a_ck:
        copy.wait_recv()

    def partial(j):
        back = wk[...].reshape(hid, piece)
        fore = wo[...].reshape(hid, part)
        part3[j, :hid, :] = (dot_nn(back, bg[:, lanes(j)]) + dot_nn(fore, fut[:, lanes(j)])).astype(BF16)
        ahead = dot_tn(all_f[...], fut[:, lanes(j)]) * c.scale_f
        part3[j, hid:, :] = ahead[: c.fcount].astype(BF16)

    each(nn, partial)

    def add_part(m, k, h):
        part3[n ^ m, h, :] = (part3[n ^ m, h, :].astype(F32) + land3[k, h, :].astype(F32)).astype(BF16)

    s_part = [
        Scatter(
            net, net.narrow, order,
            lambda m, h=h: part3.at[n ^ m, h],
            lambda k, h=h: land3.at[k, h],
            lambda m, k, h=h: add_part(m, k, h),
        )
        for order, h in zip(orders, halves(hid + c.fcount))
    ]
    for s in s_part:
        s.start()
    bt[0, ds(4 + n, 1), :piece] = sums(bg[...])
    bt[0, ds(4 + n, 1), pw : pw + part] = sums(fut[...])
    exchange_grad(1)
    for j, g in enumerate(z_f):
        g.pull(g.masks()[0])
        hand_over(j, g.masks()[0])
    a_cm = []
    for e in n_mid:
        pull_rest(n_mid[e])
        block = wmid.at[chip ^ e, core]
        a_cm.append(send(block, block, net.sibling()))
    for copy in a_cm:
        copy.wait_recv()
    layer(0, pooled, 0)
    layer(1, act.at[0], 1)
    layer(2, act.at[1], 2)
    theta = act.at[6]
    for r in bands:
        theta[r, :] = (dot_tn(weight_columns(3, r), act[2]) + bcol[r, 6:7]).astype(BF16)
    for s in s_part:
        s.finish()
        if s.step < len(near):
            s.start()
    for copy in c_chunk:
        copy.wait()
    c_pick.wait()
    c_mix.wait()

    def residual(j):
        tw[j] = dot_nn(pick[j], theta[...]).astype(BF16)
        temp[:piece, :] = dot_nn(mix_b[j], tw[j])

        def body(r, unit):
            at = ds(r, unit)
            x = chunk[j, at, :].astype(F32) - temp[at, :] * c.scale
            chunk[j, at, :] = jnp.where(row_mask(j, r, unit), x, 0).astype(BF16)

        row_loop(piece, 144, body)

    each(nn, residual)
    exchange_grad(2)
    used = ds(0, c.used)
    twa[used, lanes(n)] = tw[n, : c.used, :]
    for m in z_f[0].masks()[1:]:
        for j, g in enumerate(z_f):
            g.pull(m)
            hand_over(j, m)
    early = len(net.copies)
    for copy in a_cf[:-nn]:
        copy.wait_recv()
    for j in range(nn):
        a_cf[j - nn].wait_recv()
        for z, r in enumerate(bands):
            total = dot_nn(wf[j, z].reshape(tall, piece), chunk[j])
            if j:
                total += pre[3, r, :]
            if j < nn - 1:
                pre[3, r, :] = total
            else:
                settle(3, r, total, 3)
    layer(4, act.at[3], 4)
    layer(5, act.at[4], 5)
    f3a[:, lanes(n)] = act[5]
    n_f3 = [
        Gather(net, net.narrow, order, lambda m, h=h: f3a.at[h, lanes(n ^ m)], act.at[5, h])
        for order, h in zip(orders, halves(hid))
    ]
    while s_part[0].step < len(near):
        for s in s_part:
            s.finish()
            s.start()
    k3 = [s.last() for s in s_part]

    def collect(h, k):
        def body(r, unit):
            at = ds(h.start + r, unit)
            total = part3[n, at, :].astype(F32) + land3[k, at, :].astype(F32)
            grads[0, at, :] = (total * slope(pre[5, at, :])).astype(BF16)

        return body

    cut = (hid + c.fcount) // 2
    row_loop(cut, 96, collect(ds(0, cut), k3[0]))
    row_loop(hid - cut, 96, collect(ds(cut, hid - cut), k3[1]))
    sfore[...] = (part3[n, hid:, :].astype(F32) + land3[k3[1], hid:, :].astype(F32)).astype(BF16)
    layer_back(5, grads.at[0], 4, 1)
    layer_back(4, grads.at[1], 3, 2)
    a_tw = [send(tw.at[n ^ d, used], twa.at[used, lanes(n)], net.narrow(d)) for d in range(1, nn)]
    r_cf = []
    for j in range(nn):
        gf[j] = dot_nt(grads[2], chunk[j]).astype(BF16).reshape(nc, 2, c.hw, piece)
        r_cf.append(send(gf.at[j, :, 1 - core], cf.at[j], net.sibling()))

    def add_f(j):
        for z in range(nc):
            cf[j, z] = (gf[j, z, core].astype(F32) + cf[j, z].astype(F32)).astype(BF16)

    def add_zf(j, e, k):
        cf[j, chip ^ e] = (cf[j, chip ^ e].astype(F32) + zf[k, j].astype(F32)).astype(BF16)

    def forward_f(j):
        r_zf[j].finish()
        r_zf[j].start()

    r_zf = [
        Scatter(
            net, net.chips, back_far,
            lambda e, j=j: cf.at[j, chip ^ e],
            lambda k, j=j: zf.at[k, j],
            lambda e, k, j=j: add_zf(j, e, k),
        )
        for j in range(nn)
    ]
    for j in range(nn):
        r_cf[j].wait_recv()
        add_f(j)
        r_zf[j].start()
    for copy in net.copies[:early]:
        copy.wait_send()
    put_weight(5, dot_nt(grads[0], act[4]))
    put_weight(4, dot_nt(grads[1], act[3]))
    inner, outer = ds(c.off[4], c.off[-1] - c.off[4]), ds(0, c.off[4])
    r_ci = send(wmid.at[:, 1 - core, :, :, inner], cm.at[:, :, :, inner], net.sibling())
    c_ga.wait()
    for copy in a_ga:
        copy.wait_recv()
    temp2[...] = jnp.zeros_like(temp2)

    def resid_grad(j):
        temp[:piece, :] = dot_tn(wf[j].reshape(hid, piece), grads[2])

        def body(r, unit):
            at = ds(r, unit)
            x = land_g[j, at, :].astype(F32) + temp[at, :]
            land_g[j, at, :] = jnp.where(row_mask(j, r, unit), x, 0).astype(BF16)

        row_loop(piece, 144, body)
        pull = (dot_tn(mix_b[j], land_g[j]) * -c.scale).astype(BF16)
        temp2[...] += dot_tn(pick[j, :, :bw], pull)

    each(nn // 2, resid_grad)
    pull_first(n_f3)
    r_ci.wait_recv()
    for z in range(nc):
        both = wmid[z, core, :, :, inner].astype(F32) + cm[z, :, :, inner].astype(F32)
        cm[z, :, :, inner] = both.astype(BF16)

    def add_zi(e, k):
        both = cm[chip ^ e, :, :, inner].astype(F32) + zi[k].astype(F32)
        cm[chip ^ e, :, :, inner] = both.astype(BF16)

    def add_ni(m, k):
        both = cm[chip, n ^ m, :, inner].astype(F32) + ni[k].astype(F32)
        cm[chip, n ^ m, :, inner] = both.astype(BF16)

    r_zi = Scatter(net, net.chips, back_far, lambda e: cm.at[chip ^ e, :, :, inner], lambda k: zi.at[k], add_zi)
    r_zi.start()
    exchange_series(0)
    each(nn - nn // 2, lambda i: resid_grad(i + nn // 2))
    dth = grads.at[3]
    dth[:bw, :] = temp2[...].astype(BF16)
    dth[bw:, :] = jnp.zeros_like(dth[bw:, :])
    dth[bw : bw + c.fcount, :] = sfore[...]
    for z, r in enumerate(bands):
        grads[4, r, :] = (dot_nn(weight_rows(3, z), dth[...]) * slope(pre[2, r, :])).astype(BF16)
    layer_back(2, grads.at[4], 1, 5)
    layer_back(1, grads.at[5], 0, 6)
    forward_f(0)
    pgb[...] = dot_tn(weight(0), grads[6]).astype(BF16)
    put_weight(3, dot_nt(act[2], dth[...]))
    put_weight(2, dot_nt(grads[4], act[1]))
    put_weight(1, dot_nt(grads[5], act[0]))
    put_weight(0, dot_nt(grads[6], pooled[...]))
    r_cm = send(wmid.at[:, 1 - core, :, :, outer], cm.at[:, :, :, outer], net.sibling())
    forward_f(1)
    for k, slot_k in enumerate((6, 5, 4, 3, 2, 1, 0)):
        bt[0, k // 2 : k // 2 + 1, (k % 2) * hid : (k % 2 + 1) * hid] = sums(grads[slot_k])
    travel = [net.sibling()] + [net.narrow(b) for b in near] + [net.chips(b) for b in back_far]
    v_copies = []

    def send_bias():
        k = len(v_copies)
        v_copies.append(send(bt.at[k], bl.at[k], travel[k]))

    def add_bias():
        k = len(v_copies) - 1
        v_copies[k].wait_recv()
        bt[k + 1] = bt[k] + bl[k]

    send_bias()
    r_cm.wait_recv()
    for z in range(nc):
        both = wmid[z, core, :, :, outer].astype(F32) + cm[z, :, :, outer].astype(F32)
        cm[z, :, :, outer] = both.astype(BF16)

    def add_nm(m, k, h):
        cm[:, n ^ m, :, h] = (cm[:, n ^ m, :, h].astype(F32) + nm[k, :, :, h].astype(F32)).astype(BF16)

    r_nm = [
        Scatter(
            net, net.narrow, order,
            lambda m, h=h: cm.at[:, n ^ m, :, h],
            lambda k, h=h: nm.at[k, :, :, h],
            lambda m, k, h=h: add_nm(m, k, h),
        )
        for order, h in zip(orders, half_outer)
    ]
    for s in r_nm:
        s.start()
    add_bias()
    send_bias()
    pull_rest(n_f3)
    gk[...] = dot_nt(f3a[...], bg[...]).astype(BF16).reshape(nc, 2, c.hw, piece)
    exchange_series(1)
    go[...] = dot_nt(f3a[...], fut[...]).astype(BF16).reshape(nc, 2, c.hw, part)
    r_ck = [send(gk.at[:, 1 - core], ck, net.sibling()), send(go.at[:, 1 - core], co, net.sibling())]
    def add_k(e, k):
        ck[chip ^ e] = (ck[chip ^ e].astype(F32) + zk[k].astype(F32)).astype(BF16)

    def add_o(e, k):
        co[chip ^ e] = (co[chip ^ e].astype(F32) + zo[k].astype(F32)).astype(BF16)

    r_zk = [
        Scatter(net, net.chips, back_far, lambda e: ck.at[chip ^ e], lambda k: zk.at[k], add_k),
        Scatter(net, net.chips, back_far, lambda e: co.at[chip ^ e], lambda k: zo.at[k], add_o),
    ]

    def series_grad(j):
        temp[:piece, :] = dot_tn(pool[...], pgb[j * c.poolw : (j + 1) * c.poolw, :])
        for r in range(0, piece, 64):
            unit = min(64, piece - r)
            x = land_g[j, r : r + unit, :].astype(F32) + temp[r : r + unit, :]
            x = jnp.where(row_mask(j, r, unit), x, 0).astype(BF16)
            ser[j * piece + r : j * piece + r + unit, :] = x

    def outputs(k):
        h = parts[k]
        for copy in a_sa[k * (nn - 1) : (k + 1) * (nn - 1)]:
            copy.wait_recv()
        local(land_s.at[h], bg.at[h]).wait()
        stop = h.start + h.size
        marks = [r for r in range(h.start, stop, LANE) if stop - r >= LANE // 2] + [stop]
        for low, high in zip(marks[:-1], marks[1:]):
            temp3[: high - low, :] = dot_nn(mix_b[n, low:high, :], twa[...])
            temp4[: high - low, :] = dot_tn(wk[:, :, :, low:high].reshape(hid, high - low), f3a[...])

            def body(r, unit, low=low):
                at, here = ds(low + r, unit), ds(r, unit)
                x = (bg[at, :].astype(F32) - temp3[here, :] * c.scale).astype(BF16).astype(F32)
                x = x - (temp4[here, :] + ecol[at, 0:1])
                mask = steps(unit, nn * rows) + (n * piece + low + r) >= pads[...]
                bg[at, :] = jnp.where(mask, x, 0).astype(BF16)

            row_loop(high - low, 32, body)
        local(bg.at[h], left_out.at[h])

    def forecast():
        fore = dot_nn(mix_f[...], twa[...]) * c.scale_f
        pred[...] = fore + dot_tn(wo[...].reshape(hid, part), f3a[...]) + ecol[pw : pw + part, 0:1]

    def add_nf(m, k, h):
        cf[n ^ m, chip, h, :] = (cf[n ^ m, chip, h, :].astype(F32) + nf[k, h, :].astype(F32)).astype(BF16)

    def add_zm(e, k):
        both = cm[chip ^ e, n, :, outer].astype(F32) + zm[k].astype(F32)
        cm[chip ^ e, n, :, outer] = both.astype(BF16)

    r_zm = Scatter(net, net.chips, back_far, lambda e: cm.at[chip ^ e, n, :, outer], lambda k: zm.at[k], add_zm)
    r_nf = [
        Scatter(
            net, net.narrow, order,
            lambda m, h=h: cf.at[n ^ m, chip, h],
            lambda k, h=h: nf.at[k, h],
            lambda m, k, h=h: add_nf(m, k, h),
        )
        for order, h in zip(orders, halves(c.hw))
    ]
    series_grad(0)
    forward_f(2)
    for j in range(1, nn - 1):
        series_grad(j)
    for j in range(3, nn):
        forward_f(j)
    for copy in r_ck:
        copy.wait_recv()
    for z in range(nc):
        ck[z] = (gk[z, core].astype(F32) + ck[z].astype(F32)).astype(BF16)
        co[z] = (go[z, core].astype(F32) + co[z].astype(F32)).astype(BF16)
    for s in r_nm:
        s.finish()
        s.start()
    add_bias()
    send_bias()
    series_grad(nn - 1)
    exchange_series(2)
    c_tid = local(ser, tid_out)
    for copy in a_tw:
        copy.wait_recv()
    forecast()
    c_pred = local(pred, pred_out)
    outputs(0)
    for s in r_nm:
        s.finish()
    r_zm.start()
    add_bias()
    send_bias()
    for s in r_zk:
        s.start()
    r_zi.finish()
    r_zi.start()
    for s in r_zf:
        s.finish()
    for s in r_nf:
        s.start()
    outputs(1)
    exchange_series(3)
    exchange_series(4)
    r_zm.finish()
    r_zm.start()
    add_bias()
    send_bias()
    outputs(2)
    for s in r_zk:
        s.finish()
        s.start()
    for s in r_nf:
        s.finish()
        s.start()
    r_zi.finish()
    r_ni = Scatter(net, net.narrow, near, lambda m: cm.at[chip, n ^ m, :, inner], lambda k: ni.at[k], add_ni)
    r_ni.start()
    add_bias()
    obias[...] = bt[len(travel)]
    outputs(3)
    r_zm.finish()
    outputs(4)
    r_ni.finish()
    r_ni.start()
    for s in r_nf:
        s.finish()
    of[...] = cf[n, chip].astype(F32)
    for s in r_zk:
        s.finish()
    ok[...] = ck[chip].astype(F32)
    oo[...] = co[chip].astype(F32)
    r_ni.finish()
    om[...] = cm[chip, n].astype(F32)
    drain()
    assert len(net.copies) <= sends.shape[0] and len(owned) <= own.shape[0]


def finish(c, *refs):
    large_in, small_in, large_out, small_out = refs[:3], refs[3:8], refs[8:11], refs[11:29]
    held, (om, of, ok, oo, obias), given, sems = refs[29:32], refs[32:37], refs[37:55], refs[55]
    g1, v1, g2, v2, g3, v3, g4, v4, gf, vf1, g5, vf2, g6, vf3, gk, vk, go, vo = given
    arriving = [
        pltpu.make_async_copy(src, dst, sems.at[48 + k])
        for k, (src, dst) in enumerate(zip(small_in, (om, of, ok, oo, obias)))
    ]
    leaving = [
        pltpu.make_async_copy(src, dst, sems.at[53 + k]) for k, (src, dst) in enumerate(zip(given, small_out))
    ]
    for copy in arriving:
        copy.start()
    pieces = []
    for a, (src, via, dst) in enumerate(zip(large_in, held, large_out)):
        size = up(-(-src.shape[0] // 8), 16)
        for b, r in enumerate(range(0, src.shape[0], size)):
            h = pl.ds(r, min(size, src.shape[0] - r))
            k = 16 * a + 2 * b
            pieces.append(
                (
                    pltpu.make_async_copy(src.at[h], via.at[h], sems.at[k]),
                    pltpu.make_async_copy(via.at[h], dst.at[h], sems.at[k + 1]),
                )
            )
    for inward, outward in pieces:
        inward.start()
    for copy in arriving:
        copy.wait()
    nn, piece, part, hid, bw = c.nn, c.piece, c.part, c.hid, c.bw
    for j in range(nn):
        g1[:, j * c.pools : (j + 1) * c.pools] = om[:, j * c.poolw : j * c.poolw + c.pools]
    for k, g in ((1, g2), (2, g3), (4, g5), (5, g6)):
        g[...] = om[:, c.off[k] : c.off[k + 1]]
    fore = g4.shape[1] - c.bcount
    g4[:, : c.bcount] = om[:, c.off[3] : c.off[3] + c.bcount]
    g4[:, c.bcount :] = om[:, c.off[3] + bw : c.off[3] + bw + fore]
    gf[...] = of[...]
    gk[...] = ok[...]
    go[...] = oo[...]
    for k, v in enumerate((v1, v2, v3, None, vf1, vf2, vf3)):
        if v is not None:
            v[...] = obias[k // 2 : k // 2 + 1, (k % 2) * hid : (k % 2 + 1) * hid].reshape(hid)
    theta = obias[1:2, hid : 2 * hid]
    v4[...] = jnp.concatenate([theta[:, : c.bcount], theta[:, bw : bw + fore]], axis=1).reshape(v4.shape[0])
    vk[...] = jnp.concatenate([obias[4 + j : 5 + j, :piece] for j in range(nn)], axis=1).reshape(vk.shape[0])
    vo[...] = jnp.concatenate([obias[4 + j : 5 + j, c.pw : c.pw + part] for j in range(nn)], axis=1).reshape(vo.shape[0])
    for copy in leaving:
        copy.start()
    for inward, outward in pieces:
        inward.wait()
        outward.start()
    for inward, outward in pieces:
        outward.wait()
    for copy in leaving:
        copy.wait()


def fast(nn, nw, series, padding, *rest):
    (cf, cfb, cs, csb, ct, ctb, cb, cbb, ff, ffb, fs, fsb, ft, ftb, fk, fkb, fo, fob, grad, fut) = rest
    nc = nw // 2
    rows, length = series.shape
    piece, part = grad.shape[1], fut.shape[1]
    ahead = part * nn
    hid = cfb.shape[0]
    hs, hw = hid // (nn * nw), hid // nw
    back_count, fore_count = KB, cbb.shape[0] - KB
    bw, fw = up(back_count, LANE), up(fore_count, LANE)
    used, (pick, mix_b, mix_f, all_f) = window_tables(nn, length, ahead, back_count, fore_count)
    width = pick.shape[1]
    fcount = up(fore_count, 16)
    pools = piece // POOL
    poolw = up(pools, LANE)
    widths = (nn * poolw, hid, hid, bw + fw, hid, hid)
    off = np.concatenate([[0], np.cumsum(widths)]).tolist()
    mw = off[-1]
    pw = up(piece, LANE)
    assert bw + fw == hid
    c = types.SimpleNamespace(
        nn=nn, nc=nc, rows=rows, piece=piece, part=part, hid=hid, hs=hs, hw=hw, pw=pw, bw=bw,
        off=off, poolw=poolw, pools=pools, used=up(used, 16), fcount=fcount,
        bcount=back_count, half=up(mw // 2, LANE),
        scale=1.0 / (2 * (length // back_count)),
        scale_f=1.0 / (2 * (ahead // fore_count)),
    )
    anyspec = pl.BlockSpec(memory_space=pl.ANY)
    vspec = pl.BlockSpec(memory_space=pltpu.VMEM)
    S, V = jax.ShapeDtypeStruct, pltpu.VMEM
    bs = (up(4 + nn, 8), max(2 * hid, pw + up(part, LANE)))
    stages = 1 + len(bits(nn)) + len(bits(nc))
    gathers = (nc - 1) + 2 * nc * (nn - 1) + 2 * (nn - 1) + 3 * (nc - 1) + 2 + 2 * nc
    ncopies = gathers + 12 * (nn + nc) + 6 * nn * nc
    qw = up(part, LANE)
    scratch = [
        V((nn, width, bw + fw), BF16),
        V((nn, piece, width), BF16),
        V((length, rows), BF16),
        V((nn, piece, rows), BF16),
        V((nn, piece, rows), BF16),
        V((piece, nn * rows), BF16),
        V((part, nn * rows), BF16),
        V((nc, 2, nn, hs, mw), BF16),
        V((nn, nc, 2, hw, piece), BF16),
        V((nc, 2, hw, piece), BF16),
        V((nc, 2, hw, part), BF16),
        V((nn, hid + fcount, rows), BF16),
        V((nn - 1, hid + fcount, rows), BF16),
        V((hid, nn * rows), BF16),
        V((nn, width, rows), BF16),
        V((width, nn * rows), BF16),
        V((6, hid, rows), F32),
        V((7, hid, rows), BF16),
        V((nn * poolw, rows), BF16),
        V((part, nn * rows), F32),
        V((nn, nc, 2, hw, piece), BF16),
        V((nc, 2, hw, piece), BF16),
        V((nc, 2, hw, part), BF16),
        V((nc, nn, hs, mw), BF16),
        V((nn, nc, hw, piece), BF16),
        V((nc, hw, piece), BF16),
        V((nc, hw, part), BF16),
        V((nn - 1, nc, hs, off[4]), BF16),
        V((nc - 1, hs, off[4]), BF16),
        V((nc - 1, nn, hs, mw - off[4]), BF16),
        V((nn - 1, hs, mw - off[4]), BF16),
        V((nc - 1, nn, hw, piece), BF16),
        V((nn - 1, hw, piece), BF16),
        V((nc - 1, hw, piece), BF16),
        V((nc - 1, hw, part), BF16),
        V((piece, rows), F32),
        V((LANE + up(piece % LANE, 16), nn * rows), F32),
        V((LANE + up(piece % LANE, 16), nn * rows), F32),
        V((bw, rows), F32),
        V((7, hid, rows), BF16),
        V((fcount, rows), BF16),
        V((nn * poolw, rows), BF16),
        V((poolw, piece), BF16),
        V((1, nn * rows), jnp.int32),
        V((8, hid), F32),
        V((8, pw + qw), F32),
        V((hid, 8), F32),
        V((pw + qw, 8), F32),
        V((stages + 1,) + bs, F32),
        V((stages,) + bs, F32),
    ]
    scratch += [V(w.shape, BF16) for w in (cf, cs, ct, cb, fs, ft)]
    scratch += [V(b.shape, b.dtype) for b in (padding, cfb, csb, ctb, cbb, ffb, fsb, ftb, fkb, fob)]
    scratch += [
        V(mix_f.shape[1:], BF16),
        V(all_f.shape[1:], BF16),
        pltpu.SemaphoreType.DMA((ncopies,)),
        pltpu.SemaphoreType.DMA((ncopies,)),
        pltpu.SemaphoreType.DMA((40 + 8 * nn,)),
    ]
    leftover, pred, tid, om, of, ok, oo, obias, _, _ = pl.pallas_call(
        functools.partial(whole, c),
        out_shape=(
            S((piece, nn * rows), BF16),
            S((part, nn * rows), F32),
            S((length, rows), BF16),
            S((hs, mw), F32),
            S((hw, piece), F32),
            S((hw, piece), F32),
            S((hw, part), F32),
            S(bs, F32),
            S((nn, piece, rows), BF16),
            S((piece, nn * rows), BF16),
        ),
        in_specs=[anyspec] * 26,
        out_specs=[anyspec] * 3 + [vspec] * 5 + [anyspec] * 2,
        scratch_shapes=scratch,
        compiler_params=params(0),
    )(
        padding, cfb, csb, ctb, cbb, ffb, fsb, ftb, fkb, fob, cf, cs, ct, cb, fs, ft, mix_f, all_f,
        pick, mix_b, series.T, grad.T, fut.T, ff, fk, fo,
    )
    params_like = (cf, cfb, cs, csb, ct, ctb, cb, cbb, ff, ffb, fs, fsb, ft, ftb, fk, fkb, fo, fob)
    outs = pl.pallas_call(
        functools.partial(finish, c),
        out_shape=tuple(S(x.shape, x.dtype) for x in (leftover, pred, tid))
        + tuple(S(p.shape, F32) for p in params_like),
        in_specs=[anyspec] * 8,
        out_specs=[anyspec] * 21,
        scratch_shapes=[V(x.shape, x.dtype) for x in (leftover, pred, tid, om, of, ok, oo, obias)]
        + [V(p.shape, F32) for p in params_like]
        + [pltpu.SemaphoreType.DMA((72,))],
        compiler_params=pltpu.CompilerParams(vmem_limit_bytes=60 << 20),
    )(leftover, pred, tid, om, of, ok, oo, obias)
    return (outs[0].T, outs[1].T, outs[2].T) + tuple(outs[3:])


def upsample(coef, length):
    coef_count = coef.shape[1]
    stride = length // coef_count
    halfway = stride // 2
    padded = jnp.concatenate([coef[:, :1], coef, coef[:, -1:]], axis=1)
    preceding = jnp.repeat(padded[:, :coef_count], stride, axis=1)
    central = jnp.repeat(padded[:, 1 : coef_count + 1], stride, axis=1)
    following = jnp.repeat(padded[:, 2:], stride, axis=1)
    offsets = jnp.arange(length, dtype=jnp.int32) % stride
    in_front = offsets < halfway
    fraction = (
        jnp.where(in_front, offsets + halfway, offsets - halfway).astype(jnp.float32) + 0.5
    ) / stride
    lower_val = jnp.where(in_front[None, :], preceding, central)
    upper_val = jnp.where(in_front[None, :], central, following)
    return lower_val * (1.0 - fraction) + upper_val * fraction


def silu_slope(value):
    sigma = jax.nn.sigmoid(value)
    return sigma * (1.0 + value * (1.0 - sigma))


def project_rows(rows_in, matrix):
    return lax.dot_general(
        rows_in, matrix, (((1,), (1,)), ((), ())), preferred_element_type=jnp.float32
    )


def apply_rows(rows_in, matrix):
    return jnp.dot(rows_in, matrix, preferred_element_type=jnp.float32)


def column_outer(first_rows, second_rows):
    return lax.dot_general(
        first_rows, second_rows, (((0,), (0,)), ((), ())), preferred_element_type=jnp.float32
    )


def own_slice(values, begin, amount):
    return lax.dynamic_slice_in_dim(values, begin, amount, 0)


def column_sums(values):
    return jnp.sum(values.astype(jnp.float32), axis=0)


def general(
    series,
    padding,
    coarse_first,
    coarse_first_bias,
    coarse_second,
    coarse_second_bias,
    coarse_third,
    coarse_third_bias,
    coarse_basis,
    coarse_basis_bias,
    fine_first,
    fine_first_bias,
    fine_second,
    fine_second_bias,
    fine_third,
    fine_third_bias,
    fine_back,
    fine_back_bias,
    fine_fore,
    detailed_predict_offset,
    grad_resid,
    future_cotangent_array,
):
    slim_breadth = lax.axis_size("narrow")
    slim_position = lax.axis_index("narrow")
    onsite_tally, length = series.shape
    ahead = future_cotangent_array.shape[1] * slim_breadth
    sample_group = onsite_tally // PASSES
    piece = length // slim_breadth
    predicted_portion = ahead // slim_breadth
    group_pads = padding.reshape(slim_breadth, onsite_tally)
    own_pads = lax.dynamic_slice_in_dim(group_pads, slim_position, 1, 0)[0]
    steps_all = jnp.arange(length, dtype=jnp.int32)
    time_start = slim_position * piece
    predict_onset = slim_position * predicted_portion
    steps_piece = time_start + jnp.arange(piece, dtype=jnp.int32)
    back_bias = lax.dynamic_slice_in_dim(fine_back_bias, time_start, piece, 0)
    predict_offset = lax.dynamic_slice_in_dim(
        detailed_predict_offset, predict_onset, predicted_portion, 0
    )
    resid_grid = grad_resid.reshape(slim_breadth, PASSES, sample_group, piece)
    predict_mesh = future_cotangent_array.reshape(
        slim_breadth, PASSES, sample_group, predicted_portion
    )
    own_start = slim_position * sample_group
    coarse_local = (
        coarse_first,
        coarse_second,
        coarse_third,
        coarse_basis,
        fine_second,
        fine_third,
    )
    fine_local = (fine_first, fine_back, fine_fore)
    totals = tuple((jnp.zeros(w.shape, jnp.float32) for w in coarse_local))
    fine_totals = tuple((jnp.zeros(w.shape, jnp.float32) for w in fine_local))
    bias_totals = tuple(
        (
            jnp.zeros(b.shape, jnp.float32)
            for b in (
                coarse_first_bias,
                coarse_second_bias,
                coarse_third_bias,
                coarse_basis_bias,
                fine_first_bias,
                fine_second_bias,
                fine_third_bias,
                fine_back_bias,
                detailed_predict_offset,
            )
        )
    )
    residual_parts = []
    predicted_portions = []
    grad_parts = []
    for iteration_index in range(PASSES):
        shared = (
            lax.all_gather(coarse_first, ("wide", "narrow"), axis=0, tiled=True),
            lax.all_gather(coarse_second, ("wide", "narrow"), axis=0, tiled=True),
            lax.all_gather(coarse_third, ("wide", "narrow"), axis=0, tiled=True),
            lax.all_gather(coarse_basis, ("wide", "narrow"), axis=0, tiled=True),
            lax.all_gather(fine_second, ("wide", "narrow"), axis=0, tiled=True),
            lax.all_gather(fine_third, ("wide", "narrow"), axis=0, tiled=True),
        )
        pieces = (
            lax.all_gather(fine_first, "wide", axis=0, tiled=True),
            lax.all_gather(fine_back, "wide", axis=0, tiled=True),
            lax.all_gather(fine_fore, "wide", axis=0, tiled=True),
        )
        weight_one, weight_two, weight_three, weight_basis, inner_two, inner_three = shared
        inner_one, inner_back, inner_fore = pieces
        lower = iteration_index * sample_group
        mask = (steps_all[None, :] >= own_pads[lower : lower + sample_group, None]).astype(
            jnp.float32
        )
        started = series[lower : lower + sample_group].astype(jnp.float32) * mask
        pooled = jnp.mean(started.reshape(sample_group, length // POOL, POOL), axis=2).astype(
            jnp.bfloat16
        )
        linear_one = project_rows(pooled, weight_one) + coarse_first_bias
        hidden_one = jax.nn.silu(linear_one).astype(jnp.bfloat16)
        linear_two = project_rows(hidden_one, weight_two) + coarse_second_bias
        hidden_two = jax.nn.silu(linear_two).astype(jnp.bfloat16)
        linear_three = project_rows(hidden_two, weight_three) + coarse_third_bias
        hidden_three = jax.nn.silu(linear_three).astype(jnp.bfloat16)
        theta = apply_rows(hidden_three, weight_basis) + coarse_basis_bias
        backcast = upsample(theta[:, :KB], length)
        coarse_fore = upsample(theta[:, KB:], ahead)
        residual_here = (started - backcast) * mask
        sent_resid, sent_fore = (
            lax.all_to_all(
                residual_here.astype(jnp.bfloat16),
                "narrow",
                split_axis=1,
                concat_axis=0,
                tiled=True,
            ),
            lax.all_to_all(
                coarse_fore.astype(jnp.bfloat16), "narrow", split_axis=1, concat_axis=0, tiled=True
            ),
        )
        pads_here = group_pads[:, lower : lower + sample_group].reshape(-1)
        piece_mask = (steps_piece[None, :] >= pads_here[:, None]).astype(jnp.float32)
        first_partial = project_rows(sent_resid, inner_one)
        lift_one = lax.psum(first_partial, "narrow") + fine_first_bias
        fine_one = jax.nn.silu(lift_one).astype(jnp.bfloat16)
        lift_two = project_rows(fine_one, inner_two) + fine_second_bias
        fine_two = jax.nn.silu(lift_two).astype(jnp.bfloat16)
        lift_three = project_rows(fine_two, inner_three) + fine_third_bias
        fine_three = jax.nn.silu(lift_three).astype(jnp.bfloat16)
        coef_back = apply_rows(fine_three, inner_back) + back_bias
        coef_fore = apply_rows(fine_three, inner_fore) + predict_offset
        residual_parts.append(
            ((sent_resid.astype(jnp.float32) - coef_back) * piece_mask)
            .astype(jnp.bfloat16)
            .reshape(slim_breadth, sample_group, piece)
        )
        predicted_portions.append(
            (sent_fore.astype(jnp.float32) + coef_fore).reshape(
                slim_breadth, sample_group, predicted_portion
            )
        )
        out_grad = (
            resid_grid[:, iteration_index]
            .reshape(slim_breadth * sample_group, piece)
            .astype(jnp.float32)
        )
        predict_cotan = predict_mesh[:, iteration_index].reshape(
            slim_breadth * sample_group, predicted_portion
        )
        back_grad = (-out_grad * piece_mask).astype(jnp.bfloat16)
        coef_partial = project_rows(back_grad, inner_back) + project_rows(predict_cotan, inner_fore)
        three_grad = lax.psum(coef_partial, "narrow")
        lift_three_grad = (three_grad * silu_slope(lift_three)).astype(jnp.bfloat16)
        lift_two_grad = (apply_rows(lift_three_grad, inner_three) * silu_slope(lift_two)).astype(
            jnp.bfloat16
        )
        lift_one_grad = (apply_rows(lift_two_grad, inner_two) * silu_slope(lift_one)).astype(
            jnp.bfloat16
        )
        own_one_grad = own_slice(lift_one_grad, own_start, sample_group)
        own_two_grad = own_slice(lift_two_grad, own_start, sample_group)
        own_three_grad = own_slice(lift_three_grad, own_start, sample_group)
        own_fine_one = own_slice(fine_one, own_start, sample_group)
        own_fine_two = own_slice(fine_two, own_start, sample_group)
        sent_grad = (out_grad * piece_mask + apply_rows(lift_one_grad, inner_one)).astype(
            jnp.bfloat16
        )
        resid_back, fore_back = (
            lax.all_to_all(sent_grad, "narrow", split_axis=0, concat_axis=1, tiled=True),
            lax.all_to_all(predict_cotan, "narrow", split_axis=0, concat_axis=1, tiled=True),
        )
        grad_inner_one = column_outer(lift_one_grad, sent_resid)
        grad_inner_back = column_outer(fine_three, back_grad)
        grad_inner_fore = column_outer(fine_three, predict_cotan)
        grad_inner_two = column_outer(own_two_grad, own_fine_one)
        grad_inner_three = column_outer(own_three_grad, own_fine_two)
        resid_grad = resid_back.astype(jnp.float32)
        back_pull = jax.vjp(lambda coef: upsample(coef, length), theta[:, :KB])[1]
        fore_pull = jax.vjp(lambda coef: upsample(coef, ahead), theta[:, KB:])[1]
        back_coef_grad = back_pull(-resid_grad * mask)[0]
        fore_coef_grad = fore_pull(fore_back.astype(jnp.float32))[0]
        theta_grad = jnp.concatenate([back_coef_grad, fore_coef_grad], axis=1).astype(jnp.bfloat16)
        coarse_three_grad = (
            project_rows(theta_grad, weight_basis) * silu_slope(linear_three)
        ).astype(jnp.bfloat16)
        coarse_two_grad = (
            apply_rows(coarse_three_grad, weight_three) * silu_slope(linear_two)
        ).astype(jnp.bfloat16)
        coarse_one_grad = (apply_rows(coarse_two_grad, weight_two) * silu_slope(linear_one)).astype(
            jnp.bfloat16
        )
        pooled_grad = apply_rows(coarse_one_grad, weight_one)
        start_grad = resid_grad * mask + jnp.repeat(pooled_grad, POOL, axis=1) / POOL
        grad_parts.append((start_grad * mask).astype(jnp.bfloat16))
        grad_weight_one = column_outer(coarse_one_grad, pooled)
        grad_weight_two = column_outer(coarse_two_grad, hidden_one)
        grad_weight_three = column_outer(coarse_three_grad, hidden_two)
        grad_weight_basis = column_outer(hidden_three, theta_grad)
        bias_terms = (
            column_sums(coarse_one_grad),
            column_sums(coarse_two_grad),
            column_sums(coarse_three_grad),
            column_sums(theta_grad),
            column_sums(own_one_grad),
            column_sums(own_two_grad),
            column_sums(own_three_grad),
            lax.dynamic_update_slice_in_dim(
                jnp.zeros((length,), jnp.float32), column_sums(back_grad), time_start, 0
            ),
            lax.dynamic_update_slice_in_dim(
                jnp.zeros((ahead,), jnp.float32), column_sums(predict_cotan), predict_onset, 0
            ),
        )
        bias_totals = tuple((total + term for total, term in zip(bias_totals, bias_terms)))
        scattered = (
            lax.psum_scatter(grad_weight_one, ("wide", "narrow"), scatter_dimension=0, tiled=True),
            lax.psum_scatter(grad_weight_two, ("wide", "narrow"), scatter_dimension=0, tiled=True),
            lax.psum_scatter(
                grad_weight_three, ("wide", "narrow"), scatter_dimension=0, tiled=True
            ),
            lax.psum_scatter(
                grad_weight_basis, ("wide", "narrow"), scatter_dimension=0, tiled=True
            ),
            lax.psum_scatter(grad_inner_two, ("wide", "narrow"), scatter_dimension=0, tiled=True),
            lax.psum_scatter(grad_inner_three, ("wide", "narrow"), scatter_dimension=0, tiled=True),
        )
        spread = (
            lax.psum_scatter(
                grad_inner_one.astype(jnp.bfloat16), "wide", scatter_dimension=0, tiled=True
            ).astype(jnp.float32),
            lax.psum_scatter(
                grad_inner_back.astype(jnp.bfloat16), "wide", scatter_dimension=0, tiled=True
            ).astype(jnp.float32),
            lax.psum_scatter(
                grad_inner_fore.astype(jnp.bfloat16), "wide", scatter_dimension=0, tiled=True
            ).astype(jnp.float32),
        )
        totals = tuple((total + term for total, term in zip(totals, scattered)))
        fine_totals = tuple((total + term for total, term in zip(fine_totals, spread)))
    bias_sums = lax.psum(
        (
            bias_totals[0],
            bias_totals[1],
            bias_totals[2],
            bias_totals[3],
            bias_totals[4],
            bias_totals[5],
            bias_totals[6],
            bias_totals[7],
            bias_totals[8],
        ),
        ("wide", "narrow"),
    )
    leftover_signal = jnp.stack(residual_parts, axis=1).reshape(slim_breadth * onsite_tally, piece)
    predicted_future = jnp.stack(predicted_portions, axis=1).reshape(
        slim_breadth * onsite_tally, predicted_portion
    )
    temporal_input_derivative = jnp.concatenate(grad_parts, axis=0)
    return (
        leftover_signal,
        predicted_future,
        temporal_input_derivative,
        totals[0],
        bias_sums[0],
        totals[1],
        bias_sums[1],
        totals[2],
        bias_sums[2],
        totals[3],
        bias_sums[3],
        fine_totals[0],
        bias_sums[4],
        totals[4],
        bias_sums[5],
        totals[5],
        bias_sums[6],
        fine_totals[1],
        bias_sums[7],
        fine_totals[2],
        bias_sums[8],
    )


def fits(nn, nw, series, padding, first, first_bias, *rest):
    hid, length = first_bias.shape[0], series.shape[1]
    paired = all(k & (k - 1) == 0 for k in (nn, nw)) and nw % 2 == 0
    paired = paired and len(bits(nn)) == 2 and len(bits(nw // 2)) == 2
    paired = paired and length > 6 * LANE * nn
    return paired and hid % (16 * nn * nw) == 0 and length % (POOL * nn) == 0 and series.shape[0] % LANE == 0


def solution(mesh):
    both, rows = P(("wide", "narrow"), None), P("wide", "narrow")
    in_specs = (both, P("wide"))
    in_specs += (both, P()) * 4 + (rows, P()) + (both, P()) * 2 + (rows, P()) * 2 + (rows, rows)
    out_specs = (rows, rows, both) + (both, P()) * 4 + (rows, P()) + (both, P()) * 2 + (rows, P()) * 2
    nn, nw = mesh.shape["narrow"], mesh.shape["wide"]

    def body(*args):
        if fits(nn, nw, *args):
            return fast(nn, nw, *args)
        return general(*args)

    return jax.shard_map(body, mesh=mesh, in_specs=in_specs, out_specs=out_specs, check_vma=False)
```
